32 devices in a mesh: tile: 16 (over z, x, core), pgrp: 2 (over y).
Axes of the slice: x: 2, y: 2, z: 4, core: 2. Of those that a mesh axis runs over, the one named last changes fastest.
Arguments:
- concentrations: float32 [130, 16, 256], P(None, 'tile'), may hold values from 0.1 to 2
- tangents: float32 [64, 130, 16, 256], P('pgrp', None, 'tile'), may hold values from -6 to 6
- rates: float32 [218, 16, 256], P(None, 'tile'), may hold values from 0.01 to 1
- substeps: int32 [16, 256], P('tile'), may hold values from 1 to 4, as said below
- courant: float32 [2, 16, 256], P(None, 'tile'), may hold values from -0.9 to 0.9
- reactants: int32 [218, 2], replicated, may hold values from 0 to 129
- products: int32 [218, 2], replicated, may hold values from 0 to 129
- yields: float32 [218, 2], replicated, may hold values from 0.2 to 0.5
- reaction_index: int32 [64], P('pgrp'), may hold values from 0 to 217
Outputs:
- concentrations_out: float32 [130, 16, 256], P(None, 'tile')
- tangents_out: float32 [64, 130, 16, 256], P('pgrp', None, 'tile')
The draws below stay inside these ranges and needn't reach their ends.
Inputs may be any that keep to these rules, and one draw needn't show every extreme that they name: `substeps`: each column needs at least one substep; some column has 4.
All inputs are finite; a program needn't handle non-finite values.
Results may differ from the reference program's by a relative error of at most 0.0003.
Values sent between devices are 32-bit elements; how exact they have to be, the bound alone decides.
No kernel may reach another device: no remote copies, remote signals or barrier semaphores. Data moves between devices by JAX's collectives and lax.ppermute only.
A program may use at most 256 MiB of HBM per device.

```python
import math
import jax
import jax.numpy as jnp
from jax import lax

S = 130
R = 218
P_SIZE = 64
CX = 16
CY = 16
NMAX = 4
SWEEPS = 1
TILES = 16
CELLS = 256


def draw_substeps(key, part):
    keys = jax.random.split(key, 3)
    level = jax.random.randint(keys[0], (TILES, 1), 1, NMAX + 1)
    spread = jax.random.randint(keys[1], (TILES, CELLS), 0, NMAX)
    counts = 1 + spread % level
    peak = jax.random.randint(keys[2], (), 0, TILES)
    return counts.at[peak, 0].set(NMAX).astype(jnp.int32)


def plant(entries, stream_key, low, top_value):
    longest = entries.shape.index(max(entries.shape))
    spots = []
    for shift in (0, 1):
        where = [jax.random.randint(jax.random.fold_in(stream_key, axis), (), 0, length) for axis, length in enumerate(entries.shape)]
        where[longest] = (where[longest] + shift) % entries.shape[longest]
        spots.append(tuple(where))
    return entries.at[spots[0]].set(low).at[spots[1]].set(top_value)


def steps_of(stream_key, extent, cuts, least, top_value):
    def one(axis_at, parts):
        heights = jax.random.uniform(jax.random.fold_in(jax.random.fold_in(stream_key, 6), axis_at), (parts,), jnp.float32, least / len(cuts), top_value / len(cuts))
        return jnp.repeat(jnp.exp(heights), extent[axis_at] // parts).reshape((-1,) + (1,) * (len(extent) - axis_at - 1))

    level = one(*cuts[0])
    for cut in cuts[1:]:
        level = level * one(*cut)
    return level


def noise(own_key, shape, deviation, most, cuts=(), held_as=jnp.bfloat16):
    array = jax.random.normal(own_key, shape, jnp.float32) * deviation
    if len(cuts) > 0:
        array = steps_of(own_key, shape, cuts, -0.22, 0.18) * array
    return jnp.clip(array, min=-most, max=most).astype(held_as)


def setup_inputs(seed: int = 0) -> dict:
    splits = jax.random.split(jax.random.key(seed), 10)
    return {
        "concentrations": jnp.clip(jnp.exp(math.log(2.0) - 2.9957323 * jax.random.uniform(splits[0], (S, TILES, CELLS), jnp.float32) ** steps_of(splits[0], (S, TILES, CELLS), ((1, 16),), -0.2, 0.2)), 0.1, 2.0),
        "tangents": noise(splits[1], (P_SIZE, S, TILES, CELLS), 1.0, 6.0, ((0, 2), (2, 16)), jnp.float32),
        "rates": jnp.clip(jnp.exp(math.log(1.0) - 4.6051702 * jax.random.uniform(splits[2], (R, TILES, CELLS), jnp.float32) ** steps_of(splits[2], (R, TILES, CELLS), ((1, 16),), -0.2, 0.2)), 0.01, 1.0),
        "substeps": draw_substeps(jax.random.fold_in(splits[9], 71), 0),
        "courant": jnp.clip(jax.random.uniform(splits[4], (2, TILES, CELLS), jnp.float32, -0.9, 0.9) * steps_of(splits[4], (2, TILES, CELLS), ((1, 16),), -0.4, 0.0), -0.9, 0.9),
        "reactants": plant(jax.random.randint(splits[5], (R, 2), 0, S), jax.random.fold_in(splits[5], 1), 0, S - 1).astype(jnp.int32),
        "products": plant(jax.random.randint(splits[6], (R, 2), 0, S), jax.random.fold_in(splits[6], 1), 0, S - 1).astype(jnp.int32),
        "yields": jnp.clip(jax.random.uniform(splits[7], (R, 2), jnp.float32, 0.2, 0.5), 0.2, 0.5),
        "reaction_index": plant(jax.random.randint(splits[8], (P_SIZE,), 0, R), jax.random.fold_in(splits[8], 1), 0, R - 1).astype(jnp.int32),
    }


def stoich(reactants, products, yields, species_count):
    species = lax.iota(jnp.int32, species_count)[:, None]
    uses_one = (species == reactants[:, 0][None, :]).astype(jnp.float32)
    uses_two = (species == reactants[:, 1][None, :]).astype(jnp.float32)
    produced = yields[:, 0][None, :] * (species == products[:, 0][None, :]).astype(jnp.float32)
    produced = produced + yields[:, 1][None, :] * (species == products[:, 1][None, :]).astype(jnp.float32)
    net_change = produced - uses_one - uses_two
    return (net_change, net_change * uses_one, net_change * uses_two)

def jacobian_apply(vector, reactant_one, reactant_two, rate_rows, reactants, net_change):
    along_one = jnp.take(vector, reactants[:, 0], axis=-2)
    along_two = jnp.take(vector, reactants[:, 1], axis=-2)
    mixed = rate_rows * (reactant_two * along_one + reactant_one * along_two)
    return jnp.einsum('sr,...rx->...sx', net_change, mixed, precision=lax.Precision.HIGHEST)

def relax(right, apply, factor, diagonal, divisor):
    result = right / divisor
    for sweep in range(SWEEPS):
        result = (right + factor * (apply(result) - diagonal * result)) / divisor
    return result

def chemistry(conc, sens, rate_rows, counts, reactants, net_change, net_one, net_two, columns, chosen):
    factor = 1.0 / counts.astype(jnp.float32)
    for index in range(NMAX):
        active = index < counts
        reactant_one = jnp.take(conc, reactants[:, 0], axis=0)
        reactant_two = jnp.take(conc, reactants[:, 1], axis=0)
        fluxes = rate_rows * reactant_one * reactant_two
        diagonal = jnp.dot(net_one, rate_rows * reactant_two, precision=lax.Precision.HIGHEST) + jnp.dot(net_two, rate_rows * reactant_one, precision=lax.Precision.HIGHEST)
        divisor = 1.0 - factor * diagonal

        def apply(vector):
            return jacobian_apply(vector, reactant_one, reactant_two, rate_rows, reactants, net_change)
        base_right = factor * jnp.dot(net_change, fluxes, precision=lax.Precision.HIGHEST)
        forcing = columns[:, :, None] * jnp.take(fluxes, chosen, axis=0)[:, None, :]
        sens_right = factor * (apply(sens) + forcing)
        base_move = relax(base_right, apply, factor, diagonal, divisor)
        sens_move = relax(sens_right, apply, factor, diagonal, divisor)
        conc = jnp.where(active, conc + base_move, conc)
        sens = jnp.where(active, sens + sens_move, sens)
    return (conc, sens)

def advect(extended, courant_local, axis):
    length = extended.shape[axis] - 4

    def cut(offset):
        return lax.slice_in_dim(extended, offset, offset + length, axis=axis)
    minus_two, minus_one, centre, plus_one, plus_two = (cut(0), cut(1), cut(2), cut(3), cut(4))
    third = jnp.where(courant_local > 0, plus_one - 3.0 * centre + 3.0 * minus_one - minus_two, plus_two - 3.0 * plus_one + 3.0 * centre - minus_one)
    return centre - courant_local * (plus_one - minus_one) * 0.5 + courant_local * courant_local * (plus_one - 2.0 * centre + minus_one) * 0.5 + courant_local * (1.0 - courant_local * courant_local) / 6.0 * third

def reference(concentrations, tangents, rates, substeps, courant, reactants, products, yields, reaction_index):
    across = math.isqrt(TILES)
    net_change, net_one, net_two = stoich(reactants, products, yields, S)
    columns = jnp.take(net_change, reaction_index, axis=1).T

    def per_tile(items):
        conc, sens, rate_rows, counts = items
        return chemistry(conc, sens, rate_rows, counts, reactants, net_change, net_one, net_two, columns, reaction_index)
    conc_tiles, sens_tiles = lax.map(per_tile, (jnp.moveaxis(concentrations, 1, 0), jnp.moveaxis(tangents, 2, 0), jnp.moveaxis(rates, 1, 0), substeps))
    field = jnp.concatenate([conc_tiles[:, None], sens_tiles], axis=1)
    fields = field.shape[1]
    grid = field.reshape(across, across, fields, S, CX, CY).transpose(2, 3, 0, 4, 1, 5).reshape(fields, S, across * CX, across * CY)
    courant_grid = courant.reshape(2, across, across, CX, CY).transpose(0, 1, 3, 2, 4).reshape(2, across * CX, across * CY)
    courant_lines = courant_grid[1].reshape(across, CX, across * CY).transpose(1, 0, 2).reshape(CX, across * across * CY)

    def both_sections(values):
        padded = jnp.pad(values, ((0, 0), (2, 2), (0, 0)))
        moved = advect(padded, courant_grid[0], 1)
        lines = moved.reshape(S, across, CX, across * CY).transpose(0, 2, 1, 3).reshape(S, CX, across * across * CY)
        padded = jnp.pad(lines, ((0, 0), (0, 0), (2, 2)))
        done = advect(padded, courant_lines, 2)
        return done.reshape(S, CX, across, across * CY).transpose(0, 2, 1, 3).reshape(S, across * CX, across * CY)
    advected = lax.map(both_sections, grid)
    result = advected.reshape(fields, S, across, CX, across, CY).transpose(0, 1, 2, 4, 3, 5).reshape(fields, S, TILES, CX * CY)
    return (result[0], result[1:])
```

```python
import functools
import math

import jax
import jax.numpy as jnp
import numpy as np
from jax import lax
from jax.experimental import pallas as pl
from jax.experimental.pallas import tpu as pltpu
from jax.sharding import PartitionSpec as P

CX = 16
CY = 16
NMAX = 4
LANES = 128
FAR = 99
UNROLL = 8
BUFFERS = 2
F32 = jnp.float32
BF16 = jnp.bfloat16


def orders():
    last, end = CX - 2, CY - 2
    west = [(i, j) for i in range(2) for j in range(CY)]
    east = [(i, j) for i in range(last, CX) for j in range(CY)]
    south = [(i, j) for j in range(2) for i in range(CX)]
    north = [(i, j) for j in range(end, CY) for i in range(CX)]
    strips = west + east + south + north
    edge = list(dict.fromkeys(strips))
    inner = [(i, j) for i in range(CX) for j in range(CY) if (i, j) not in set(edge)]
    order = edge + inner
    rows, columns = ((last, CX), (0, 2)), ((end, CY), (0, 2))
    corners = [
        [(i, j) for i in range(*rows[d // 2]) for j in range(*columns[d % 2])] for d in range(4)
    ]
    return order, strips, corners


def one_hot(source, wanted):
    place = {cell: k for k, cell in enumerate(source)}
    table = np.zeros((len(source), len(wanted)), np.float32)
    for lane, cell in enumerate(wanted):
        if cell is not None:
            table[place[cell], lane] = 1.0
    return table


def static_tables():
    order, strips, corners = orders()
    cells = [(i, j) for i in range(CX) for j in range(CY)]
    group = order[:LANES]
    permute = one_hot(cells, order)
    strip = one_hot(group, strips)
    corner = []
    for q in range(4):
        lanes = [None] * LANES
        for d in range(4):
            for c in range(4):
                lanes[d * 16 + q * 4 + c] = corners[d][c]
        corner.append(one_hot(group, lanes))
    place = {}
    for lane, cell in enumerate(strips):
        place.setdefault(cell, lane)
    conc_corner = np.zeros((4, LANES, LANES), np.float32)
    for d in range(4):
        for c in range(4):
            conc_corner[d, place[corners[d][c]], d * 16 + c] = 1.0
    entries = list(order)
    entries += [(i - CX, j) for i, j in strips[32:64]]
    entries += [(i + CX, j) for i, j in strips[0:32]]
    entries += [(i, j - CY) for i, j in strips[96:128]]
    entries += [(i, j + CY) for i, j in strips[64:96]]
    shift = ((-CX, -CY), (-CX, CY), (CX, -CY), (CX, CY))
    for d in range(4):
        for q in range(4):
            entries += [(i + shift[d][0], j + shift[d][1]) for i, j in corners[d]]
    entries += [(FAR, FAR)] * (4 * LANES - len(entries))
    middle = cells + [(i, j - CY) for i, j in strips[96:128]]
    middle += [(i, j + CY) for i, j in strips[64:96]]
    middle += [(-FAR, -FAR)] * (3 * LANES - len(middle))
    columns = np.array(entries, np.int32)
    mid_rows = np.array(middle, np.int32).T
    mid_columns = np.array(middle, np.int32)
    out_rows = np.array(cells, np.int32).T
    return {
        "permute": permute,
        "strip": strip,
        "corner": np.concatenate(corner, axis=0),
        "conc_corner": conc_corner.reshape(4 * LANES, LANES),
        "columns": columns,
        "mid_rows": mid_rows,
        "mid_columns": mid_columns,
        "out_rows": out_rows,
    }


def dot(left, right):
    return jnp.dot(left, right, preferred_element_type=F32)


def parts_of(value, count):
    parts = []
    for k in range(count):
        part = value.astype(BF16)
        parts.append(part)
        if k + 1 < count:
            value = value - part.astype(F32)
    return parts


def select_left(exact, value, count):
    return sum(dot(exact, part) for part in parts_of(value, count))


def select_right(value, exact, count):
    return sum(dot(part, exact) for part in parts_of(value, count))


def product(left_parts, value):
    high, low = parts_of(value, 2)
    return dot(left_parts[0], high) + (dot(left_parts[0], low) + dot(left_parts[1], high))


def product_right(value, right_parts):
    high, low = parts_of(value, 2)
    return dot(high, right_parts[0]) + (dot(low, right_parts[0]) + dot(high, right_parts[1]))


def lane_of(rows):
    return lax.broadcasted_iota(jnp.int32, (rows, LANES), 1)


def swap_blocks(arrays):
    lane = lane_of(arrays[0].shape[0])
    low = lane < 64
    even = (lane // 32) % 2 == 0
    a, b, c, d = arrays
    a, c = (
        jnp.where(low, a, pltpu.roll(c, 64, 1)),
        jnp.where(low, pltpu.roll(a, 64, 1), c),
    )
    b, d = (
        jnp.where(low, b, pltpu.roll(d, 64, 1)),
        jnp.where(low, pltpu.roll(b, 64, 1), d),
    )
    a, b = (
        jnp.where(even, a, pltpu.roll(b, 32, 1)),
        jnp.where(even, pltpu.roll(a, 96, 1), b),
    )
    c, d = (
        jnp.where(even, c, pltpu.roll(d, 32, 1)),
        jnp.where(even, pltpu.roll(c, 96, 1), d),
    )
    return [a, b, c, d]


def tangent_copies(source, target, sems):
    return [
        pltpu.make_async_copy(source.at[p], target.at[:, p // 8, :, p % 8, :], sems.at[p // 8])
        for p in range(source.shape[0])
    ]


def pick_columns(raw, table, target):
    species = raw.shape[0]
    for q in range(raw.shape[1]):
        both = jnp.concatenate(
            [
                raw[:, q, 0].reshape(species * 8, LANES),
                raw[:, q, 1].reshape(species * 8, LANES),
            ],
            axis=1,
        )
        picked = select_right(both, table[...], 2)
        target[0:species, q * 8 : (q + 1) * 8, :] = picked.reshape(species, 8, LANES)
    target[species] = jnp.zeros(target.shape[1:], F32)


def tangent_chemistry(
    ilist, ylist, chosen, a_ref, b_ref, flux_ref, fd_ref, fda_ref, h_ref, t, x, used, made, highest
):
    reactions = a_ref.shape[1]
    species = t.shape[0] - 1
    group = t.shape[1]
    zero = jnp.zeros(t.shape[1:], F32)
    sublane = lax.broadcasted_iota(jnp.int32, (8, LANES), 0)

    def clear(s, carry):
        for ref in used + made:
            ref[s] = zero
        return carry

    lax.fori_loop(0, species + 1, clear, 0)

    def apply(source, n):
        def body(step, carry):
            mixes = []
            for k in range(UNROLL):
                r = step * UNROLL + k
                mixes.append(
                    a_ref[n, pl.ds(r, 1), :] * source[ilist[r]]
                    + b_ref[n, pl.ds(r, 1), :] * source[ilist[reactions + r]]
                )
            for k in range(UNROLL):
                r = step * UNROLL + k
                i1, i2 = ilist[r], ilist[reactions + r]
                q1, q2 = ilist[2 * reactions + r], ilist[3 * reactions + r]
                lost, gained = used[k % BUFFERS], made[k % BUFFERS]
                mix = mixes[k]
                one, two = lost[i1], lost[i2]
                three, four = gained[q1], gained[q2]
                lost[i1] = one - mix
                lost[i2] = two - mix
                gained[q1] = three + ylist[r] * mix
                gained[q2] = four + ylist[reactions + r] * mix
            return carry

        lax.fori_loop(0, reactions // UNROLL, body, 0)

    def force(n):
        def body(p8, carry):
            at = sublane == p8
            for q in range(group // 8):
                r = chosen[q * 8 + p8]
                value = jnp.where(at, flux_ref[n, pl.ds(r, 1), :], 0.0)
                i1, i2 = ilist[r], ilist[reactions + r]
                q1, q2 = ilist[2 * reactions + r], ilist[3 * reactions + r]
                lost, gained = used[q % BUFFERS], made[q % BUFFERS]
                rows = slice(q * 8, (q + 1) * 8)
                one, two = lost[i1, rows, :], lost[i2, rows, :]
                three, four = gained[q1, rows, :], gained[q2, rows, :]
                lost[i1, rows, :] = one - value
                lost[i2, rows, :] = two - value
                gained[q1, rows, :] = three + ylist[r] * value
                gained[q2, rows, :] = four + ylist[reactions + r] * value
            return carry

        lax.fori_loop(0, 8, body, 0)

    def total(s):
        value = used[0][s] + made[0][s]
        for k in range(1, BUFFERS):
            value = value + (used[k][s] + made[k][s])
        return value

    def substep(n, carry):
        force(n)
        apply(t, n)

        def first(s, inner):
            right = total(s)
            start = right * fd_ref[n, pl.ds(s, 1), :]
            x[s] = start
            used[0][s] = start * h_ref[n, pl.ds(s, 1), :]
            for ref in used[1:] + made:
                ref[s] = zero
            return inner

        lax.fori_loop(0, species, first, 0, unroll=2)
        apply(x, n)

        def second(s, inner):
            t[s] = t[s] + total(s) * fda_ref[n, pl.ds(s, 1), :]
            for ref in used + made:
                ref[s] = zero
            return inner

        lax.fori_loop(0, species, second, 0, unroll=2)
        return carry

    x[species] = zero
    lax.fori_loop(0, highest, substep, 0)


def edge_kernel(
    ilist, ylist, chosen,
    conc, rates, counts, rrows, rcolumns, yrows, permute, strip, corner, tangents,
    t_out, conc_out, counts_out, a_b, b_b, flux_b, fd_b, fda_b, h_b,
    s0, s1, s2, s3, d0, d1, d2, d3,
    raw, t, x, a_a, b_a, flux_a, fd_a, fda_a, h_a, fold, net_parts, hot, base, *rest,
):
    sems = rest[-1]
    used, made = list(rest[:BUFFERS]), list(rest[BUFFERS : 2 * BUFFERS])
    species = conc.shape[0]
    reactions = a_a.shape[1]
    copies = tangent_copies(tangents, raw, sems)
    for copy in copies:
        copy.start()

    row = lax.broadcasted_iota(jnp.int32, (species, reactions), 0)
    uses_one = row == rrows[0:1, :]
    uses_two = row == rrows[1:2, :]
    net = (
        jnp.where(row == rrows[2:3, :], yrows[0:1, :], 0.0)
        + jnp.where(row == rrows[3:4, :], yrows[1:2, :], 0.0)
        - jnp.where(uses_one, 1.0, 0.0)
        - jnp.where(uses_two, 1.0, 0.0)
    )
    for k, value in enumerate((net, jnp.where(uses_one, net, 0.0), jnp.where(uses_two, net, 0.0))):
        high, low = parts_of(value, 2)
        net_parts[2 * k] = high
        net_parts[2 * k + 1] = low
    lane = lax.broadcasted_iota(jnp.int32, (reactions, species), 1)
    hot[0:reactions] = jnp.where(lane == rcolumns[:, 0:1], 1.0, 0.0).astype(BF16)
    hot[reactions:] = jnp.where(lane == rcolumns[:, 1:2], 1.0, 0.0).astype(BF16)
    same = rcolumns[:, 0:1] == rcolumns[:, 1:2]

    order = permute[...]
    base[...] = select_right(conc[...], order, 3)
    rate = select_right(rates[...], order, 3)
    count = dot(jnp.broadcast_to(counts[...].astype(F32), (8, counts.shape[1])).astype(BF16), order)
    counts_out[...] = count
    count = count[0:1, :]
    factor = 1.0 / count
    highest = jnp.max(count).astype(jnp.int32)

    def keep(n, value, ref_a, ref_b):
        ref_a[n] = value[:, :LANES]
        ref_b[n] = value[:, LANES:]

    def substep(n, carry):
        c = base[...]
        picked = select_left(hot[...], c, 3)
        one, two = picked[:reactions], picked[reactions:]
        a = rate * two
        b = rate * one
        flux = a * one
        nets = (net_parts[0], net_parts[1])
        diagonal = product((net_parts[2], net_parts[3]), a) + product(
            (net_parts[4], net_parts[5]), b
        )
        change = product(nets, flux)
        divisor = 1.0 - factor * diagonal
        fd = factor / divisor
        start = fd * change
        along = select_left(hot[...], start, 2)
        again = product(nets, a * along[:reactions] + b * along[reactions:])
        move = fd * (change + (again - diagonal * start))
        active = n.astype(F32) < count
        base[...] = c + jnp.where(active, move, 0.0)
        keep(n, jnp.where(same, 2.0 * (a + b), a), a_a, a_b)
        keep(n, jnp.where(same, 0.0, b), b_a, b_b)
        keep(n, jnp.where(same, 2.0 * flux, flux), flux_a, flux_b)
        keep(n, fd, fd_a, fd_b)
        keep(n, jnp.where(active, fd, 0.0), fda_a, fda_b)
        keep(n, count - 2.0 * diagonal, h_a, h_b)
        return carry

    lax.fori_loop(0, highest, substep, 0)
    conc_out[...] = base[...]

    for copy in copies:
        copy.wait()
    pick_columns(raw, permute.at[:, 0:LANES], t)
    own = jnp.max(count[:, :LANES]).astype(jnp.int32)
    tangent_chemistry(
        ilist, ylist, chosen, a_a, b_a, flux_a, fd_a, fda_a, h_a, t, x, used, made, own
    )
    t_out[...] = t[0:species]

    rows = species * 8
    blocks = [t[0:species, q * 8 : (q + 1) * 8, :].reshape(rows, LANES) for q in range(4)]
    strips = swap_blocks([select_right(block, strip[...], 2) for block in blocks])
    base_strips = select_right(base[:, 0:LANES], strip[...], 3)
    for ref, value in zip((s0, s1, s2, s3), strips, strict=True):
        ref[0:rows] = value
        ref[rows : rows + species] = base_strips
        ref[rows + species :] = jnp.zeros((ref.shape[0] - rows - species, LANES), F32)
    points = select_right(jnp.concatenate(blocks, axis=1), corner[...], 2)
    short = fold.shape[0] // 8
    fold[0:species] = points.reshape(species, 8, LANES)
    fold[species:] = jnp.zeros((fold.shape[0] - species, 8, LANES), F32)
    place = lane_of(short * 8) // 16
    for d, ref in enumerate((d0, d1, d2, d3)):
        value = jnp.zeros((short * 8, LANES), F32)
        for g in range(8):
            piece = fold[g * short : (g + 1) * short].reshape(short * 8, LANES)
            by = (16 * (g - d)) % LANES
            value = jnp.where(place == g, pltpu.roll(piece, by, 1) if by else piece, value)
        ref[0 : short * 8] = value
        ref[short * 8 : short * 8 + species] = base_strips
        ref[short * 8 + species :] = jnp.zeros(
            (ref.shape[0] - short * 8 - species, LANES), F32
        )


def inner_kernel(
    ilist, ylist, chosen,
    counts, a_b, b_b, flux_b, fd_b, fda_b, h_b, permute, tangents,
    t_out,
    raw, t, x, *rest,
):
    sems = rest[-1]
    used, made = list(rest[:BUFFERS]), list(rest[BUFFERS : 2 * BUFFERS])
    copies = tangent_copies(tangents, raw, sems)
    for copy in copies:
        copy.start()
    own = jnp.max(counts[0:1, LANES:]).astype(jnp.int32)
    for copy in copies:
        copy.wait()
    pick_columns(raw, permute.at[:, LANES:], t)
    tangent_chemistry(
        ilist, ylist, chosen, a_b, b_b, flux_b, fd_b, fda_b, h_b, t, x, used, made, own
    )
    t_out[...] = t[0 : t_out.shape[0]]


def weights(c):
    g = c * (1.0 - c * c) / 6.0
    up = c > 0
    half, square = 0.5 * c, 0.5 * c * c
    return (
        jnp.where(up, -g, 0.0),
        half + square + jnp.where(up, 3.0 * g, -g),
        1.0 - c * c + jnp.where(up, -3.0 * g, 3.0 * g),
        square - half + jnp.where(up, g, -3.0 * g),
        jnp.where(up, 0.0, g),
    )


def advect_kernel(
    t_a, t_b, conc, h0, h1, h2, h3, d0, d1, d2, d3, cx, cy,
    columns, mid_rows, mid_columns, out_rows, conc_corner,
    t_out, conc_out,
    done, unfold, w_parts, sem,
):
    species = conc.shape[0]
    rows = species * 8
    di = columns[:, 0:1] - mid_rows[0:1, :]
    dj = columns[:, 1:2] - mid_rows[1:2, :]
    first = jnp.zeros(di.shape, F32)
    for k, weight in enumerate(weights(cx[...])):
        first = jnp.where((di == k - 2) & (dj == 0), weight, first)
    di = mid_columns[:, 0:1] - out_rows[0:1, :]
    dj = mid_columns[:, 1:2] - out_rows[1:2, :]
    second = jnp.zeros(di.shape, F32)
    for k, weight in enumerate(weights(cy[...])):
        second = jnp.where((dj == k - 2) & (di == 0), weight, second)
    whole = jnp.dot(first, second, precision=lax.Precision.HIGHEST, preferred_element_type=F32)
    high, low = parts_of(whole, 2)
    w_parts[0] = high
    w_parts[1] = low

    halo = 2 * LANES
    line = lax.broadcasted_iota(jnp.int32, (LANES, halo), 0)

    def halo_weights(q):
        mask = (line // 4) % 4 == q
        return [
            jnp.concatenate(
                [
                    w_parts[k, halo : halo + LANES, :],
                    jnp.where(mask, w_parts[k, halo + LANES :, :], jnp.zeros((), BF16)),
                ],
                axis=0,
            )
            for k in range(2)
        ]

    local = [w_parts[k, 0:halo, :] for k in range(2)]

    short = unfold.shape[0] // 8
    place = lane_of(short * 8) // 16
    for g in range(8):
        value = jnp.zeros((short * 8, LANES), F32)
        for d, ref in enumerate((d0, d1, d2, d3)):
            piece = ref[0 : short * 8]
            by = (16 * (d - g)) % LANES
            value = jnp.where(place == d, pltpu.roll(piece, by, 1) if by else piece, value)
        unfold[g * short : (g + 1) * short] = value.reshape(short, 8, LANES)
    strips = swap_blocks([ref[0:rows] for ref in (h0, h1, h2, h3)])
    points = unfold[0:species].reshape(rows, LANES)
    copies = []
    for q in range(4):
        part = slice(q * 8, (q + 1) * 8)
        own = jnp.concatenate(
            [t_a[:, part, :].reshape(rows, LANES), t_b[:, part, :].reshape(rows, LANES)], axis=1
        )
        outer = jnp.concatenate([strips[q], points], axis=1)
        value = product_right(own, local) + product_right(outer, halo_weights(q))
        done[:, q, 0] = value[:, :LANES].reshape(species, 8, LANES)
        done[:, q, 1] = value[:, LANES:].reshape(species, 8, LANES)
        for p8 in range(8):
            copy = pltpu.make_async_copy(
                done.at[:, q, :, p8, :], t_out.at[q * 8 + p8], sem
            )
            copy.start()
            copies.append(copy)

    lane = lane_of(species)
    w, e, s, n = [ref[rows : rows + species] for ref in (h0, h1, h2, h3)]
    sides = jnp.where(
        lane < 64,
        jnp.where(lane < 32, pltpu.roll(w, 96, 1), pltpu.roll(e, 32, 1)),
        jnp.where(lane < 96, pltpu.roll(s, 96, 1), pltpu.roll(n, 32, 1)),
    )
    tips = jnp.zeros((species, LANES), F32)
    for d, ref in enumerate((d0, d1, d2, d3)):
        tips = tips + select_right(
            ref[short * 8 : short * 8 + species],
            conc_corner[d * LANES : (d + 1) * LANES, :],
            2,
        )
    conc_out[...] = product_right(conc[...], local) + product_right(
        jnp.concatenate([sides, tips], axis=1), halo_weights(0)
    )
    for copy in copies:
        copy.wait()


def passed_along(value, axis, by):
    size = lax.axis_size(axis)
    pairs = [(i, i + by) for i in range(size) if 0 <= i + by < size]
    return lax.ppermute(value, axis, pairs)


def padded(value, length, fill):
    return jnp.pad(value, (0, length - value.shape[0]), constant_values=fill)


def per_device(
    concentrations, tangents, rates, substeps, courant, reactants, products, yields, reaction_index
):
    species = concentrations.shape[0]
    cells = CX * CY
    group = tangents.shape[0]
    real = rates.shape[0]
    reactions = -(-real // UNROLL) * UNROLL
    across = math.isqrt(lax.axis_size("tile"))
    table = static_tables()
    vmem = pl.BlockSpec(memory_space=pltpu.VMEM)
    smem = pl.BlockSpec(memory_space=pltpu.SMEM)
    hbm = pl.BlockSpec(memory_space=pl.ANY)
    limit = pltpu.CompilerParams(vmem_limit_bytes=60 * 2**20)

    def shape(*sizes, dtype=F32):
        return jax.ShapeDtypeStruct(sizes, dtype)

    grid = courant[0, 0].reshape(CX, CY)
    south = passed_along(grid[:, CY - 2 :].T.reshape(1, 2 * CX), "tile", 1)
    north = passed_along(grid[:, :2].T.reshape(1, 2 * CX), "tile", -1)
    cx = jnp.concatenate(
        [courant[0], south, north, jnp.zeros((1, 3 * LANES - cells - 4 * CX), F32)], axis=1
    )

    r0, r1, p0, p1 = reactants[:, 0], reactants[:, 1], products[:, 0], products[:, 1]
    same, equal = r0 == r1, p0 == p1
    scale = jnp.where(same, 0.5, 1.0)
    ilist = jnp.concatenate(
        [
            padded(v, reactions, species)
            for v in (r0, jnp.where(same, species, r1), p0, jnp.where(equal, species, p1))
        ]
    )
    ylist = jnp.concatenate(
        [
            padded(scale * v, reactions, 0.0)
            for v in (
                yields[:, 0] + jnp.where(equal, yields[:, 1], 0.0),
                jnp.where(equal, 0.0, yields[:, 1]),
            )
        ]
    )
    more = reactions - real
    rrows = jnp.pad(
        jnp.concatenate([reactants, products], axis=1).T, ((0, 0), (0, more)), constant_values=-1
    )
    rcolumns = jnp.pad(reactants, ((0, more), (0, 0)), constant_values=-1)
    yrows = jnp.pad(yields.T, ((0, 0), (0, more)))
    rate_rows = jnp.pad(rates[:, 0, :], ((0, more), (0, 0)))
    conc = concentrations[:, 0, :]
    sens = tangents.reshape(group, species, cells // LANES, LANES)
    permute = jnp.asarray(table["permute"], BF16)

    short = -(-species // 8)
    rest = -(-species // 8) * 8
    per_group = [shape(NMAX, reactions, LANES)] * 3 + [shape(NMAX, species, LANES)] * 3
    work = [pltpu.VMEM((species + 1, group, LANES), F32)] * (2 + 2 * BUFFERS)
    raw = pltpu.VMEM((species, group // 8, cells // LANES, 8, LANES), F32)
    held = [pltpu.VMEM(s.shape, F32) for s in per_group]
    strip_rows, corner_rows = species * 8 + rest, short * 8 + rest

    outs = pl.pallas_call(
        edge_kernel,
        out_shape=[
            shape(species, group, LANES),
            shape(species, cells),
            shape(8, cells),
            *per_group,
            *([shape(strip_rows, LANES)] * 4),
            *([shape(corner_rows, LANES)] * 4),
        ],
        in_specs=[smem] * 3 + [vmem] * 9 + [hbm],
        out_specs=[vmem] * 17,
        scratch_shapes=[
            raw,
            *work[:2],
            *held,
            pltpu.VMEM((short * 8, 8, LANES), F32),
            pltpu.VMEM((6, species, reactions), BF16),
            pltpu.VMEM((2 * reactions, species), BF16),
            pltpu.VMEM((species, cells), F32),
            *work[2:],
            pltpu.SemaphoreType.DMA((group // 8,)),
        ],
        compiler_params=limit,
        name="edge_columns",
    )(
        ilist, ylist, reaction_index,
        conc, rate_rows, substeps, rrows, rcolumns, yrows, permute,
        jnp.asarray(table["strip"], BF16), jnp.asarray(table["corner"], BF16), sens,
    )
    t_a, conc_end, counts = outs[:3]
    held_b = outs[3:9]
    to_west, to_east, to_south, to_north = outs[9:13]
    tips = outs[13:17]

    h0 = passed_along(to_east, "tile", across)
    h1 = passed_along(to_west, "tile", -across)
    h2 = passed_along(to_north, "tile", 1)
    h3 = passed_along(to_south, "tile", -1)
    offsets = (across + 1, across - 1, -(across - 1), -(across + 1))
    corners = [passed_along(tip, "tile", by) for tip, by in zip(tips, offsets, strict=True)]

    t_b = pl.pallas_call(
        inner_kernel,
        out_shape=shape(species, group, LANES),
        in_specs=[smem] * 3 + [vmem] * 8 + [hbm],
        out_specs=vmem,
        scratch_shapes=[raw, *work, pltpu.SemaphoreType.DMA((group // 8,))],
        compiler_params=limit,
        name="inner_columns",
    )(ilist, ylist, reaction_index, counts, *held_b, permute, sens)

    result, conc_out = pl.pallas_call(
        advect_kernel,
        out_shape=[shape(group, species, cells // LANES, LANES), shape(species, cells)],
        in_specs=[vmem] * 18,
        out_specs=[hbm, vmem],
        scratch_shapes=[
            raw,
            pltpu.VMEM((short * 8, 8, LANES), F32),
            pltpu.VMEM((2, 4 * LANES, cells), BF16),
            pltpu.SemaphoreType.DMA,
        ],
        compiler_params=limit,
        name="advection",
    )(
        t_a, t_b, conc_end, h0, h1, h2, h3, *corners, cx, courant[1],
        jnp.asarray(table["columns"]), jnp.asarray(table["mid_rows"]),
        jnp.asarray(table["mid_columns"]), jnp.asarray(table["out_rows"]),
        jnp.asarray(table["conc_corner"], BF16),
    )
    return (
        conc_out.reshape(species, 1, cells),
        result.reshape(group, species, 1, cells),
    )


def solution(mesh):
    in_specs = (
        P(None, "tile", None),
        P("pgrp", None, "tile", None),
        P(None, "tile", None),
        P("tile", None),
        P(None, "tile", None),
        P(),
        P(),
        P(),
        P("pgrp"),
    )
    out_specs = (P(None, "tile", None), P("pgrp", None, "tile", None))
    return jax.shard_map(
        per_device, mesh=mesh, in_specs=in_specs, out_specs=out_specs, check_vma=False
    )
```

```python
import functools
import math

import jax
import jax.numpy as jnp
import numpy as np
from jax import lax
from jax.experimental import pallas as pl
from jax.experimental.pallas import tpu as pltpu
from jax.sharding import PartitionSpec as P

CX = 16
CY = 16
NMAX = 4
LANES = 128
UNROLL = 8
BUFFERS = 2
SPLIT = 2
F32 = jnp.float32
BF16 = jnp.bfloat16


def orders():
    last, end = CX - 2, CY - 2
    west = [(i, j) for i in range(2) for j in range(CY)]
    east = [(i, j) for i in range(last, CX) for j in range(CY)]
    south = [(i, j) for j in range(2) for i in range(CX)]
    north = [(i, j) for j in range(end, CY) for i in range(CX)]
    strips = west + east + south + north
    edge = list(dict.fromkeys(strips))
    inner = [(i, j) for i in range(CX) for j in range(CY) if (i, j) not in set(edge)]
    return edge + inner, strips


def one_hot(source, wanted):
    place = {cell: k for k, cell in enumerate(source)}
    table = np.zeros((len(source), len(wanted)), np.float32)
    for lane, cell in enumerate(wanted):
        if cell is not None:
            table[place[cell], lane] = 1.0
    return table


def static_tables():
    order, strips = orders()
    cells = [(i, j) for i in range(CX) for j in range(CY)]
    west = [(i - CX, j) for i, j in strips[32:64]]
    east = [(i + CX, j) for i, j in strips[0:32]]
    south = [(i, j - CY) for i, j in strips[96:128]]
    north = [(i, j + CY) for i, j in strips[64:96]]
    blocks = [order[32 * k : 32 * k + 32] for k in range(4)] + [west, east]
    side_in = [(i, j, q) for block in blocks for q in range(4) for i, j in block]
    own_sides = (strips[64:96], strips[96:128])
    side_out = [(i, j, q) for block in own_sides for q in range(4) for i, j in block]
    entries = order + west + east + south + north
    return {
        "permute": one_hot(cells, order),
        "side_pick": one_hot(cells, [(i, j) for i, j, _ in side_out]),
        "side_in": np.array(side_in, np.int32),
        "side_out": np.array(side_out, np.int32).T,
        "entries": np.array(entries, np.int32),
        "cells": np.array(cells, np.int32),
        "cells_rows": np.array(cells, np.int32).T,
    }


def dot(left, right):
    return jnp.dot(left, right, preferred_element_type=F32)


def parts_of(value, count):
    parts = []
    for k in range(count):
        part = value.astype(BF16)
        parts.append(part)
        if k + 1 < count:
            value = value - part.astype(F32)
    return parts


def select_left(exact, value, count):
    return sum(dot(exact, part) for part in parts_of(value, count))


def select_right(value, exact, count):
    return sum(dot(part, exact) for part in parts_of(value, count))


def product(left_parts, value):
    high, low = parts_of(value, 2)
    return dot(left_parts[0], high) + (dot(left_parts[0], low) + dot(left_parts[1], high))


def product_right(value, right_parts):
    high, low = parts_of(value, 2)
    return dot(high, right_parts[0]) + (dot(low, right_parts[0]) + dot(high, right_parts[1]))


def lane_of(rows):
    return lax.broadcasted_iota(jnp.int32, (rows, LANES), 1)


def swap_blocks(arrays):
    lane = lane_of(arrays[0].shape[0])
    low = lane < 64
    even = (lane // 32) % 2 == 0
    a, b, c, d = arrays
    a, c = (
        jnp.where(low, a, pltpu.roll(c, 64, 1)),
        jnp.where(low, pltpu.roll(a, 64, 1), c),
    )
    b, d = (
        jnp.where(low, b, pltpu.roll(d, 64, 1)),
        jnp.where(low, pltpu.roll(b, 64, 1), d),
    )
    a, b = (
        jnp.where(even, a, pltpu.roll(b, 32, 1)),
        jnp.where(even, pltpu.roll(a, 96, 1), b),
    )
    c, d = (
        jnp.where(even, c, pltpu.roll(d, 32, 1)),
        jnp.where(even, pltpu.roll(c, 96, 1), d),
    )
    return [a, b, c, d]


def tangent_copies(source, target, sems):
    return [
        pltpu.make_async_copy(source.at[p], target.at[:, p // 8, :, p % 8, :], sems.at[p // 8])
        for p in range(source.shape[0])
    ]


def up_to(value, step):
    return -(-value // step) * step


def rows_of(reactions, species):
    padded = up_to(species, 8)
    starts = [0, reactions, 2 * reactions]
    starts += [3 * reactions + k * padded for k in range(3)]
    return starts, 3 * reactions + 3 * padded


def several(count):
    return max(k for k in range(1, 14) if count % k == 0)


def tangent_chemistry(ilist, ylist, chosen, held, reactions, t, x, used, made, start, stop, base):
    species = t.shape[0] - 1
    group = t.shape[1]
    (at_a, at_b, at_flux, at_fd, at_fda, at_again), _ = rows_of(reactions, species)
    sublane = lax.broadcasted_iota(jnp.int32, (8, LANES), 0)
    batch = several(species)

    def apply(source, n):
        def body(step, carry):
            mixes, places = [], []
            for k in range(UNROLL):
                r = step * UNROLL + k
                place = [ilist[row, r] for row in range(4)]
                mixes.append(
                    held[n, pl.ds(at_a + r, 1), :] * source[place[0]]
                    + held[n, pl.ds(at_b + r, 1), :] * source[place[1]]
                )
                places.append(place)
            for k0 in range(0, UNROLL, BUFFERS):
                olds = []
                for k in range(BUFFERS):
                    i1, i2, q1, q2 = places[k0 + k]
                    olds.append((used[k][i1], used[k][i2], made[k][q1], made[k][q2]))
                for k in range(BUFFERS):
                    r = step * UNROLL + k0 + k
                    i1, i2, q1, q2 = places[k0 + k]
                    mix, old = mixes[k0 + k], olds[k]
                    used[k][i1] = old[0] - mix
                    used[k][i2] = old[1] - mix
                    made[k][q1] = old[2] + ylist[0, r] * mix
                    made[k][q2] = old[3] + ylist[1, r] * mix
            return carry

        lax.fori_loop(0, reactions // UNROLL, body, 0)

    def force(n):
        def body(p8, carry):
            at = sublane == p8
            for q in range(group // 8):
                r = chosen[q * 8 + p8]
                value = jnp.where(at, held[n, pl.ds(at_flux + r, 1), :], 0.0)
                i1, i2, q1, q2 = [ilist[row, r] for row in range(4)]
                lost, gained = used[q % BUFFERS], made[q % BUFFERS]
                rows = slice(q * 8, (q + 1) * 8)
                one, two = lost[i1, rows, :], lost[i2, rows, :]
                three, four = gained[q1, rows, :], gained[q2, rows, :]
                lost[i1, rows, :] = one - value
                lost[i2, rows, :] = two - value
                gained[q1, rows, :] = three + ylist[0, r] * value
                gained[q2, rows, :] = four + ylist[1, r] * value
            return carry

        lax.fori_loop(0, 8, body, 0)

    def total(s):
        value = used[0][s] + made[0][s]
        for k in range(1, BUFFERS):
            value = value + (used[k][s] + made[k][s])
        return value

    def each(work, target):
        def body(step, carry):
            news = [work(step * batch + k) for k in range(batch)]
            for k, (value, kept) in enumerate(news):
                target[step * batch + k] = value
                used[0][step * batch + k] = kept
            return carry

        lax.fori_loop(0, species // batch, body, 0)

    def substep(index, carry):
        n = index - base
        force(n)
        apply(t, n)

        def first(s):
            right = total(s)
            value = right * held[n, pl.ds(at_fd + s, 1), :]
            return value, used[0][s] + right * held[n, pl.ds(at_again + s, 1), :]

        each(first, x)
        apply(x, n)

        def second(s):
            right = total(s)
            return t[s] + right * held[n, pl.ds(at_fda + s, 1), :], used[0][s] - right

        each(second, t)
        return carry

    lax.fori_loop(start, stop, substep, 0)


def clear(refs):
    zero = jnp.zeros(refs[0].shape[1:], F32)

    def body(s, carry):
        for ref in refs:
            ref[s] = zero
        return carry

    lax.fori_loop(0, refs[0].shape[0], body, 0)


def weights(c):
    g = c * (1.0 - c * c) / 6.0
    up = c > 0
    half, square = 0.5 * c, 0.5 * c * c
    return (
        jnp.where(up, -g, 0.0),
        half + square + jnp.where(up, 3.0 * g, -g),
        1.0 - c * c + jnp.where(up, -3.0 * g, 3.0 * g),
        square - half + jnp.where(up, g, -3.0 * g),
        jnp.where(up, 0.0, g),
    )


def edge_kernel(
    chosen, reactants, products, yields, counts, permute, conc, rates, tangents,
    ilist_out, ylist_out, counts_out, conc_out, t_out, t_b, held_b, s0, s1, s2, s3,
    raw, t, x, held, other, inner, conc_in, rates_in, pairs, net_parts, hot, base,
    ilist, ylist, *rest,
):
    sems = rest[-1]
    used, made = list(rest[:BUFFERS]), list(rest[BUFFERS : 2 * BUFFERS])
    species, real = conc.shape[0], rates.shape[0]
    reactions = rates_in.shape[1]
    halves = conc_in.shape[0]
    starts, _ = rows_of(reactions, species)
    aligned = real // 8 * 8
    for half in range(halves):
        rates_in[half, aligned:] = jnp.zeros((reactions - aligned, LANES), F32)
    small = [
        pltpu.make_async_copy(conc.at[:, half, :], conc_in.at[half], sems.at[4])
        for half in range(halves)
    ] + [
        pltpu.make_async_copy(rates.at[:, half, :], rates_in.at[half, 0:real, :], sems.at[5])
        for half in range(halves)
    ]
    copies = tangent_copies(tangents, raw, sems)
    for copy in small + copies:
        copy.start()

    pairs[...] = jnp.full(pairs.shape, -1, jnp.int32)
    pairs[0:2, 0:real] = reactants[...]
    pairs[2:4, 0:real] = products[...]
    ylist_out[...] = jnp.zeros(ylist_out.shape, F32)
    ylist_out[0:2, 0:real] = yields[...]
    r0, r1, p0, p1 = [pairs[k : k + 1, :] for k in range(4)]
    y0, y1 = ylist_out[0:1, :], ylist_out[1:2, :]
    same, equal = r0 == r1, p0 == p1
    scale = jnp.where(same, 0.5, 1.0)
    for k, value in enumerate(
        (r0, jnp.where(same, species, r1), p0, jnp.where(equal, species, p1))
    ):
        ilist_out[k : k + 1, :] = jnp.where(r0 < 0, species, value)
    ilist_out[4:8, :] = jnp.zeros((4, pairs.shape[1]), jnp.int32)
    ylist_out[0:1, :] = scale * (y0 + jnp.where(equal, y1, 0.0))
    ylist_out[1:2, :] = scale * jnp.where(equal, 0.0, y1)
    lists = [
        pltpu.make_async_copy(ilist_out, ilist, sems.at[6]),
        pltpu.make_async_copy(ylist_out, ylist, sems.at[7]),
    ]
    for copy in lists:
        copy.start()

    row = lax.broadcasted_iota(jnp.int32, (species, reactions), 0)
    r0, r1, p0, p1 = [value[:, 0:reactions] for value in (r0, r1, p0, p1)]
    y0, y1 = y0[:, 0:reactions], y1[:, 0:reactions]
    uses_one = row == r0
    uses_two = row == r1
    net = (
        jnp.where(row == p0, y0, 0.0)
        + jnp.where(row == p1, y1, 0.0)
        - jnp.where(uses_one, 1.0, 0.0)
        - jnp.where(uses_two, 1.0, 0.0)
    )
    for k, value in enumerate((net, jnp.where(uses_one, net, 0.0), jnp.where(uses_two, net, 0.0))):
        high, low = parts_of(value, 2)
        net_parts[2 * k] = high
        net_parts[2 * k + 1] = low
    lane = lane_of(reactions)
    columns = []
    for k in range(2):
        column = jnp.transpose(jnp.broadcast_to(pairs[k : k + 1, :], (LANES, pairs.shape[1])))
        column = column[0:reactions]
        columns.append(column[:, 0:1])
        for at in range(0, species, LANES):
            width = min(LANES, species - at)
            value = jnp.where(column == lane + at, 1.0, 0.0)[:, 0:width]
            hot[k * reactions : (k + 1) * reactions, at : at + width] = value.astype(BF16)
    same = columns[0] == columns[1]

    order = permute[...]
    count = dot(jnp.broadcast_to(counts[...].astype(F32), (8, counts.shape[1])).astype(BF16), order)
    counts_out[...] = count
    count = count[0:1, :]
    factor = 1.0 / count
    highest = jnp.max(count).astype(jnp.int32)
    for copy in small:
        copy.wait()
    base[...] = select_right(jnp.concatenate([conc_in[0], conc_in[1]], axis=1), order, 3)
    rate = select_right(jnp.concatenate([rates_in[0], rates_in[1]], axis=1), order, 3)

    def keep(n, k, value):
        rows = slice(starts[k], starts[k] + value.shape[0])
        held[n, rows, :] = value[:, :LANES]
        other[n, rows, :] = value[:, LANES:]

    def substep(n, carry):
        c = base[...]
        picked = select_left(hot[...], c, 3)
        one, two = picked[:reactions], picked[reactions:]
        a = rate * two
        b = rate * one
        flux = a * one
        nets = (net_parts[0], net_parts[1])
        diagonal = product((net_parts[2], net_parts[3]), a) + product(
            (net_parts[4], net_parts[5]), b
        )
        change = product(nets, flux)
        divisor = 1.0 - factor * diagonal
        fd = factor / divisor
        start = fd * change
        along = select_left(hot[...], start, 2)
        again = product(nets, a * along[:reactions] + b * along[reactions:])
        move = fd * (change + (again - diagonal * start))
        active = n.astype(F32) < count
        base[...] = c + jnp.where(active, move, 0.0)
        keep(n, 0, jnp.where(same, 2.0 * (a + b), a))
        keep(n, 1, jnp.where(same, 0.0, b))
        keep(n, 2, jnp.where(same, 2.0 * flux, flux))
        keep(n, 3, fd)
        keep(n, 4, jnp.where(active, fd, 0.0))
        keep(n, 5, fd * (count - 2.0 * diagonal) - 1.0)
        return carry

    lax.fori_loop(0, highest, substep, 0)
    conc_out[...] = base[...]
    tables = pltpu.make_async_copy(other, held_b, sems.at[8])
    tables.start()

    for copy in copies:
        copy.wait()
    for q in range(raw.shape[1]):
        both = jnp.concatenate(
            [raw[:, q, half].reshape(species * 8, LANES) for half in range(halves)], axis=1
        )
        picked = select_right(both, order, 2)
        rows = slice(q * 8, (q + 1) * 8)
        t[0:species, rows, :] = picked[:, :LANES].reshape(species, 8, LANES)
        inner[:, rows, :] = picked[:, LANES:].reshape(species, 8, LANES)
    inner_out = pltpu.make_async_copy(inner, t_b, sems.at[9])
    inner_out.start()
    t[species] = jnp.zeros(t.shape[1:], F32)
    clear([x, *used, *made])
    for copy in lists:
        copy.wait()
    own = jnp.max(count[:, :LANES]).astype(jnp.int32)
    tangent_chemistry(ilist, ylist, chosen, held, reactions, t, x, used, made, 0, own, 0)
    t_out[...] = t[0:species]

    rows = species * 8
    tail = s0.shape[0] - rows
    strips = swap_blocks(
        [t[0:species, q * 8 : (q + 1) * 8, :].reshape(rows, LANES) for q in range(4)]
    )
    zero = jnp.zeros((species, LANES), F32)
    tails = swap_blocks([base[:, 0:LANES], zero, zero, zero])
    for ref, value, last in zip((s0, s1, s2, s3), strips, tails, strict=True):
        ref[0:rows] = value
        ref[rows:] = jnp.zeros((tail, LANES), F32)
        ref[rows : rows + species] = last
    tables.wait()
    inner_out.wait()


def section(di, dj, c):
    value = jnp.zeros(di.shape, F32)
    for k, weight in enumerate(weights(c)):
        value = jnp.where((di == k - 2) & (dj == 0), weight, value)
    return value


def inner_kernel(
    ilist, ylist, chosen, counts, courant, side_pick, side_in, side_out, s0, s1, s2, s3,
    held_b, t_b,
    t_out, part, side_high, side_low,
    held, t, x, *rest,
):
    sems = rest[-1]
    used, made = list(rest[:BUFFERS]), list(rest[BUFFERS : 2 * BUFFERS])
    species = t_b.shape[0]
    copies = [
        pltpu.make_async_copy(t_b, t.at[0:species], sems.at[0]),
        pltpu.make_async_copy(held_b.at[0:SPLIT], held, sems.at[1]),
    ]
    for copy in copies:
        copy.start()

    cx = jnp.concatenate([courant[0:1, :], courant[1:2, :]], axis=1)
    c = select_right(jnp.broadcast_to(cx, (8, cx.shape[1])), side_pick[...], 3)[0:1, :]
    di = side_in[:, 0:1] - side_out[0:1, :]
    dj = side_in[:, 1:2] - side_out[1:2, :]
    map_ = jnp.where(side_in[:, 2:3] == side_out[2:3, :], section(di, dj, c), 0.0)
    high, low = parts_of(map_, 2)
    near = 4 * LANES
    side_high[...] = high[near:]
    side_low[...] = low[near:]
    strips = jnp.concatenate([s0[...], s1[...], s2[...], s3[...]], axis=1)
    part[...] = product_right(strips, (high[:near], low[:near]))

    t[species] = jnp.zeros(t.shape[1:], F32)
    clear([x, *used, *made])
    for copy in copies:
        copy.wait()
    own = jnp.max(counts[0:1, LANES:]).astype(jnp.int32)
    tangent_chemistry(
        ilist, ylist, chosen, held, reactions_of(held, species), t, x, used, made,
        0, jnp.minimum(own, SPLIT), 0,
    )
    copy = pltpu.make_async_copy(t.at[0:species], t_out, sems.at[0])
    copy.start()
    copy.wait()


def reactions_of(held, species):
    return (held.shape[1] - 3 * up_to(species, 8)) // 3


def side_kernel(part, west, east, side_high, side_low, to_south, to_north):
    both = jnp.concatenate([west[...], east[...]], axis=1)
    value = part[...] + product_right(both, (side_high[...], side_low[...]))
    to_south[...] = value[:, :LANES]
    to_north[...] = value[:, LANES:]


def later_kernel(ilist, ylist, chosen, counts, held_b, t_b, t_out, held, t, x, *rest):
    sems = rest[-1]
    used, made = list(rest[:BUFFERS]), list(rest[BUFFERS : 2 * BUFFERS])
    species = t_b.shape[0]
    copies = [
        pltpu.make_async_copy(t_b, t.at[0:species], sems.at[0]),
        pltpu.make_async_copy(held_b.at[SPLIT:], held, sems.at[1]),
    ]
    for copy in copies:
        copy.start()
    t[species] = jnp.zeros(t.shape[1:], F32)
    clear([x, *used, *made])
    for copy in copies:
        copy.wait()
    own = jnp.max(counts[0:1, LANES:]).astype(jnp.int32)
    tangent_chemistry(
        ilist, ylist, chosen, held, reactions_of(held, species), t, x, used, made,
        SPLIT, own, SPLIT,
    )
    copy = pltpu.make_async_copy(t.at[0:species], t_out, sems.at[0])
    copy.start()
    copy.wait()


def advect_kernel(
    conc, h0, h1, h2, h3, courant, entries, cells, cells_rows, t_a, t_b,
    t_out, conc_out,
    first_in, second_in, done, conc_done, sems,
):
    species = conc.shape[0]
    rows = species * 8
    loads = []
    for q in range(4):
        part = slice(q * 8, (q + 1) * 8)
        loads.append(
            [
                pltpu.make_async_copy(t_a.at[:, part, :], first_in.at[q], sems.at[q]),
                pltpu.make_async_copy(t_b.at[:, part, :], second_in.at[q], sems.at[q]),
            ]
        )
        for copy in loads[q]:
            copy.start()

    cx = jnp.concatenate([courant[0:1, :], courant[1:2, :]], axis=1)
    cy = jnp.concatenate([courant[2:3, :], courant[3:4, :]], axis=1)
    di = entries[:, 0:1] - cells_rows[0:1, :]
    dj = entries[:, 1:2] - cells_rows[1:2, :]
    along_x = section(di, dj, cx)
    late = lax.broadcasted_iota(jnp.int32, di.shape, 0) >= di.shape[0] - 64
    along_y = jnp.where(late, section(dj, di, cy), 0.0)
    both = section(cells[:, 1:2] - cells_rows[1:2, :], cells[:, 0:1] - cells_rows[0:1, :], cy)
    whole = along_y + jnp.dot(
        along_x, both, precision=lax.Precision.HIGHEST, preferred_element_type=F32
    )
    high, low = parts_of(whole, 2)
    own = 2 * LANES
    local, outer = (high[:own], low[:own]), (high[own:], low[own:])

    halo = swap_blocks([h0[...], h1[...], h2[...], h3[...]])
    base = product_right(conc[...], local) + product_right(halo[0][rows : rows + species], outer)
    copies = []
    for half in range(2):
        conc_done[half] = base[:, half * LANES : (half + 1) * LANES]
        copies.append(
            pltpu.make_async_copy(conc_done.at[half], conc_out.at[:, half, :], sems.at[5])
        )
        copies[-1].start()
    for q in range(4):
        for copy in loads[q]:
            copy.wait()
        inside = jnp.concatenate(
            [first_in[q].reshape(rows, LANES), second_in[q].reshape(rows, LANES)], axis=1
        )
        value = product_right(inside, local) + product_right(halo[q][0:rows], outer)
        for half in range(2):
            done[:, q, half] = value[:, half * LANES : (half + 1) * LANES].reshape(
                species, 8, LANES
            )
        for p8 in range(8):
            copies.append(
                pltpu.make_async_copy(done.at[:, q, :, p8, :], t_out.at[q * 8 + p8], sems.at[4])
            )
            copies[-1].start()
    for copy in copies:
        copy.wait()


def passed_along(value, axis, by):
    size = lax.axis_size(axis)
    pairs = [(i, i + by) for i in range(size) if 0 <= i + by < size]
    return lax.ppermute(value, axis, pairs)


def per_device(
    concentrations, tangents, rates, substeps, courant, reactants, products, yields, reaction_index
):
    species = concentrations.shape[0]
    cells = CX * CY
    halves = cells // LANES
    group = tangents.shape[0]
    real = rates.shape[0]
    reactions = up_to(real, UNROLL)
    listed = up_to(reactions, LANES)
    across = math.isqrt(lax.axis_size("tile"))
    table = static_tables()
    vmem = pl.BlockSpec(memory_space=pltpu.VMEM)
    smem = pl.BlockSpec(memory_space=pltpu.SMEM)
    hbm = pl.BlockSpec(memory_space=pl.ANY)
    limit = pltpu.CompilerParams(vmem_limit_bytes=48 * 2**20)
    _, held_rows = rows_of(reactions, species)

    def shape(*sizes, dtype=F32):
        return jax.ShapeDtypeStruct(sizes, dtype)

    def bits(name):
        return jnp.asarray(table[name], BF16)

    conc = concentrations.reshape(species, halves, LANES)
    sens = tangents.reshape(group, species, halves, LANES)
    rate_rows = rates.reshape(real, halves, LANES)
    numbers = courant.reshape(2 * halves, LANES)

    state = shape(species, group, LANES)
    strip = shape(species * 8 + up_to(species, 8), LANES)
    wide = shape(strip.shape[0], 2 * LANES)
    held = shape(NMAX, held_rows, LANES)
    work = [pltpu.VMEM((species + 1, group, LANES), F32)] * (2 + 2 * BUFFERS)
    raw = pltpu.VMEM((species, group // 8, halves, 8, LANES), F32)

    ilist, ylist, counts, conc_end, t_a, t_b, held_b, s0, s1, s2, s3 = pl.pallas_call(
        edge_kernel,
        out_shape=[
            shape(8, listed, dtype=jnp.int32),
            shape(8, listed),
            shape(8, cells),
            shape(species, cells),
            state,
            state,
            held,
            *([strip] * 4),
        ],
        in_specs=[smem] + [vmem] * 5 + [hbm] * 3,
        out_specs=[vmem] * 5 + [hbm] * 2 + [vmem] * 4,
        scratch_shapes=[
            raw,
            *work[:2],
            pltpu.VMEM(held.shape, F32),
            pltpu.VMEM(held.shape, F32),
            pltpu.VMEM(state.shape, F32),
            pltpu.VMEM((halves, species, LANES), F32),
            pltpu.VMEM((halves, reactions, LANES), F32),
            pltpu.VMEM((8, listed), jnp.int32),
            pltpu.VMEM((6, species, reactions), BF16),
            pltpu.VMEM((2 * reactions, species), BF16),
            pltpu.VMEM((species, cells), F32),
            pltpu.SMEM((8, listed), jnp.int32),
            pltpu.SMEM((8, listed), F32),
            *work[2:],
            pltpu.SemaphoreType.DMA((10,)),
        ],
        compiler_params=limit,
        name="edge_columns",
    )(
        reaction_index, reactants.T, products.T, yields.T, substeps, bits("permute"),
        conc, rate_rows, sens,
    )

    west = passed_along(s1, "tile", across)
    east = passed_along(s0, "tile", -across)

    inner_scratch = [
        pltpu.VMEM((SPLIT, held_rows, LANES), F32),
        *work,
        pltpu.SemaphoreType.DMA((2,)),
    ]
    t_b, part, side_high, side_low = pl.pallas_call(
        inner_kernel,
        out_shape=[state, wide] + [shape(2 * LANES, 2 * LANES, dtype=BF16)] * 2,
        in_specs=[smem] * 3 + [vmem] * 9 + [hbm] * 2,
        out_specs=[hbm] + [vmem] * 3,
        scratch_shapes=inner_scratch,
        compiler_params=limit,
        name="inner_columns",
    )(
        ilist, ylist, reaction_index, counts, numbers, bits("side_pick"),
        jnp.asarray(table["side_in"]), jnp.asarray(table["side_out"]), s0, s1, s2, s3,
        held_b, t_b,
    )

    to_south, to_north = pl.pallas_call(
        side_kernel,
        out_shape=[strip, strip],
        in_specs=[vmem] * 5,
        out_specs=[vmem] * 2,
        compiler_params=limit,
        name="y_edges",
    )(part, west, east, side_high, side_low)
    south = passed_along(to_north, "tile", 1)
    north = passed_along(to_south, "tile", -1)

    t_b = pl.pallas_call(
        later_kernel,
        out_shape=state,
        in_specs=[smem] * 3 + [vmem] + [hbm] * 2,
        out_specs=hbm,
        scratch_shapes=inner_scratch,
        compiler_params=limit,
        name="inner_later",
    )(ilist, ylist, reaction_index, counts, held_b, t_b)

    result, conc_out = pl.pallas_call(
        advect_kernel,
        out_shape=[shape(group, species, halves, LANES), shape(species, halves, LANES)],
        in_specs=[vmem] * 9 + [hbm] * 2,
        out_specs=[hbm, hbm],
        scratch_shapes=[
            pltpu.VMEM((group // 8, species, 8, LANES), F32),
            pltpu.VMEM((group // 8, species, 8, LANES), F32),
            raw,
            pltpu.VMEM((halves, species, LANES), F32),
            pltpu.SemaphoreType.DMA((6,)),
        ],
        compiler_params=limit,
        name="advection",
    )(
        conc_end, west, east, south, north, numbers,
        jnp.asarray(table["entries"]), jnp.asarray(table["cells"]),
        jnp.asarray(table["cells_rows"]), t_a, t_b,
    )
    return (
        conc_out.reshape(species, 1, cells),
        result.reshape(group, species, 1, cells),
    )


def solution(mesh):
    in_specs = (
        P(None, "tile", None),
        P("pgrp", None, "tile", None),
        P(None, "tile", None),
        P("tile", None),
        P(None, "tile", None),
        P(),
        P(),
        P(),
        P("pgrp"),
    )
    out_specs = (P(None, "tile", None), P("pgrp", None, "tile", None))
    return jax.shard_map(
        per_device, mesh=mesh, in_specs=in_specs, out_specs=out_specs, check_vma=False
    )
```

```python
import functools
import math

import jax
import jax.numpy as jnp
import numpy as np
from jax import lax
from jax.experimental import pallas as pl
from jax.experimental.pallas import tpu as pltpu
from jax.sharding import PartitionSpec as P

CX = 16
CY = 16
NMAX = 4
LANES = 128
UNROLL = 8
BUFFERS = 2
SPLIT = 2
VMEM_LIMIT = 36 * 2**20
F32 = jnp.float32
BF16 = jnp.bfloat16


def orders():
    last, end = CX - 2, CY - 2
    west = [(i, j) for i in range(2) for j in range(CY)]
    east = [(i, j) for i in range(last, CX) for j in range(CY)]
    south = [(i, j) for j in range(2) for i in range(CX)]
    north = [(i, j) for j in range(end, CY) for i in range(CX)]
    strips = west + east + south + north
    edge = list(dict.fromkeys(strips))
    inner = [(i, j) for i in range(CX) for j in range(CY) if (i, j) not in set(edge)]
    return edge + inner, strips


def one_hot(source, wanted):
    place = {cell: k for k, cell in enumerate(source)}
    table = np.zeros((len(source), len(wanted)), np.float32)
    for lane, cell in enumerate(wanted):
        if cell is not None:
            table[place[cell], lane] = 1.0
    return table


def static_tables():
    order, strips = orders()
    cells = [(i, j) for i in range(CX) for j in range(CY)]
    west = [(i - CX, j) for i, j in strips[32:64]]
    east = [(i + CX, j) for i, j in strips[0:32]]
    south = [(i, j - CY) for i, j in strips[96:128]]
    north = [(i, j + CY) for i, j in strips[64:96]]
    blocks = [order[32 * k : 32 * k + 32] for k in range(4)] + [west, east]
    side_in = [(i, j, q) for block in blocks for q in range(4) for i, j in block]
    own_sides = (strips[64:96], strips[96:128])
    side_out = [(i, j, q) for block in own_sides for q in range(4) for i, j in block]
    entries = order + west + east + south + north
    return {
        "permute": one_hot(cells, order),
        "side_pick": one_hot(cells, [(i, j) for i, j, _ in side_out]),
        "side_in": np.array(side_in, np.int32),
        "side_out": np.array(side_out, np.int32).T,
        "entries": np.array(entries, np.int32),
        "cells": np.array(cells, np.int32),
        "cells_rows": np.array(cells, np.int32).T,
    }


def dot(left, right):
    return jnp.dot(left, right, preferred_element_type=F32)


def parts_of(value, count):
    parts = []
    for k in range(count):
        part = value.astype(BF16)
        parts.append(part)
        if k + 1 < count:
            value = value - part.astype(F32)
    return parts


def select_left(exact, value, count):
    return sum(dot(exact, part) for part in parts_of(value, count))


def select_right(value, exact, count):
    return sum(dot(part, exact) for part in parts_of(value, count))


def product(left_parts, value):
    high, low = parts_of(value, 2)
    return dot(left_parts[0], high) + (dot(left_parts[0], low) + dot(left_parts[1], high))


def product_right(value, right_parts):
    high, low = parts_of(value, 2)
    return dot(high, right_parts[0]) + (dot(low, right_parts[0]) + dot(high, right_parts[1]))


def lane_of(rows):
    return lax.broadcasted_iota(jnp.int32, (rows, LANES), 1)


def swap_blocks(arrays):
    lane = lane_of(arrays[0].shape[0])
    low = lane < 64
    even = (lane // 32) % 2 == 0
    a, b, c, d = arrays
    a, c = (
        jnp.where(low, a, pltpu.roll(c, 64, 1)),
        jnp.where(low, pltpu.roll(a, 64, 1), c),
    )
    b, d = (
        jnp.where(low, b, pltpu.roll(d, 64, 1)),
        jnp.where(low, pltpu.roll(b, 64, 1), d),
    )
    a, b = (
        jnp.where(even, a, pltpu.roll(b, 32, 1)),
        jnp.where(even, pltpu.roll(a, 96, 1), b),
    )
    c, d = (
        jnp.where(even, c, pltpu.roll(d, 32, 1)),
        jnp.where(even, pltpu.roll(c, 96, 1), d),
    )
    return [a, b, c, d]


def tangent_copies(source, target, sems):
    return [
        pltpu.make_async_copy(source.at[p], target.at[:, p // 8, :, p % 8, :], sems.at[p // 8])
        for p in range(source.shape[0])
    ]


def up_to(value, step):
    return -(-value // step) * step


def rows_of(reactions, species):
    padded = up_to(species, 8)
    starts = [0, reactions, 2 * reactions]
    starts += [3 * reactions + k * padded for k in range(3)]
    return starts, 3 * reactions + 3 * padded


def tangent_chemistry(ilist, ylist, chosen, held, reactions, group, t, x, used, made, start, stop):
    species = t.shape[0] // group - 1
    listed = ilist.shape[0] // 4
    at_a, at_b, at_flux, at_fd, at_fda, at_again = [at // 8 for at in rows_of(reactions, species)[0]]
    sublane = lax.broadcasted_iota(jnp.int32, (8, LANES), 0)

    def rows(place):
        return pl.ds(pl.multiple_of(place, group), group)

    def apply(source, n):
        def body(step, carry):
            mixes, places = [], []
            for k in range(UNROLL):
                r = step * UNROLL + k
                tile, k8 = step * (UNROLL // 8) + k // 8, k % 8
                place = [rows(ilist[row * listed + r]) for row in range(4)]
                mixes.append(
                    held[n, at_a + tile, k8 : k8 + 1, :] * source[place[0], :]
                    + held[n, at_b + tile, k8 : k8 + 1, :] * source[place[1], :]
                )
                places.append(place)
            for k0 in range(0, UNROLL, BUFFERS):
                olds = []
                for k in range(BUFFERS):
                    i1, i2, q1, q2 = places[k0 + k]
                    lost, gained = used[k], made[k]
                    olds.append((lost[i1, :], lost[i2, :], gained[q1, :], gained[q2, :]))
                for k in range(BUFFERS):
                    r = step * UNROLL + k0 + k
                    i1, i2, q1, q2 = places[k0 + k]
                    mix, old = mixes[k0 + k], olds[k]
                    used[k][i1, :] = old[0] - mix
                    used[k][i2, :] = old[1] - mix
                    made[k][q1, :] = old[2] + ylist[r] * mix
                    made[k][q2, :] = old[3] + ylist[listed + r] * mix
            return carry

        lax.fori_loop(0, reactions // UNROLL, body, 0)

    def force(n):
        def body(p8, carry):
            at = sublane == p8
            for q in range(group // 8):
                r = chosen[q * 8 + p8]
                flux = held[n, at_flux + r // 8, pl.ds(r % 8, 1), :]
                value = jnp.where(at, flux, 0.0)
                i1, i2, q1, q2 = [
                    pl.ds(pl.multiple_of(ilist[row * listed + r] + q * 8, 8), 8) for row in range(4)
                ]
                lost, gained = used[q % BUFFERS], made[q % BUFFERS]
                one, two = lost[i1, :], lost[i2, :]
                three, four = gained[q1, :], gained[q2, :]
                lost[i1, :] = one - value
                lost[i2, :] = two - value
                gained[q1, :] = three + ylist[r] * value
                gained[q2, :] = four + ylist[listed + r] * value
            return carry

        lax.fori_loop(0, 8, body, 0)

    def total(at):
        value = used[0][at, :] + made[0][at, :]
        for k in range(1, BUFFERS):
            value = value + (used[k][at, :] + made[k][at, :])
        return value

    def each(work, target):
        def batch(step, count):
            places = [rows((step * 8 + k) * group) for k in range(count)]
            news = [work(place, step, k) for k, place in enumerate(places)]
            for place, (value, kept) in zip(places, news, strict=True):
                target[place, :] = value
                used[0][place, :] = kept

        def body(step, carry):
            batch(step, 8)
            return carry

        lax.fori_loop(0, species // 8, body, 0)
        if species % 8:
            batch(species // 8, species % 8)

    def substep(n, carry):
        force(n)
        apply(t, n)

        def first(at, tile, k):
            right = total(at)
            value = right * held[n, at_fd + tile, k : k + 1, :]
            return value, used[0][at, :] + right * held[n, at_again + tile, k : k + 1, :]

        each(first, x)
        apply(x, n)

        def second(at, tile, k):
            right = total(at)
            value = t[at, :] + right * held[n, at_fda + tile, k : k + 1, :]
            return value, used[0][at, :] - right

        each(second, t)
        return carry

    lax.fori_loop(start, stop, substep, 0)


def clear(refs):
    zero = jnp.zeros((LANES, LANES), F32)
    length = refs[0].shape[0]
    for at in range(0, length, LANES):
        for ref in refs:
            ref[at : min(at + LANES, length), :] = zero[0 : min(LANES, length - at)]


def weights(c):
    g = c * (1.0 - c * c) / 6.0
    up = c > 0
    half, square = 0.5 * c, 0.5 * c * c
    return (
        jnp.where(up, -g, 0.0),
        half + square + jnp.where(up, 3.0 * g, -g),
        1.0 - c * c + jnp.where(up, -3.0 * g, 3.0 * g),
        square - half + jnp.where(up, g, -3.0 * g),
        jnp.where(up, 0.0, g),
    )


def edge_kernel(
    chosen_in, reactants_in, products_in, yields_in, counts_in, permute_in, conc, rates, tangents,
    ilist_out, ylist_out, counts_out, conc_out, t, inner, other, s0, s1, s2, s3,
    raw, x, held, conc_in, rates_in, reactants, products, yields, counts, permute,
    pairs, columns, net_parts, hot, uses, base, chosen, ilist, ylist, *rest,
):
    sems = rest[-1]
    used, made = list(rest[:BUFFERS]), list(rest[BUFFERS : 2 * BUFFERS])
    species, real = conc.shape[0], rates.shape[0]
    group = tangents.shape[0]
    reactions = rates_in.shape[1]
    halves = conc_in.shape[0]
    starts, _ = rows_of(reactions, species)
    aligned = real // 8 * 8
    for half in range(halves):
        rates_in[half, aligned:] = jnp.zeros((reactions - aligned, LANES), F32)
    small = [
        pltpu.make_async_copy(conc.at[:, half, :], conc_in.at[half], sems.at[4])
        for half in range(halves)
    ] + [
        pltpu.make_async_copy(rates.at[:, half, :], rates_in.at[half, 0:real, :], sems.at[5])
        for half in range(halves)
    ]
    copies = tangent_copies(tangents, raw, sems)
    tiny = [
        pltpu.make_async_copy(source, target, sems.at[8])
        for source, target in (
            (chosen_in, chosen),
            (reactants_in, reactants),
            (products_in, products),
            (yields_in, yields),
            (counts_in, counts),
            (permute_in, permute),
        )
    ]
    for copy in tiny + small + copies:
        copy.start()
    for copy in tiny:
        copy.wait()

    pairs[...] = jnp.full(pairs.shape, -1, jnp.int32)
    pairs[0:2, 0:real] = reactants[...]
    pairs[2:4, 0:real] = products[...]
    columns[...] = jnp.zeros(columns.shape, F32)
    columns[0:2, 0:real] = yields[...]
    r0, r1, p0, p1 = [pairs[k : k + 1, :] for k in range(4)]
    y0, y1 = columns[0:1, :], columns[1:2, :]
    same, equal = r0 == r1, p0 == p1
    scale = jnp.where(same, 0.5, 1.0)
    parts = pairs.shape[1] // LANES
    ilist_out[...] = jnp.zeros(ilist_out.shape, jnp.int32)
    ylist_out[...] = jnp.zeros(ylist_out.shape, F32)
    for k, value in enumerate(
        (r0, jnp.where(same, species, r1), p0, jnp.where(equal, species, p1))
    ):
        value = jnp.where(r0 < 0, species, value) * group
        for part in range(parts):
            row = k * parts + part
            ilist_out[row : row + 1, :] = value[:, part * LANES : (part + 1) * LANES]
    for k, value in enumerate(
        (scale * (y0 + jnp.where(equal, y1, 0.0)), scale * jnp.where(equal, 0.0, y1))
    ):
        for part in range(parts):
            row = k * parts + part
            ylist_out[row : row + 1, :] = value[:, part * LANES : (part + 1) * LANES]
    lists = [
        pltpu.make_async_copy(source.at[row], target.at[pl.ds(row * LANES, LANES)], sems.at[6])
        for source, target, count in ((ilist_out, ilist, 4), (ylist_out, ylist, 2))
        for row in range(count * parts)
    ]
    for copy in lists:
        copy.start()

    row = lax.broadcasted_iota(jnp.int32, (species, reactions), 0)
    r0, r1, p0, p1 = [value[:, 0:reactions] for value in (r0, r1, p0, p1)]
    y0, y1 = y0[:, 0:reactions], y1[:, 0:reactions]
    uses_one = row == r0
    uses_two = row == r1
    net = (
        jnp.where(row == p0, y0, 0.0)
        + jnp.where(row == p1, y1, 0.0)
        - jnp.where(uses_one, 1.0, 0.0)
        - jnp.where(uses_two, 1.0, 0.0)
    )
    high, low = parts_of(net, 2)
    net_parts[0] = high
    net_parts[1] = low
    uses[0] = jnp.where(uses_one, 1.0, 0.0).astype(BF16)
    uses[1] = jnp.where(uses_two, 1.0, 0.0).astype(BF16)
    for k, value in enumerate((r0, r1)):
        change = (
            jnp.where(value == p0, y0, 0.0)
            + jnp.where(value == p1, y1, 0.0)
            - jnp.where(value == r0, 1.0, 0.0)
            - jnp.where(value == r1, 1.0, 0.0)
        )
        columns[k : k + 1, 0:reactions] = value.astype(F32)
        columns[2 + k : 3 + k, 0:reactions] = change
    turned = jnp.transpose(columns[...])[0:reactions]
    column = [turned[:, k : k + 1] for k in range(4)]
    lane = lane_of(reactions).astype(F32)
    for k in range(2):
        for at in range(0, species, LANES):
            width = min(LANES, species - at)
            value = jnp.where(column[k] == lane + float(at), 1.0, 0.0)[:, 0:width]
            hot[k * reactions : (k + 1) * reactions, at : at + width] = value.astype(BF16)
    same = column[0] == column[1]
    own_one, own_two = column[2], column[3]

    order = permute[...].astype(BF16)
    count = dot(jnp.broadcast_to(counts[...].astype(F32), (8, counts.shape[1])).astype(BF16), order)
    counts_out[...] = count
    count = count[0:1, :]
    factor = 1.0 / count
    highest = jnp.max(count).astype(jnp.int32)
    for copy in small:
        copy.wait()
    base[...] = select_right(jnp.concatenate([conc_in[0], conc_in[1]], axis=1), order, 3)
    rate = select_right(jnp.concatenate([rates_in[0], rates_in[1]], axis=1), order, 3)

    def keep(n, k, value):
        for ref, part in ((held, value[:, :LANES]), (other, value[:, LANES:])):
            full = value.shape[0] // 8 * 8
            first, tile = starts[k] // 8, (starts[k] + full) // 8
            ref[n, first:tile] = part[:full].reshape(full // 8, 8, LANES)
            if full < value.shape[0]:
                ref[n, tile, 0 : value.shape[0] - full, :] = part[full:]

    def substep(n, carry):
        c = base[...]
        picked = select_left(hot[...], c, 2)
        one, two = picked[:reactions], picked[reactions:]
        a = rate * two
        b = rate * one
        flux = a * one
        nets = (net_parts[0], net_parts[1])
        diagonal = select_left(uses[0], own_one * a, 2) + select_left(uses[1], own_two * b, 2)
        change = product(nets, flux)
        divisor = 1.0 - factor * diagonal
        fd = factor / divisor
        start = fd * change
        along = select_left(hot[...], start, 2)
        again = product(nets, a * along[:reactions] + b * along[reactions:])
        move = fd * (change + (again - diagonal * start))
        active = n.astype(F32) < count
        base[...] = c + jnp.where(active, move, 0.0)
        keep(n, 0, jnp.where(same, 2.0 * (a + b), a))
        keep(n, 1, jnp.where(same, 0.0, b))
        keep(n, 2, jnp.where(same, 2.0 * flux, flux))
        keep(n, 3, fd)
        keep(n, 4, jnp.where(active, fd, 0.0))
        keep(n, 5, fd * (count - 2.0 * diagonal) - 1.0)
        return carry

    lax.fori_loop(0, highest, substep, 0)
    conc_out[...] = base[...]

    for copy in copies:
        copy.wait()
    for q in range(raw.shape[1]):
        both = jnp.concatenate(
            [raw[:, q, half].reshape(species * 8, LANES) for half in range(halves)], axis=1
        )
        picked = select_right(both, order, 2)
        rows = slice(q * 8, (q + 1) * 8)
        for ref, part in ((t, picked[:, :LANES]), (inner, picked[:, LANES:])):
            by_species(ref, group)[0:species, rows, :] = part.reshape(species, 8, LANES)
    for ref in (t, inner):
        ref[species * group :, :] = jnp.zeros((group, LANES), F32)
    clear([x, *used, *made])
    for copy in lists:
        copy.wait()
    own = jnp.max(count[:, :LANES]).astype(jnp.int32)
    tangent_chemistry(ilist, ylist, chosen, held, reactions, group, t, x, used, made, 0, own)

    rows = species * 8
    tail = s0.shape[0] - rows
    strips = swap_blocks(
        [
            by_species(t, group)[0:species, q * 8 : (q + 1) * 8, :].reshape(rows, LANES)
            for q in range(4)
        ]
    )
    zero = jnp.zeros((species, LANES), F32)
    tails = swap_blocks([base[:, 0:LANES], zero, zero, zero])
    for ref, value, last in zip((s0, s1, s2, s3), strips, tails, strict=True):
        ref[0:rows] = value
        ref[rows:] = jnp.zeros((tail, LANES), F32)
        ref[rows : rows + species] = last


def by_species(ref, group):
    return ref.reshape(ref.shape[0] // group, group, LANES)


def section(di, dj, c):
    value = jnp.zeros(di.shape, F32)
    for k, weight in enumerate(weights(c)):
        value = jnp.where((di == k - 2) & (dj == 0), weight, value)
    return value


def inner_kernel(
    ilist, ylist, chosen, counts, courant, side_pick, side_in, side_out, s0, s1, s2, s3,
    held, t_b,
    t, part, side_high, side_low,
    x, *rest,
):
    used, made = list(rest[:BUFFERS]), list(rest[BUFFERS : 2 * BUFFERS])
    group = chosen.shape[0]
    species = t_b.shape[0] // group - 1
    cx = jnp.concatenate([courant[0:1, :], courant[1:2, :]], axis=1)
    c = select_right(jnp.broadcast_to(cx, (8, cx.shape[1])), side_pick[...].astype(BF16), 3)[0:1, :]
    di = side_in[:, 0:1] - side_out[0:1, :]
    dj = side_in[:, 1:2] - side_out[1:2, :]
    map_ = jnp.where(side_in[:, 2:3] == side_out[2:3, :], section(di, dj, c), 0.0)
    high, low = parts_of(map_, 2)
    near = 4 * LANES
    side_high[...] = high[near:]
    side_low[...] = low[near:]
    strips = jnp.concatenate([s0[...], s1[...], s2[...], s3[...]], axis=1)
    part[...] = product_right(strips, (high[:near], low[:near]))

    t[...] = t_b[...]
    clear([x, *used, *made])
    own = jnp.max(counts[0:1, LANES:]).astype(jnp.int32)
    tangent_chemistry(
        ilist, ylist, chosen, held, reactions_of(held, species), group, t, x, used, made,
        0, jnp.minimum(own, SPLIT),
    )


def reactions_of(held, species):
    return (held.shape[1] * 8 - 3 * up_to(species, 8)) // 3


def side_kernel(part, west, east, side_high, side_low, to_south, to_north):
    both = jnp.concatenate([west[...], east[...]], axis=1)
    value = part[...] + product_right(both, (side_high[...], side_low[...]))
    to_south[...] = value[:, :LANES]
    to_north[...] = value[:, LANES:]


def later_kernel(ilist, ylist, chosen, counts, held, t_b, t, x, *rest):
    used, made = list(rest[:BUFFERS]), list(rest[BUFFERS : 2 * BUFFERS])
    group = chosen.shape[0]
    species = t_b.shape[0] // group - 1
    t[...] = t_b[...]
    clear([x, *used, *made])
    own = jnp.max(counts[0:1, LANES:]).astype(jnp.int32)
    tangent_chemistry(
        ilist, ylist, chosen, held, reactions_of(held, species), group, t, x, used, made,
        SPLIT, own,
    )


def advect_kernel(
    conc, h0, h1, h2, h3, courant, entries, cells, cells_rows, t_a, t_b,
    t_out, conc_out,
    done, conc_done, sems,
):
    species = conc.shape[0]
    rows = species * 8
    cx = jnp.concatenate([courant[0:1, :], courant[1:2, :]], axis=1)
    cy = jnp.concatenate([courant[2:3, :], courant[3:4, :]], axis=1)
    di = entries[:, 0:1] - cells_rows[0:1, :]
    dj = entries[:, 1:2] - cells_rows[1:2, :]
    along_x = section(di, dj, cx)
    late = lax.broadcasted_iota(jnp.int32, di.shape, 0) >= di.shape[0] - 64
    along_y = jnp.where(late, section(dj, di, cy), 0.0)
    both = section(cells[:, 1:2] - cells_rows[1:2, :], cells[:, 0:1] - cells_rows[0:1, :], cy)
    whole = along_y + jnp.dot(
        along_x, both, precision=lax.Precision.HIGHEST, preferred_element_type=F32
    )
    high, low = parts_of(whole, 2)
    own = 2 * LANES
    local, outer = (high[:own], low[:own]), (high[own:], low[own:])

    halo = swap_blocks([h0[...], h1[...], h2[...], h3[...]])
    base = product_right(conc[...], local) + product_right(halo[0][rows : rows + species], outer)
    copies = []
    for half in range(2):
        conc_done[half] = base[:, half * LANES : (half + 1) * LANES]
        copies.append(
            pltpu.make_async_copy(conc_done.at[half], conc_out.at[:, half, :], sems.at[1])
        )
        copies[-1].start()
    for q in range(4):
        part = slice(q * 8, (q + 1) * 8)
        inside = jnp.concatenate(
            [by_species(ref, t_out.shape[0])[0:species, part, :].reshape(rows, LANES) for ref in (t_a, t_b)],
            axis=1,
        )
        value = product_right(inside, local) + product_right(halo[q][0:rows], outer)
        for half in range(2):
            done[:, q, half] = value[:, half * LANES : (half + 1) * LANES].reshape(
                species, 8, LANES
            )
        for p8 in range(8):
            copies.append(
                pltpu.make_async_copy(done.at[:, q, :, p8, :], t_out.at[q * 8 + p8], sems.at[0])
            )
            copies[-1].start()
    for copy in copies:
        copy.wait()


def passed_along(value, axis, by):
    size = lax.axis_size(axis)
    pairs = [(i, i + by) for i in range(size) if 0 <= i + by < size]
    return lax.ppermute(value, axis, pairs)


def per_device(
    concentrations, tangents, rates, substeps, courant, reactants, products, yields, reaction_index
):
    species = concentrations.shape[0]
    cells = CX * CY
    halves = cells // LANES
    group = tangents.shape[0]
    real = rates.shape[0]
    reactions = up_to(real, UNROLL)
    listed = up_to(reactions, LANES)
    lists = up_to(4 * listed // LANES, 8)
    across = math.isqrt(lax.axis_size("tile"))
    table = static_tables()
    vmem = pl.BlockSpec(memory_space=pltpu.VMEM)
    smem = pl.BlockSpec(memory_space=pltpu.SMEM)
    hbm = pl.BlockSpec(memory_space=pltpu.HBM)
    limit = pltpu.CompilerParams(vmem_limit_bytes=VMEM_LIMIT)
    _, held_rows = rows_of(reactions, species)

    def shape(*sizes, dtype=F32):
        return jax.ShapeDtypeStruct(sizes, dtype)

    conc = concentrations.reshape(species, halves, LANES)
    sens = tangents.reshape(group, species, halves, LANES)
    rate_rows = rates.reshape(real, halves, LANES)
    numbers = courant.reshape(2 * halves, LANES)

    state = shape((species + 1) * group, LANES)
    strip = shape(species * 8 + up_to(species, 8), LANES)
    wide = shape(strip.shape[0], 2 * LANES)
    held = shape(NMAX, held_rows // 8, 8, LANES)
    work = [pltpu.VMEM(state.shape, F32)] * (1 + 2 * BUFFERS)
    raw = pltpu.VMEM((species, group // 8, halves, 8, LANES), F32)

    ilist, ylist, counts, conc_end, t_a, t_b, held_b, s0, s1, s2, s3 = pl.pallas_call(
        edge_kernel,
        out_shape=[
            shape(lists, LANES, dtype=jnp.int32),
            shape(lists, LANES),
            shape(8, cells),
            shape(species, cells),
            state,
            state,
            held,
            *([strip] * 4),
        ],
        in_specs=[hbm] * 9,
        out_specs=[vmem] * 11,
        scratch_shapes=[
            raw,
            work[0],
            pltpu.VMEM(held.shape, F32),
            pltpu.VMEM((halves, species, LANES), F32),
            pltpu.VMEM((halves, reactions, LANES), F32),
            pltpu.VMEM((2, real), jnp.int32),
            pltpu.VMEM((2, real), jnp.int32),
            pltpu.VMEM((2, real), F32),
            pltpu.VMEM((1, cells), jnp.int32),
            pltpu.VMEM((cells, cells), F32),
            pltpu.VMEM((8, listed), jnp.int32),
            pltpu.VMEM((LANES, listed), F32),
            pltpu.VMEM((2, species, reactions), BF16),
            pltpu.VMEM((2 * reactions, species), BF16),
            pltpu.VMEM((2, species, reactions), BF16),
            pltpu.VMEM((species, cells), F32),
            pltpu.SMEM((group,), jnp.int32),
            pltpu.SMEM((4 * listed,), jnp.int32),
            pltpu.SMEM((2 * listed,), F32),
            *work[1:],
            pltpu.SemaphoreType.DMA((9,)),
        ],
        compiler_params=limit,
        name="edge_columns",
    )(
        *[
            pltpu.with_memory_space_constraint(value, pltpu.HBM)
            for value in (
                reaction_index, reactants.T, products.T, yields.T, substeps,
                jnp.asarray(table["permute"]), conc, rate_rows, sens,
            )
        ]
    )

    ilist, ylist = ilist.reshape(-1)[: 4 * listed], ylist.reshape(-1)
    west = passed_along(s1, "tile", across)
    east = passed_along(s0, "tile", -across)

    t_b, part, side_high, side_low = pl.pallas_call(
        inner_kernel,
        out_shape=[state, wide] + [shape(2 * LANES, 2 * LANES, dtype=BF16)] * 2,
        in_specs=[smem] * 3 + [vmem] * 11,
        out_specs=[vmem] * 4,
        scratch_shapes=work,
        compiler_params=limit,
        name="inner_columns",
    )(
        ilist, ylist, reaction_index, counts, numbers, jnp.asarray(table["side_pick"]),
        jnp.asarray(table["side_in"]), jnp.asarray(table["side_out"]), s0, s1, s2, s3,
        held_b, t_b,
    )

    to_south, to_north = pl.pallas_call(
        side_kernel,
        out_shape=[strip, strip],
        in_specs=[vmem] * 5,
        out_specs=[vmem] * 2,
        compiler_params=limit,
        name="y_edges",
    )(part, west, east, side_high, side_low)
    south = passed_along(to_north, "tile", 1)
    north = passed_along(to_south, "tile", -1)

    t_b = pl.pallas_call(
        later_kernel,
        out_shape=state,
        in_specs=[smem] * 3 + [vmem] * 3,
        out_specs=vmem,
        scratch_shapes=work,
        compiler_params=limit,
        name="inner_later",
    )(ilist, ylist, reaction_index, counts, held_b, t_b)

    result, conc_out = pl.pallas_call(
        advect_kernel,
        out_shape=[shape(group, species, halves, LANES), shape(species, halves, LANES)],
        in_specs=[vmem] * 11,
        out_specs=[hbm, hbm],
        scratch_shapes=[
            raw,
            pltpu.VMEM((halves, species, LANES), F32),
            pltpu.SemaphoreType.DMA((2,)),
        ],
        compiler_params=limit,
        name="advection",
    )(
        conc_end, west, east, south, north, numbers,
        jnp.asarray(table["entries"]), jnp.asarray(table["cells"]),
        jnp.asarray(table["cells_rows"]), t_a, t_b,
    )
    return (
        conc_out.reshape(species, 1, cells),
        result.reshape(group, species, 1, cells),
    )


def solution(mesh):
    in_specs = (
        P(None, "tile", None),
        P("pgrp", None, "tile", None),
        P(None, "tile", None),
        P("tile", None),
        P(None, "tile", None),
        P(),
        P(),
        P(),
        P("pgrp"),
    )
    out_specs = (P(None, "tile", None), P("pgrp", None, "tile", None))
    return jax.shard_map(
        per_device, mesh=mesh, in_specs=in_specs, out_specs=out_specs, check_vma=False
    )
```

```python
import functools
import math

import jax
import jax.numpy as jnp
import numpy as np
from jax import lax
from jax.experimental import pallas as pl
from jax.experimental.pallas import tpu as pltpu
from jax.sharding import PartitionSpec as P

CX = 16
CY = 16
NMAX = 4
LANES = 128
UNROLL = 8
BUFFERS = 2
SPLIT = 2
VMEM_LIMIT = 36 * 2**20
F32 = jnp.float32
BF16 = jnp.bfloat16


def orders():
    last, end = CX - 2, CY - 2
    west = [(i, j) for i in range(2) for j in range(CY)]
    east = [(i, j) for i in range(last, CX) for j in range(CY)]
    south = [(i, j) for j in range(2) for i in range(CX)]
    north = [(i, j) for j in range(end, CY) for i in range(CX)]
    strips = west + east + south + north
    edge = list(dict.fromkeys(strips))
    inner = [(i, j) for i in range(CX) for j in range(CY) if (i, j) not in set(edge)]
    return edge + inner, strips


def one_hot(source, wanted):
    place = {cell: k for k, cell in enumerate(source)}
    table = np.zeros((len(source), len(wanted)), np.float32)
    for lane, cell in enumerate(wanted):
        if cell is not None:
            table[place[cell], lane] = 1.0
    return table


def static_tables():
    order, strips = orders()
    cells = [(i, j) for i in range(CX) for j in range(CY)]
    west = [(i - CX, j) for i, j in strips[32:64]]
    east = [(i + CX, j) for i, j in strips[0:32]]
    south = [(i, j - CY) for i, j in strips[96:128]]
    north = [(i, j + CY) for i, j in strips[64:96]]
    blocks = [order[32 * k : 32 * k + 32] for k in range(4)] + [west, east]
    side_in = [(i, j, q) for block in blocks for q in range(4) for i, j in block]
    own_sides = (strips[64:96], strips[96:128])
    side_out = [(i, j, q) for block in own_sides for q in range(4) for i, j in block]
    entries = order + west + east + south + north
    return {
        "permute": one_hot(cells, order),
        "side_pick": one_hot(cells, [(i, j) for i, j, _ in side_out]),
        "side_in": np.array(side_in, np.int32),
        "side_out": np.array(side_out, np.int32).T,
        "entries": np.array(entries, np.int32),
        "cells": np.array(cells, np.int32),
        "cells_rows": np.array(cells, np.int32).T,
    }


def dot(left, right):
    return jnp.dot(left, right, preferred_element_type=F32)


def parts_of(value, count):
    parts = []
    for k in range(count):
        part = value.astype(BF16)
        parts.append(part)
        if k + 1 < count:
            value = value - part.astype(F32)
    return parts


def select_left(exact, value, count):
    return sum(dot(exact, part) for part in parts_of(value, count))


def select_right(value, exact, count):
    return sum(dot(part, exact) for part in parts_of(value, count))


def product(left_parts, value):
    high, low = parts_of(value, 2)
    return dot(left_parts[0], high) + (dot(left_parts[0], low) + dot(left_parts[1], high))


def product_right(value, right_parts):
    high, low = parts_of(value, 2)
    return dot(high, right_parts[0]) + (dot(low, right_parts[0]) + dot(high, right_parts[1]))


def lane_of(rows):
    return lax.broadcasted_iota(jnp.int32, (rows, LANES), 1)


def swap_blocks(arrays):
    lane = lane_of(arrays[0].shape[0])
    low = lane < 64
    even = (lane // 32) % 2 == 0
    a, b, c, d = arrays
    a, c = (
        jnp.where(low, a, pltpu.roll(c, 64, 1)),
        jnp.where(low, pltpu.roll(a, 64, 1), c),
    )
    b, d = (
        jnp.where(low, b, pltpu.roll(d, 64, 1)),
        jnp.where(low, pltpu.roll(b, 64, 1), d),
    )
    a, b = (
        jnp.where(even, a, pltpu.roll(b, 32, 1)),
        jnp.where(even, pltpu.roll(a, 96, 1), b),
    )
    c, d = (
        jnp.where(even, c, pltpu.roll(d, 32, 1)),
        jnp.where(even, pltpu.roll(c, 96, 1), d),
    )
    return [a, b, c, d]


def tangent_copies(source, target, sems):
    return [
        pltpu.make_async_copy(source.at[p], target.at[:, p // 8, :, p % 8, :], sems.at[p // 8])
        for p in range(source.shape[0])
    ]


def up_to(value, step):
    return -(-value // step) * step


def rows_of(reactions, species):
    padded = up_to(species, 8)
    starts = [0, reactions, 2 * reactions]
    starts += [3 * reactions + k * padded for k in range(3)]
    return starts, 3 * reactions + 3 * padded


def tangent_chemistry(ilist, ylist, chosen, held, reactions, group, t, x, used, made, start, stop):
    species = t.shape[0] // group - 1
    listed = ilist.shape[0] // 4
    at_a, at_b, at_flux, at_fd, at_fda, at_again = [at // 8 for at in rows_of(reactions, species)[0]]
    sublane = lax.broadcasted_iota(jnp.int32, (8, LANES), 0)

    def rows(place):
        return pl.ds(pl.multiple_of(place, group), group)

    def apply(source, n):
        def body(step, carry):
            mixes, places = [], []
            for k in range(UNROLL):
                r = step * UNROLL + k
                tile, k8 = step * (UNROLL // 8) + k // 8, k % 8
                place = [rows(ilist[row * listed + r]) for row in range(4)]
                mixes.append(
                    held[n, at_a + tile, k8 : k8 + 1, :] * source[place[0], :]
                    + held[n, at_b + tile, k8 : k8 + 1, :] * source[place[1], :]
                )
                places.append(place)
            for k0 in range(0, UNROLL, BUFFERS):
                olds = []
                for k in range(BUFFERS):
                    i1, i2, q1, q2 = places[k0 + k]
                    lost, gained = used[k], made[k]
                    olds.append((lost[i1, :], lost[i2, :], gained[q1, :], gained[q2, :]))
                for k in range(BUFFERS):
                    r = step * UNROLL + k0 + k
                    i1, i2, q1, q2 = places[k0 + k]
                    mix, old = mixes[k0 + k], olds[k]
                    used[k][i1, :] = old[0] - mix
                    used[k][i2, :] = old[1] - mix
                    made[k][q1, :] = old[2] + ylist[r] * mix
                    made[k][q2, :] = old[3] + ylist[listed + r] * mix
            return carry

        lax.fori_loop(0, reactions // UNROLL, body, 0)

    def force(n):
        def body(p8, carry):
            at = sublane == p8
            for q in range(group // 8):
                r = chosen[q * 8 + p8]
                flux = held[n, at_flux + r // 8, pl.ds(r % 8, 1), :]
                value = jnp.where(at, flux, 0.0)
                i1, i2, q1, q2 = [
                    pl.ds(pl.multiple_of(ilist[row * listed + r] + q * 8, 8), 8) for row in range(4)
                ]
                lost, gained = used[q % BUFFERS], made[q % BUFFERS]
                one, two = lost[i1, :], lost[i2, :]
                three, four = gained[q1, :], gained[q2, :]
                lost[i1, :] = one - value
                lost[i2, :] = two - value
                gained[q1, :] = three + ylist[r] * value
                gained[q2, :] = four + ylist[listed + r] * value
            return carry

        lax.fori_loop(0, 8, body, 0)

    def total(at):
        value = used[0][at, :] + made[0][at, :]
        for k in range(1, BUFFERS):
            value = value + (used[k][at, :] + made[k][at, :])
        return value

    def each(work, target):
        def batch(step, count):
            places = [rows((step * 8 + k) * group) for k in range(count)]
            news = [work(place, step, k) for k, place in enumerate(places)]
            for place, (value, kept) in zip(places, news, strict=True):
                target[place, :] = value
                used[0][place, :] = kept

        def body(step, carry):
            batch(step, 8)
            return carry

        lax.fori_loop(0, species // 8, body, 0)
        if species % 8:
            batch(species // 8, species % 8)

    def substep(n, carry):
        force(n)
        apply(t, n)

        def first(at, tile, k):
            right = total(at)
            value = right * held[n, at_fd + tile, k : k + 1, :]
            return value, used[0][at, :] + right * held[n, at_again + tile, k : k + 1, :]

        each(first, x)
        apply(x, n)

        def second(at, tile, k):
            right = total(at)
            value = t[at, :] + right * held[n, at_fda + tile, k : k + 1, :]
            return value, used[0][at, :] - right

        each(second, t)
        return carry

    lax.fori_loop(start, stop, substep, 0)


def clear(refs):
    zero = jnp.zeros((LANES, LANES), F32)
    length = refs[0].shape[0]
    for at in range(0, length, LANES):
        for ref in refs:
            ref[at : min(at + LANES, length), :] = zero[0 : min(LANES, length - at)]


def weights(c):
    g = c * (1.0 - c * c) / 6.0
    up = c > 0
    half, square = 0.5 * c, 0.5 * c * c
    return (
        jnp.where(up, -g, 0.0),
        half + square + jnp.where(up, 3.0 * g, -g),
        1.0 - c * c + jnp.where(up, -3.0 * g, 3.0 * g),
        square - half + jnp.where(up, g, -3.0 * g),
        jnp.where(up, 0.0, g),
    )


def edge_kernel(
    chosen_in, reactants_in, products_in, yields_in, counts_in, permute_in, conc, rates, tangents,
    ilist_out, ylist_out, counts_out, conc_out, t, inner, other, s0, s1, s2, s3,
    raw, x, held, conc_in, rates_in, reactants, products, yields, counts, permute,
    pairs, columns, net_parts, hot, uses, base, chosen, ilist, ylist, *rest,
):
    sems = rest[-1]
    used, made = list(rest[:BUFFERS]), list(rest[BUFFERS : 2 * BUFFERS])
    species, real = conc.shape[0], rates.shape[0]
    group = tangents.shape[0]
    reactions = rates_in.shape[1]
    halves = conc_in.shape[0]
    starts, _ = rows_of(reactions, species)
    aligned = real // 8 * 8
    for half in range(halves):
        rates_in[half, aligned:] = jnp.zeros((reactions - aligned, LANES), F32)
    small = [
        pltpu.make_async_copy(conc.at[:, half, :], conc_in.at[half], sems.at[4])
        for half in range(halves)
    ] + [
        pltpu.make_async_copy(rates.at[:, half, :], rates_in.at[half, 0:real, :], sems.at[5])
        for half in range(halves)
    ]
    copies = tangent_copies(tangents, raw, sems)
    tiny = [
        pltpu.make_async_copy(source, target, sems.at[8])
        for source, target in (
            (chosen_in, chosen),
            (reactants_in, reactants),
            (products_in, products),
            (yields_in, yields),
            (counts_in, counts),
            (permute_in, permute),
        )
    ]
    for copy in tiny + small + copies:
        copy.start()
    for copy in tiny:
        copy.wait()

    pairs[...] = jnp.full(pairs.shape, -1, jnp.int32)
    pairs[0:2, 0:real] = reactants[...]
    pairs[2:4, 0:real] = products[...]
    columns[...] = jnp.zeros(columns.shape, F32)
    columns[0:2, 0:real] = yields[...]
    r0, r1, p0, p1 = [pairs[k : k + 1, :] for k in range(4)]
    y0, y1 = columns[0:1, :], columns[1:2, :]
    same, equal = r0 == r1, p0 == p1
    scale = jnp.where(same, 0.5, 1.0)
    parts = pairs.shape[1] // LANES
    ilist_out[...] = jnp.zeros(ilist_out.shape, jnp.int32)
    ylist_out[...] = jnp.zeros(ylist_out.shape, F32)
    for k, value in enumerate(
        (r0, jnp.where(same, species, r1), p0, jnp.where(equal, species, p1))
    ):
        value = jnp.where(r0 < 0, species, value) * group
        for part in range(parts):
            row = k * parts + part
            ilist_out[row : row + 1, :] = value[:, part * LANES : (part + 1) * LANES]
    for k, value in enumerate(
        (scale * (y0 + jnp.where(equal, y1, 0.0)), scale * jnp.where(equal, 0.0, y1))
    ):
        for part in range(parts):
            row = k * parts + part
            ylist_out[row : row + 1, :] = value[:, part * LANES : (part + 1) * LANES]
    lists = [
        pltpu.make_async_copy(source.at[row], target.at[pl.ds(row * LANES, LANES)], sems.at[6])
        for source, target, count in ((ilist_out, ilist, 4), (ylist_out, ylist, 2))
        for row in range(count * parts)
    ]
    for copy in lists:
        copy.start()

    row = lax.broadcasted_iota(jnp.int32, (species, reactions), 0)
    r0, r1, p0, p1 = [value[:, 0:reactions] for value in (r0, r1, p0, p1)]
    y0, y1 = y0[:, 0:reactions], y1[:, 0:reactions]
    uses_one = row == r0
    uses_two = row == r1
    net = (
        jnp.where(row == p0, y0, 0.0)
        + jnp.where(row == p1, y1, 0.0)
        - jnp.where(uses_one, 1.0, 0.0)
        - jnp.where(uses_two, 1.0, 0.0)
    )
    high, low = parts_of(net, 2)
    net_parts[0] = high
    net_parts[1] = low
    uses[0] = jnp.where(uses_one, 1.0, 0.0).astype(BF16)
    uses[1] = jnp.where(uses_two, 1.0, 0.0).astype(BF16)
    for k, value in enumerate((r0, r1)):
        change = (
            jnp.where(value == p0, y0, 0.0)
            + jnp.where(value == p1, y1, 0.0)
            - jnp.where(value == r0, 1.0, 0.0)
            - jnp.where(value == r1, 1.0, 0.0)
        )
        columns[k : k + 1, 0:reactions] = value.astype(F32)
        columns[2 + k : 3 + k, 0:reactions] = change
    turned = jnp.transpose(columns[...])[0:reactions]
    column = [turned[:, k : k + 1] for k in range(4)]
    lane = lane_of(reactions).astype(F32)
    for k in range(2):
        for at in range(0, species, LANES):
            width = min(LANES, species - at)
            value = jnp.where(column[k] == lane + float(at), 1.0, 0.0)[:, 0:width]
            hot[k * reactions : (k + 1) * reactions, at : at + width] = value.astype(BF16)
    same = column[0] == column[1]
    own_one, own_two = column[2], column[3]

    order = permute[...].astype(BF16)
    count = dot(jnp.broadcast_to(counts[...].astype(F32), (8, counts.shape[1])).astype(BF16), order)
    counts_out[...] = count
    count = count[0:1, :]
    factor = 1.0 / count
    highest = jnp.max(count).astype(jnp.int32)
    for copy in small:
        copy.wait()
    base[...] = select_right(jnp.concatenate([conc_in[0], conc_in[1]], axis=1), order, 3)
    rate = select_right(jnp.concatenate([rates_in[0], rates_in[1]], axis=1), order, 3)

    def keep(n, k, value):
        for ref, part in ((held, value[:, :LANES]), (other, value[:, LANES:])):
            full = value.shape[0] // 8 * 8
            first, tile = starts[k] // 8, (starts[k] + full) // 8
            ref[n, first:tile] = part[:full].reshape(full // 8, 8, LANES)
            if full < value.shape[0]:
                ref[n, tile, 0 : value.shape[0] - full, :] = part[full:]

    def substep(n, carry):
        c = base[...]
        picked = select_left(hot[...], c, 2)
        one, two = picked[:reactions], picked[reactions:]
        a = rate * two
        b = rate * one
        flux = a * one
        nets = (net_parts[0], net_parts[1])
        diagonal = select_left(uses[0], own_one * a, 2) + select_left(uses[1], own_two * b, 2)
        change = product(nets, flux)
        divisor = 1.0 - factor * diagonal
        fd = factor / divisor
        start = fd * change
        along = select_left(hot[...], start, 2)
        again = product(nets, a * along[:reactions] + b * along[reactions:])
        move = fd * (change + (again - diagonal * start))
        active = n.astype(F32) < count
        base[...] = c + jnp.where(active, move, 0.0)
        keep(n, 0, jnp.where(same, 2.0 * (a + b), a))
        keep(n, 1, jnp.where(same, 0.0, b))
        keep(n, 2, jnp.where(same, 2.0 * flux, flux))
        keep(n, 3, fd)
        keep(n, 4, jnp.where(active, fd, 0.0))
        keep(n, 5, fd * (count - 2.0 * diagonal) - 1.0)
        return carry

    lax.fori_loop(0, highest, substep, 0)
    conc_out[...] = base[...]

    for copy in copies:
        copy.wait()
    for q in range(raw.shape[1]):
        both = jnp.concatenate(
            [raw[:, q, half].reshape(species * 8, LANES) for half in range(halves)], axis=1
        )
        picked = select_right(both, order, 2)
        rows = slice(q * 8, (q + 1) * 8)
        for ref, part in ((t, picked[:, :LANES]), (inner, picked[:, LANES:])):
            by_species(ref, group)[0:species, rows, :] = part.reshape(species, 8, LANES)
    for ref in (t, inner):
        ref[species * group :, :] = jnp.zeros((group, LANES), F32)
    clear([*used, *made])
    x[species * group :, :] = jnp.zeros((group, LANES), F32)
    for copy in lists:
        copy.wait()
    own = jnp.max(count[:, :LANES]).astype(jnp.int32)
    tangent_chemistry(ilist, ylist, chosen, held, reactions, group, t, x, used, made, 0, own)

    rows = species * 8
    strips = swap_blocks(
        [
            by_species(t, group)[0:species, q * 8 : (q + 1) * 8, :].reshape(rows, LANES)
            for q in range(4)
        ]
    )
    quarter = up_to(-(-species // 4), 8)
    tails = []
    for q in range(4):
        part = base[q * quarter : min((q + 1) * quarter, species), 0:LANES]
        if part.shape[0] < quarter:
            empty = jnp.zeros((quarter - part.shape[0], LANES), F32)
            part = jnp.concatenate([part, empty], axis=0)
        tails.append(part)
    tails = swap_blocks(tails)
    even = even_row()
    strips[0:2] = ordered(even, strips[1], strips[0])
    tails[0:2] = ordered(even, tails[1], tails[0])
    for ref, value, last in zip((s0, s1, s2, s3), strips, tails, strict=True):
        ref[0:rows] = value
        ref[rows:] = last


def even_row():
    return (lax.axis_index("tile") // math.isqrt(lax.axis_size("tile"))) % 2 == 0


def even_tile():
    return lax.axis_index("tile") % 2 == 0


def ordered(even, one, two):
    return jnp.where(even, one, two), jnp.where(even, two, one)


def by_species(ref, group):
    return ref.reshape(ref.shape[0] // group, group, LANES)


def section(di, dj, c):
    value = jnp.zeros(di.shape, F32)
    for k, weight in enumerate(weights(c)):
        value = jnp.where((di == k - 2) & (dj == 0), weight, value)
    return value


def inner_kernel(
    ilist, ylist, chosen, counts, courant, side_pick, side_in, side_out, s0, s1, s2, s3,
    held, t_b,
    t, part, side_high, side_low,
    x, *rest,
):
    used, made = list(rest[:BUFFERS]), list(rest[BUFFERS : 2 * BUFFERS])
    group = chosen.shape[0]
    species = t_b.shape[0] // group - 1
    cx = jnp.concatenate([courant[0:1, :], courant[1:2, :]], axis=1)
    c = select_right(jnp.broadcast_to(cx, (8, cx.shape[1])), side_pick[...].astype(BF16), 3)[0:1, :]
    di = side_in[:, 0:1] - side_out[0:1, :]
    dj = side_in[:, 1:2] - side_out[1:2, :]
    map_ = jnp.where(side_in[:, 2:3] == side_out[2:3, :], section(di, dj, c), 0.0)
    high, low = parts_of(map_, 2)
    near = 4 * LANES
    side_high[...] = high[near:]
    side_low[...] = low[near:]
    last, first = ordered(even_row(), s0[...], s1[...])
    strips = jnp.concatenate([first, last, s2[...], s3[...]], axis=1)
    part[...] = product_right(strips, (high[:near], low[:near]))

    t[...] = t_b[...]
    clear([*used, *made])
    x[species * group :, :] = jnp.zeros((group, LANES), F32)
    own = jnp.max(counts[0:1, LANES:]).astype(jnp.int32)
    tangent_chemistry(
        ilist, ylist, chosen, held, reactions_of(held, species), group, t, x, used, made,
        0, jnp.minimum(own, SPLIT),
    )


def reactions_of(held, species):
    return (held.shape[1] * 8 - 3 * up_to(species, 8)) // 3


def side_kernel(part, one, two, side_high, side_low, to_one, to_two):
    east, west = ordered(even_row(), one[...], two[...])
    both = jnp.concatenate([west, east], axis=1)
    value = part[...] + product_right(both, (side_high[...], side_low[...]))
    to_one[...], to_two[...] = ordered(even_tile(), value[:, LANES:], value[:, :LANES])


def later_kernel(ilist, ylist, chosen, counts, held, t_b, t, x, *rest):
    used, made = list(rest[:BUFFERS]), list(rest[BUFFERS : 2 * BUFFERS])
    group = chosen.shape[0]
    species = t_b.shape[0] // group - 1
    t[...] = t_b[...]
    clear([*used, *made])
    x[species * group :, :] = jnp.zeros((group, LANES), F32)
    own = jnp.max(counts[0:1, LANES:]).astype(jnp.int32)
    tangent_chemistry(
        ilist, ylist, chosen, held, reactions_of(held, species), group, t, x, used, made,
        SPLIT, own,
    )


def advect_kernel(
    conc, h0, h1, h2, h3, courant, entries, cells, cells_rows, t_a, t_b,
    t_out, conc_out,
    done, conc_done, sems,
):
    species = conc.shape[0]
    rows = species * 8
    cx = jnp.concatenate([courant[0:1, :], courant[1:2, :]], axis=1)
    cy = jnp.concatenate([courant[2:3, :], courant[3:4, :]], axis=1)
    di = entries[:, 0:1] - cells_rows[0:1, :]
    dj = entries[:, 1:2] - cells_rows[1:2, :]
    along_x = section(di, dj, cx)
    late = lax.broadcasted_iota(jnp.int32, di.shape, 0) >= di.shape[0] - 64
    along_y = jnp.where(late, section(dj, di, cy), 0.0)
    both = section(cells[:, 1:2] - cells_rows[1:2, :], cells[:, 0:1] - cells_rows[0:1, :], cy)
    whole = along_y + jnp.dot(
        along_x, both, precision=lax.Precision.HIGHEST, preferred_element_type=F32
    )
    high, low = parts_of(whole, 2)
    own = 2 * LANES
    local, outer = (high[:own], low[:own]), (high[own:], low[own:])

    east, west = ordered(even_row(), h0[...], h1[...])
    north, south = ordered(even_tile(), h2[...], h3[...])
    halo = swap_blocks([west, east, south, north])
    twice = jnp.concatenate([outer[0], outer[0]], axis=0)

    def from_halo(value):
        high, low = parts_of(value, 2)
        return dot(jnp.concatenate([high, low], axis=1), twice) + dot(high, outer[1])

    outside = jnp.concatenate([value[rows:] for value in halo], axis=0)
    base = product_right(conc[...], local) + from_halo(outside[0:species])
    copies = []
    for half in range(2):
        conc_done[half] = base[:, half * LANES : (half + 1) * LANES]
        copies.append(
            pltpu.make_async_copy(conc_done.at[half], conc_out.at[:, half, :], sems.at[1])
        )
        copies[-1].start()
    for q in range(4):
        part = slice(q * 8, (q + 1) * 8)
        inside = jnp.concatenate(
            [by_species(ref, t_out.shape[0])[0:species, part, :].reshape(rows, LANES) for ref in (t_a, t_b)],
            axis=1,
        )
        value = product_right(inside, local) + from_halo(halo[q][0:rows])
        for half in range(2):
            done[:, q, half] = value[:, half * LANES : (half + 1) * LANES].reshape(
                species, 8, LANES
            )
        for p8 in range(8):
            copies.append(
                pltpu.make_async_copy(done.at[:, q, :, p8, :], t_out.at[q * 8 + p8], sems.at[0])
            )
            copies[-1].start()
    for copy in copies:
        copy.wait()


def exchanged(value, by, odd):
    size = lax.axis_size("tile")
    pairs = [(i, i + by) for i in range(size - by) if (i // by) % 2 == odd]
    return lax.ppermute(value, "tile", pairs + [(j, i) for i, j in pairs])


def per_device(
    concentrations, tangents, rates, substeps, courant, reactants, products, yields, reaction_index
):
    species = concentrations.shape[0]
    cells = CX * CY
    halves = cells // LANES
    group = tangents.shape[0]
    real = rates.shape[0]
    reactions = up_to(real, UNROLL)
    listed = up_to(reactions, LANES)
    lists = up_to(4 * listed // LANES, 8)
    across = math.isqrt(lax.axis_size("tile"))
    table = static_tables()
    vmem = pl.BlockSpec(memory_space=pltpu.VMEM)
    smem = pl.BlockSpec(memory_space=pltpu.SMEM)
    hbm = pl.BlockSpec(memory_space=pltpu.HBM)
    limit = pltpu.CompilerParams(vmem_limit_bytes=VMEM_LIMIT)
    _, held_rows = rows_of(reactions, species)

    def shape(*sizes, dtype=F32):
        return jax.ShapeDtypeStruct(sizes, dtype)

    conc = concentrations.reshape(species, halves, LANES)
    sens = tangents.reshape(group, species, halves, LANES)
    rate_rows = rates.reshape(real, halves, LANES)
    numbers = courant.reshape(2 * halves, LANES)

    state = shape((species + 1) * group, LANES)
    strip = shape(species * 8 + up_to(-(-species // 4), 8), LANES)
    wide = shape(strip.shape[0], 2 * LANES)
    held = shape(NMAX, held_rows // 8, 8, LANES)
    work = [pltpu.VMEM(state.shape, F32)] * (1 + 2 * BUFFERS)
    raw = pltpu.VMEM((species, group // 8, halves, 8, LANES), F32)

    ilist, ylist, counts, conc_end, t_a, t_b, held_b, s0, s1, s2, s3 = pl.pallas_call(
        edge_kernel,
        out_shape=[
            shape(lists, LANES, dtype=jnp.int32),
            shape(lists, LANES),
            shape(8, cells),
            shape(species, cells),
            state,
            state,
            held,
            *([strip] * 4),
        ],
        in_specs=[hbm] * 9,
        out_specs=[vmem] * 11,
        scratch_shapes=[
            raw,
            work[0],
            pltpu.VMEM(held.shape, F32),
            pltpu.VMEM((halves, species, LANES), F32),
            pltpu.VMEM((halves, reactions, LANES), F32),
            pltpu.VMEM((2, real), jnp.int32),
            pltpu.VMEM((2, real), jnp.int32),
            pltpu.VMEM((2, real), F32),
            pltpu.VMEM((1, cells), jnp.int32),
            pltpu.VMEM((cells, cells), F32),
            pltpu.VMEM((8, listed), jnp.int32),
            pltpu.VMEM((LANES, listed), F32),
            pltpu.VMEM((2, species, reactions), BF16),
            pltpu.VMEM((2 * reactions, species), BF16),
            pltpu.VMEM((2, species, reactions), BF16),
            pltpu.VMEM((species, cells), F32),
            pltpu.SMEM((group,), jnp.int32),
            pltpu.SMEM((4 * listed,), jnp.int32),
            pltpu.SMEM((2 * listed,), F32),
            *work[1:],
            pltpu.SemaphoreType.DMA((9,)),
        ],
        compiler_params=limit,
        name="edge_columns",
    )(
        *[
            pltpu.with_memory_space_constraint(value, pltpu.HBM)
            for value in (
                reaction_index, reactants.T, products.T, yields.T, substeps,
                jnp.asarray(table["permute"]), conc, rate_rows, sens,
            )
        ]
    )

    ilist, ylist = ilist.reshape(-1)[: 4 * listed], ylist.reshape(-1)
    x_one = exchanged(s0, across, 0)
    x_two = exchanged(s1, across, 1)

    t_b, part, side_high, side_low = pl.pallas_call(
        inner_kernel,
        out_shape=[state, wide] + [shape(2 * LANES, 2 * LANES, dtype=BF16)] * 2,
        in_specs=[smem] * 3 + [vmem] * 11,
        out_specs=[vmem] * 4,
        scratch_shapes=work,
        compiler_params=limit,
        name="inner_columns",
    )(
        ilist, ylist, reaction_index, counts, numbers, jnp.asarray(table["side_pick"]),
        jnp.asarray(table["side_in"]), jnp.asarray(table["side_out"]), s0, s1, s2, s3,
        held_b, t_b,
    )

    to_one, to_two = pl.pallas_call(
        side_kernel,
        out_shape=[strip, strip],
        in_specs=[vmem] * 5,
        out_specs=[vmem] * 2,
        compiler_params=limit,
        name="y_edges",
    )(part, x_one, x_two, side_high, side_low)
    y_one = exchanged(to_one, 1, 0)
    y_two = exchanged(to_two, 1, 1)

    t_b = pl.pallas_call(
        later_kernel,
        out_shape=state,
        in_specs=[smem] * 3 + [vmem] * 3,
        out_specs=vmem,
        scratch_shapes=work,
        compiler_params=limit,
        name="inner_later",
    )(ilist, ylist, reaction_index, counts, held_b, t_b)

    result, conc_out = pl.pallas_call(
        advect_kernel,
        out_shape=[shape(group, species, halves, LANES), shape(species, halves, LANES)],
        in_specs=[vmem] * 11,
        out_specs=[hbm, hbm],
        scratch_shapes=[
            raw,
            pltpu.VMEM((halves, species, LANES), F32),
            pltpu.SemaphoreType.DMA((2,)),
        ],
        compiler_params=limit,
        name="advection",
    )(
        conc_end, x_one, x_two, y_one, y_two, numbers,
        jnp.asarray(table["entries"]), jnp.asarray(table["cells"]),
        jnp.asarray(table["cells_rows"]), t_a, t_b,
    )
    return (
        conc_out.reshape(species, 1, cells),
        result.reshape(group, species, 1, cells),
    )


def solution(mesh):
    in_specs = (
        P(None, "tile", None),
        P("pgrp", None, "tile", None),
        P(None, "tile", None),
        P("tile", None),
        P(None, "tile", None),
        P(),
        P(),
        P(),
        P("pgrp"),
    )
    out_specs = (P(None, "tile", None), P("pgrp", None, "tile", None))
    return jax.shard_map(
        per_device, mesh=mesh, in_specs=in_specs, out_specs=out_specs, check_vma=False
    )
```

```python
import functools
import math

import jax
import jax.numpy as jnp
import numpy as np
from jax import lax
from jax.experimental import pallas as pl
from jax.experimental.pallas import tpu as pltpu
from jax.sharding import PartitionSpec as P

CX = 16
CY = 16
NMAX = 4
LANES = 128
UNROLL = 32
BUFFERS = 2
SPLIT = 2
VMEM_LIMIT = 36 * 2**20
F32 = jnp.float32
BF16 = jnp.bfloat16


def orders():
    last, end = CX - 2, CY - 2
    west = [(i, j) for i in range(2) for j in range(CY)]
    east = [(i, j) for i in range(last, CX) for j in range(CY)]
    south = [(i, j) for j in range(2) for i in range(CX)]
    north = [(i, j) for j in range(end, CY) for i in range(CX)]
    strips = west + east + south + north
    edge = list(dict.fromkeys(strips))
    inner = [(i, j) for i in range(CX) for j in range(CY) if (i, j) not in set(edge)]
    return edge + inner, strips


def one_hot(source, wanted):
    place = {cell: k for k, cell in enumerate(source)}
    table = np.zeros((len(source), len(wanted)), np.float32)
    for lane, cell in enumerate(wanted):
        if cell is not None:
            table[place[cell], lane] = 1.0
    return table


def static_tables():
    order, strips = orders()
    cells = [(i, j) for i in range(CX) for j in range(CY)]
    west = [(i - CX, j) for i, j in strips[32:64]]
    east = [(i + CX, j) for i, j in strips[0:32]]
    south = [(i, j - CY) for i, j in strips[96:128]]
    north = [(i, j + CY) for i, j in strips[64:96]]
    blocks = [order[32 * k : 32 * k + 32] for k in range(4)] + [west, east]
    side_in = [(i, j, q) for block in blocks for q in range(4) for i, j in block]
    own_sides = (strips[64:96], strips[96:128])
    side_out = [(i, j, q) for block in own_sides for q in range(4) for i, j in block]
    entries = order + west + east + south + north
    return {
        "permute": one_hot(cells, order),
        "side_pick": one_hot(cells, [(i, j) for i, j, _ in side_out]),
        "side_in": np.array(side_in, np.int32),
        "side_out": np.array(side_out, np.int32).T,
        "entries": np.array(entries, np.int32),
        "cells": np.array(cells, np.int32),
        "cells_rows": np.array(cells, np.int32).T,
    }


def dot(left, right):
    return jnp.dot(left, right, preferred_element_type=F32)


def parts_of(value, count):
    parts = []
    for k in range(count):
        part = value.astype(BF16)
        parts.append(part)
        if k + 1 < count:
            value = value - part.astype(F32)
    return parts


def select_left(exact, value, count):
    return sum(dot(exact, part) for part in parts_of(value, count))


def select_right(value, exact, count):
    return sum(dot(part, exact) for part in parts_of(value, count))


def product(left_parts, value):
    high, low = parts_of(value, 2)
    return dot(left_parts[0], high) + (dot(left_parts[0], low) + dot(left_parts[1], high))


def product_right(value, right_parts):
    high, low = parts_of(value, 2)
    return dot(high, right_parts[0]) + (dot(low, right_parts[0]) + dot(high, right_parts[1]))


def lane_of(rows):
    return lax.broadcasted_iota(jnp.int32, (rows, LANES), 1)


def swap_blocks(arrays):
    lane = lane_of(arrays[0].shape[0])
    low = lane < 64
    even = (lane // 32) % 2 == 0
    a, b, c, d = arrays
    a, c = (
        jnp.where(low, a, pltpu.roll(c, 64, 1)),
        jnp.where(low, pltpu.roll(a, 64, 1), c),
    )
    b, d = (
        jnp.where(low, b, pltpu.roll(d, 64, 1)),
        jnp.where(low, pltpu.roll(b, 64, 1), d),
    )
    a, b = (
        jnp.where(even, a, pltpu.roll(b, 32, 1)),
        jnp.where(even, pltpu.roll(a, 96, 1), b),
    )
    c, d = (
        jnp.where(even, c, pltpu.roll(d, 32, 1)),
        jnp.where(even, pltpu.roll(c, 96, 1), d),
    )
    return [a, b, c, d]


def tangent_copies(source, target, sems):
    return [
        pltpu.make_async_copy(source.at[p], target.at[:, p // 8, :, p % 8, :], sems.at[p // 8])
        for p in range(source.shape[0])
    ]


def up_to(value, step):
    return -(-value // step) * step


def rows_of(reactions, species):
    padded = up_to(species, 8)
    starts = [0, reactions, 2 * reactions]
    starts += [3 * reactions + k * padded for k in range(3)]
    return starts, 3 * reactions + 3 * padded


def tangent_chemistry(
    ilist, ylist, chosen, held, real, group, origin, t, x, used, made, start, stop
):
    species = t.shape[0] // group - 1
    reactions = up_to(real, 8)
    listed = ilist.shape[0] // 4
    at_a, at_b, at_flux, at_fd, at_fda, at_again = [at // 8 for at in rows_of(reactions, species)[0]]
    sublane = lax.broadcasted_iota(jnp.int32, (8, LANES), 0)

    def rows(place):
        return pl.ds(pl.multiple_of(place, group), group)

    def apply(source, n):
        def some(step, count):
            for k0 in range(0, count, BUFFERS):
                batch = range(k0, min(k0 + BUFFERS, count))
                mixes, places, olds = [], [], []
                for k in batch:
                    r = step * UNROLL + k
                    tile, k8 = step * (UNROLL // 8) + k // 8, k % 8
                    place = [rows(ilist[row * listed + r]) for row in range(4)]
                    mixes.append(
                        held[n, at_a + tile, k8 : k8 + 1, :] * source[place[0], :]
                        + held[n, at_b + tile, k8 : k8 + 1, :] * source[place[1], :]
                    )
                    places.append(place)
                for k, (i1, i2, q1, q2) in enumerate(places):
                    lost, gained = used[k], made[k]
                    olds.append((lost[i1, :], lost[i2, :], gained[q1, :], gained[q2, :]))
                for k, (i1, i2, q1, q2) in enumerate(places):
                    r = step * UNROLL + k0 + k
                    mix, old = mixes[k], olds[k]
                    used[k][i1, :] = old[0] - mix
                    used[k][i2, :] = old[1] - mix
                    made[k][q1, :] = old[2] + ylist[r] * mix
                    made[k][q2, :] = old[3] + ylist[listed + r] * mix

        def body(step, carry):
            some(step, UNROLL)
            return carry

        lax.fori_loop(0, real // UNROLL, body, 0)
        if real % UNROLL:
            some(real // UNROLL, real % UNROLL)

    def force(n):
        def body(p8, carry):
            at = sublane == p8
            for q in range(group // 8):
                r = chosen[q * 8 + p8]
                flux = held[n, at_flux + r // 8, pl.ds(r % 8, 1), :]
                value = jnp.where(at, flux, 0.0)
                i1, i2, q1, q2 = [
                    pl.ds(pl.multiple_of(ilist[row * listed + r] + q * 8, 8), 8) for row in range(4)
                ]
                lost, gained = used[q % BUFFERS], made[q % BUFFERS]
                one, two = lost[i1, :], lost[i2, :]
                three, four = gained[q1, :], gained[q2, :]
                lost[i1, :] = one - value
                lost[i2, :] = two - value
                gained[q1, :] = three + ylist[r] * value
                gained[q2, :] = four + ylist[listed + r] * value
            return carry

        lax.fori_loop(0, 8, body, 0)

    def total(at):
        value = used[0][at, :] + made[0][at, :]
        for k in range(1, BUFFERS):
            value = value + (used[k][at, :] + made[k][at, :])
        return value

    def each(work, target):
        def batch(step, count):
            places = [rows((step * 8 + k) * group) for k in range(count)]
            news = [work(place, step, k) for k, place in enumerate(places)]
            for place, (value, kept) in zip(places, news, strict=True):
                target[place, :] = value
                used[0][place, :] = kept

        def body(step, carry):
            batch(step, 8)
            return carry

        lax.fori_loop(0, species // 8, body, 0)
        if species % 8:
            batch(species // 8, species % 8)

    def substep(n, before):
        force(n)
        apply(before, n)

        def first(at, tile, k):
            right = total(at)
            value = right * held[n, at_fd + tile, k : k + 1, :]
            return value, used[0][at, :] + right * held[n, at_again + tile, k : k + 1, :]

        each(first, x)
        apply(x, n)

        def second(at, tile, k):
            right = total(at)
            value = before[at, :] + right * held[n, at_fda + tile, k : k + 1, :]
            return value, used[0][at, :] - right

        each(second, t)

    def more(n, carry):
        substep(n, t)
        return carry

    if origin is t:
        lax.fori_loop(start, stop, more, 0)
        return

    t[species * group :, :] = jnp.zeros((group, LANES), F32)

    @pl.when(start < stop)
    def _():
        substep(start, origin)
        lax.fori_loop(start + 1, stop, more, 0)

    @pl.when(start >= stop)
    def _():
        t[...] = origin[...]


def clear(refs):
    zero = jnp.zeros((LANES, LANES), F32)
    length = refs[0].shape[0]
    for at in range(0, length, LANES):
        for ref in refs:
            ref[at : min(at + LANES, length), :] = zero[0 : min(LANES, length - at)]


def weights(c):
    g = c * (1.0 - c * c) / 6.0
    up = c > 0
    half, square = 0.5 * c, 0.5 * c * c
    return (
        jnp.where(up, -g, 0.0),
        half + square + jnp.where(up, 3.0 * g, -g),
        1.0 - c * c + jnp.where(up, -3.0 * g, 3.0 * g),
        square - half + jnp.where(up, g, -3.0 * g),
        jnp.where(up, 0.0, g),
    )


def edge_kernel(
    chosen_in, reactants_in, products_in, yields_in, counts_in, permute_in, conc, rates, tangents,
    ilist_out, ylist_out, counts_out, conc_out, t, inner, other, s0, s1, s2, s3,
    raw, x, held, conc_in, rates_in, reactants, products, yields, counts, permute,
    pairs, columns, net_parts, hot, uses, base, chosen, ilist, ylist, *rest,
):
    sems = rest[-1]
    used, made = list(rest[:BUFFERS]), list(rest[BUFFERS : 2 * BUFFERS])
    species, real = conc.shape[0], rates.shape[0]
    group = tangents.shape[0]
    reactions = rates_in.shape[1]
    halves = conc_in.shape[0]
    starts, _ = rows_of(reactions, species)
    aligned = real // 8 * 8
    for half in range(halves):
        rates_in[half, aligned:] = jnp.zeros((reactions - aligned, LANES), F32)
    small = [
        pltpu.make_async_copy(conc.at[:, half, :], conc_in.at[half], sems.at[4])
        for half in range(halves)
    ] + [
        pltpu.make_async_copy(rates.at[:, half, :], rates_in.at[half, 0:real, :], sems.at[5])
        for half in range(halves)
    ]
    copies = tangent_copies(tangents, raw, sems)
    tiny = [
        pltpu.make_async_copy(source, target, sems.at[8])
        for source, target in (
            (chosen_in, chosen),
            (reactants_in, reactants),
            (products_in, products),
            (yields_in, yields),
            (counts_in, counts),
            (permute_in, permute),
        )
    ]
    for copy in tiny + small + copies:
        copy.start()
    clear([*used, *made])
    x[species * group :, :] = jnp.zeros((group, LANES), F32)
    for copy in tiny:
        copy.wait()

    pairs[...] = jnp.full(pairs.shape, -1, jnp.int32)
    pairs[0:2, 0:real] = reactants[...]
    pairs[2:4, 0:real] = products[...]
    columns[...] = jnp.zeros(columns.shape, F32)
    columns[0:2, 0:real] = yields[...]
    r0, r1, p0, p1 = [pairs[k : k + 1, :] for k in range(4)]
    y0, y1 = columns[0:1, :], columns[1:2, :]
    same, equal = r0 == r1, p0 == p1
    scale = jnp.where(same, 0.5, 1.0)
    parts = pairs.shape[1] // LANES
    ilist_out[...] = jnp.zeros(ilist_out.shape, jnp.int32)
    ylist_out[...] = jnp.zeros(ylist_out.shape, F32)
    for k, value in enumerate(
        (r0, jnp.where(same, species, r1), p0, jnp.where(equal, species, p1))
    ):
        value = jnp.where(r0 < 0, species, value) * group
        for part in range(parts):
            row = k * parts + part
            ilist_out[row : row + 1, :] = value[:, part * LANES : (part + 1) * LANES]
    for k, value in enumerate(
        (scale * (y0 + jnp.where(equal, y1, 0.0)), scale * jnp.where(equal, 0.0, y1))
    ):
        for part in range(parts):
            row = k * parts + part
            ylist_out[row : row + 1, :] = value[:, part * LANES : (part + 1) * LANES]
    lists = [
        pltpu.make_async_copy(source.at[row], target.at[pl.ds(row * LANES, LANES)], sems.at[6])
        for source, target, count in ((ilist_out, ilist, 4), (ylist_out, ylist, 2))
        for row in range(count * parts)
    ]
    for copy in lists:
        copy.start()

    row = lax.broadcasted_iota(jnp.int32, (species, reactions), 0)
    r0, r1, p0, p1 = [value[:, 0:reactions] for value in (r0, r1, p0, p1)]
    y0, y1 = y0[:, 0:reactions], y1[:, 0:reactions]
    uses_one = row == r0
    uses_two = row == r1
    net = (
        jnp.where(row == p0, y0, 0.0)
        + jnp.where(row == p1, y1, 0.0)
        - jnp.where(uses_one, 1.0, 0.0)
        - jnp.where(uses_two, 1.0, 0.0)
    )
    high, low = parts_of(net, 2)
    net_parts[0] = high
    net_parts[1] = low
    uses[0] = jnp.where(uses_one, 1.0, 0.0).astype(BF16)
    uses[1] = jnp.where(uses_two, 1.0, 0.0).astype(BF16)
    for k, value in enumerate((r0, r1)):
        change = (
            jnp.where(value == p0, y0, 0.0)
            + jnp.where(value == p1, y1, 0.0)
            - jnp.where(value == r0, 1.0, 0.0)
            - jnp.where(value == r1, 1.0, 0.0)
        )
        columns[k : k + 1, 0:reactions] = value.astype(F32)
        columns[2 + k : 3 + k, 0:reactions] = change
    turned = jnp.transpose(columns[...])[0:reactions]
    column = [turned[:, k : k + 1] for k in range(4)]
    lane = lane_of(reactions).astype(F32)
    for k in range(2):
        for at in range(0, species, LANES):
            width = min(LANES, species - at)
            value = jnp.where(column[k] == lane + float(at), 1.0, 0.0)[:, 0:width]
            hot[k * reactions : (k + 1) * reactions, at : at + width] = value.astype(BF16)
    same = column[0] == column[1]
    own_one, own_two = column[2], column[3]

    order = permute[...].astype(BF16)
    count = dot(jnp.broadcast_to(counts[...].astype(F32), (8, counts.shape[1])).astype(BF16), order)
    counts_out[...] = count
    count = count[0:1, :]
    factor = 1.0 / count
    highest = jnp.max(count).astype(jnp.int32)
    for copy in small:
        copy.wait()
    base[...] = select_right(jnp.concatenate([conc_in[0], conc_in[1]], axis=1), order, 3)
    rate = select_right(jnp.concatenate([rates_in[0], rates_in[1]], axis=1), order, 3)

    def keep(n, k, value):
        for ref, part in ((held, value[:, :LANES]), (other, value[:, LANES:])):
            full = value.shape[0] // 8 * 8
            first, tile = starts[k] // 8, (starts[k] + full) // 8
            ref[n, first:tile] = part[:full].reshape(full // 8, 8, LANES)
            if full < value.shape[0]:
                ref[n, tile, 0 : value.shape[0] - full, :] = part[full:]

    def substep(n, carry):
        c = base[...]
        picked = select_left(hot[...], c, 2)
        one, two = picked[:reactions], picked[reactions:]
        a = rate * two
        b = rate * one
        flux = a * one
        nets = (net_parts[0], net_parts[1])
        diagonal = select_left(uses[0], own_one * a, 2) + select_left(uses[1], own_two * b, 2)
        change = product(nets, flux)
        divisor = 1.0 - factor * diagonal
        fd = factor / divisor
        start = fd * change
        along = select_left(hot[...], start, 2)
        again = product(nets, a * along[:reactions] + b * along[reactions:])
        move = fd * (change + (again - diagonal * start))
        active = n.astype(F32) < count
        base[...] = c + jnp.where(active, move, 0.0)
        keep(n, 0, jnp.where(same, 2.0 * (a + b), a))
        keep(n, 1, jnp.where(same, 0.0, b))
        keep(n, 2, jnp.where(same, 2.0 * flux, flux))
        keep(n, 3, fd)
        keep(n, 4, jnp.where(active, fd, 0.0))
        keep(n, 5, fd * (count - 2.0 * diagonal) - 1.0)
        return carry

    lax.fori_loop(0, highest, substep, 0)
    conc_out[...] = base[...]

    for copy in copies:
        copy.wait()
    for q in range(raw.shape[1]):
        both = jnp.concatenate(
            [raw[:, q, half].reshape(species * 8, LANES) for half in range(halves)], axis=1
        )
        picked = select_right(both, order, 2)
        rows = slice(q * 8, (q + 1) * 8)
        for ref, part in ((t, picked[:, :LANES]), (inner, picked[:, LANES:])):
            by_species(ref, group)[0:species, rows, :] = part.reshape(species, 8, LANES)
    for ref in (t, inner):
        ref[species * group :, :] = jnp.zeros((group, LANES), F32)
    for copy in lists:
        copy.wait()
    own = jnp.max(count[:, :LANES]).astype(jnp.int32)
    tangent_chemistry(ilist, ylist, chosen, held, real, group, t, t, x, used, made, 0, own)

    rows = species * 8
    strips = swap_blocks(
        [
            by_species(t, group)[0:species, q * 8 : (q + 1) * 8, :].reshape(rows, LANES)
            for q in range(4)
        ]
    )
    quarter = up_to(-(-species // 4), 8)
    tails = []
    for q in range(4):
        part = base[q * quarter : min((q + 1) * quarter, species), 0:LANES]
        if part.shape[0] < quarter:
            empty = jnp.zeros((quarter - part.shape[0], LANES), F32)
            part = jnp.concatenate([part, empty], axis=0)
        tails.append(part)
    tails = swap_blocks(tails)
    even = even_row()
    strips[0:2] = ordered(even, strips[1], strips[0])
    tails[0:2] = ordered(even, tails[1], tails[0])
    for ref, value, last in zip((s0, s1, s2, s3), strips, tails, strict=True):
        ref[0:rows] = value
        ref[rows:] = last


def even_row():
    return (lax.axis_index("tile") // math.isqrt(lax.axis_size("tile"))) % 2 == 0


def even_tile():
    return lax.axis_index("tile") % 2 == 0


def ordered(even, one, two):
    return jnp.where(even, one, two), jnp.where(even, two, one)


def by_species(ref, group):
    return ref.reshape(ref.shape[0] // group, group, LANES)


def section(di, dj, c):
    value = jnp.zeros(di.shape, F32)
    for k, weight in enumerate(weights(c)):
        value = jnp.where((di == k - 2) & (dj == 0), weight, value)
    return value


def inner_kernel(
    real, ilist, ylist, chosen, counts, courant, side_pick, side_in, side_out, s0, s1, s2, s3,
    held, t_b,
    t, part, side_high, side_low,
    x, *rest,
):
    used, made = list(rest[:BUFFERS]), list(rest[BUFFERS : 2 * BUFFERS])
    group = chosen.shape[0]
    species = t_b.shape[0] // group - 1
    cx = jnp.concatenate([courant[0:1, :], courant[1:2, :]], axis=1)
    c = select_right(jnp.broadcast_to(cx, (8, cx.shape[1])), side_pick[...].astype(BF16), 3)[0:1, :]
    di = side_in[:, 0:1] - side_out[0:1, :]
    dj = side_in[:, 1:2] - side_out[1:2, :]
    map_ = jnp.where(side_in[:, 2:3] == side_out[2:3, :], section(di, dj, c), 0.0)
    high, low = parts_of(map_, 2)
    near = 4 * LANES
    side_high[...] = high[near:]
    side_low[...] = low[near:]
    last, first = ordered(even_row(), s0[...], s1[...])
    strips = jnp.concatenate([first, last, s2[...], s3[...]], axis=1)
    part[...] = product_right(strips, (high[:near], low[:near]))

    clear([*used, *made])
    x[species * group :, :] = jnp.zeros((group, LANES), F32)
    own = jnp.max(counts[0:1, LANES:]).astype(jnp.int32)
    tangent_chemistry(
        ilist, ylist, chosen, held, real, group, t_b, t, x, used, made,
        0, jnp.minimum(own, SPLIT),
    )


def side_kernel(part, one, two, side_high, side_low, to_one, to_two):
    east, west = ordered(even_row(), one[...], two[...])
    both = jnp.concatenate([west, east], axis=1)
    value = part[...] + product_right(both, (side_high[...], side_low[...]))
    to_one[...], to_two[...] = ordered(even_tile(), value[:, LANES:], value[:, :LANES])


def later_kernel(
    real, ilist, ylist, chosen, counts, held, t_b, courant, entries, cells, cells_rows,
    t, map_high, map_low,
    x, *rest,
):
    cx = jnp.concatenate([courant[0:1, :], courant[1:2, :]], axis=1)
    cy = jnp.concatenate([courant[2:3, :], courant[3:4, :]], axis=1)
    di = entries[:, 0:1] - cells_rows[0:1, :]
    dj = entries[:, 1:2] - cells_rows[1:2, :]
    along_x = section(di, dj, cx)
    late = lax.broadcasted_iota(jnp.int32, di.shape, 0) >= di.shape[0] - 64
    along_y = jnp.where(late, section(dj, di, cy), 0.0)
    both = section(cells[:, 1:2] - cells_rows[1:2, :], cells[:, 0:1] - cells_rows[0:1, :], cy)
    whole = along_y + jnp.dot(
        along_x, both, precision=lax.Precision.HIGHEST, preferred_element_type=F32
    )
    map_high[...], map_low[...] = parts_of(whole, 2)
    used, made = list(rest[:BUFFERS]), list(rest[BUFFERS : 2 * BUFFERS])
    group = chosen.shape[0]
    species = t_b.shape[0] // group - 1
    clear([*used, *made])
    x[species * group :, :] = jnp.zeros((group, LANES), F32)
    own = jnp.max(counts[0:1, LANES:]).astype(jnp.int32)
    tangent_chemistry(
        ilist, ylist, chosen, held, real, group, t_b, t, x, used, made,
        SPLIT, own,
    )


def advect_kernel(
    conc, h0, h1, h2, h3, map_high, map_low, t_a, t_b,
    t_out, conc_out,
    done, conc_done, halo_ref, sems,
):
    species = conc.shape[0]
    group = t_out.shape[0]
    rows = species * 8
    high, low = map_high[...], map_low[...]
    own = 2 * LANES
    local, outer = (high[:own], low[:own]), (high[own:], low[own:])

    east, west = ordered(even_row(), h0[...], h1[...])
    north, south = ordered(even_tile(), h2[...], h3[...])
    halo = swap_blocks([west, east, south, north])
    twice = jnp.concatenate([outer[0], outer[0]], axis=0)

    def from_halo(value):
        high, low = parts_of(value, 2)
        return dot(jnp.concatenate([high, low], axis=1), twice) + dot(high, outer[1])

    outside = jnp.concatenate([value[rows:] for value in halo], axis=0)
    base = product_right(conc[...], local) + from_halo(outside[0:species])
    copies = []
    for half in range(2):
        conc_done[half] = base[:, half * LANES : (half + 1) * LANES]
        copies.append(
            pltpu.make_async_copy(conc_done.at[half], conc_out.at[:, half, :], sems.at[1])
        )
        copies[-1].start()
    for q in range(4):
        halo_ref[q] = halo[q][0:rows]

    def sent(q):
        return [
            pltpu.make_async_copy(done.at[:, q, :, p8, :], t_out.at[q * 8 + p8], sems.at[0])
            for p8 in range(8)
        ]

    def body(q, carry):
        part = pl.ds(pl.multiple_of(q * 8, 8), 8)
        inside = jnp.concatenate(
            [by_species(ref, group)[0:species, part, :].reshape(rows, LANES) for ref in (t_a, t_b)],
            axis=1,
        )
        value = product_right(inside, local) + from_halo(halo_ref[q])
        for half in range(2):
            done[:, q, half] = value[:, half * LANES : (half + 1) * LANES].reshape(
                species, 8, LANES
            )
        for copy in sent(q):
            copy.start()
        return carry

    lax.fori_loop(0, group // 8, body, 0)
    for q in range(group // 8):
        copies += sent(q)
    for copy in copies:
        copy.wait()


def exchanged(value, by, odd):
    size = lax.axis_size("tile")
    pairs = [(i, i + by) for i in range(size - by) if (i // by) % 2 == odd]
    return lax.ppermute(value, "tile", pairs + [(j, i) for i, j in pairs])


def per_device(
    concentrations, tangents, rates, substeps, courant, reactants, products, yields, reaction_index
):
    species = concentrations.shape[0]
    cells = CX * CY
    halves = cells // LANES
    group = tangents.shape[0]
    real = rates.shape[0]
    reactions = up_to(real, 8)
    listed = up_to(reactions, LANES)
    lists = up_to(4 * listed // LANES, 8)
    across = math.isqrt(lax.axis_size("tile"))
    table = static_tables()
    vmem = pl.BlockSpec(memory_space=pltpu.VMEM)
    smem = pl.BlockSpec(memory_space=pltpu.SMEM)
    hbm = pl.BlockSpec(memory_space=pltpu.HBM)
    limit = pltpu.CompilerParams(vmem_limit_bytes=VMEM_LIMIT)
    _, held_rows = rows_of(reactions, species)

    def shape(*sizes, dtype=F32):
        return jax.ShapeDtypeStruct(sizes, dtype)

    conc = concentrations.reshape(species, halves, LANES)
    sens = tangents.reshape(group, species, halves, LANES)
    rate_rows = rates.reshape(real, halves, LANES)
    numbers = courant.reshape(2 * halves, LANES)

    state = shape((species + 1) * group, LANES)
    strip = shape(species * 8 + up_to(-(-species // 4), 8), LANES)
    wide = shape(strip.shape[0], 2 * LANES)
    held = shape(NMAX, held_rows // 8, 8, LANES)
    work = [pltpu.VMEM(state.shape, F32)] * (1 + 2 * BUFFERS)
    raw = pltpu.VMEM((species, group // 8, halves, 8, LANES), F32)

    ilist, ylist, counts, conc_end, t_a, t_b, held_b, s0, s1, s2, s3 = pl.pallas_call(
        edge_kernel,
        out_shape=[
            shape(lists, LANES, dtype=jnp.int32),
            shape(lists, LANES),
            shape(8, cells),
            shape(species, cells),
            state,
            state,
            held,
            *([strip] * 4),
        ],
        in_specs=[hbm] * 9,
        out_specs=[vmem] * 11,
        scratch_shapes=[
            raw,
            work[0],
            pltpu.VMEM(held.shape, F32),
            pltpu.VMEM((halves, species, LANES), F32),
            pltpu.VMEM((halves, reactions, LANES), F32),
            pltpu.VMEM((2, real), jnp.int32),
            pltpu.VMEM((2, real), jnp.int32),
            pltpu.VMEM((2, real), F32),
            pltpu.VMEM((1, cells), jnp.int32),
            pltpu.VMEM((cells, cells), F32),
            pltpu.VMEM((8, listed), jnp.int32),
            pltpu.VMEM((LANES, listed), F32),
            pltpu.VMEM((2, species, reactions), BF16),
            pltpu.VMEM((2 * reactions, species), BF16),
            pltpu.VMEM((2, species, reactions), BF16),
            pltpu.VMEM((species, cells), F32),
            pltpu.SMEM((group,), jnp.int32),
            pltpu.SMEM((4 * listed,), jnp.int32),
            pltpu.SMEM((2 * listed,), F32),
            *work[1:],
            pltpu.SemaphoreType.DMA((9,)),
        ],
        compiler_params=limit,
        name="edge_columns",
    )(
        *[
            pltpu.with_memory_space_constraint(value, pltpu.HBM)
            for value in (
                reaction_index, reactants.T, products.T, yields.T, substeps,
                jnp.asarray(table["permute"]), conc, rate_rows, sens,
            )
        ]
    )

    ilist, ylist = ilist.reshape(-1)[: 4 * listed], ylist.reshape(-1)
    x_one = exchanged(s0, across, 0)
    x_two = exchanged(s1, across, 1)

    t_b, part, side_high, side_low = pl.pallas_call(
        functools.partial(inner_kernel, real),
        out_shape=[state, wide] + [shape(2 * LANES, 2 * LANES, dtype=BF16)] * 2,
        in_specs=[smem] * 3 + [vmem] * 11,
        out_specs=[vmem] * 4,
        scratch_shapes=work,
        compiler_params=limit,
        name="inner_columns",
    )(
        ilist, ylist, reaction_index, counts, numbers, jnp.asarray(table["side_pick"]),
        jnp.asarray(table["side_in"]), jnp.asarray(table["side_out"]), s0, s1, s2, s3,
        held_b, t_b,
    )

    to_one, to_two = pl.pallas_call(
        side_kernel,
        out_shape=[strip, strip],
        in_specs=[vmem] * 5,
        out_specs=[vmem] * 2,
        compiler_params=limit,
        name="y_edges",
    )(part, x_one, x_two, side_high, side_low)
    y_one = exchanged(to_one, 1, 0)
    y_two = exchanged(to_two, 1, 1)

    map_ = shape(3 * LANES, cells, dtype=BF16)
    t_b, map_high, map_low = pl.pallas_call(
        functools.partial(later_kernel, real),
        out_shape=[state, map_, map_],
        in_specs=[smem] * 3 + [vmem] * 7,
        out_specs=[vmem] * 3,
        scratch_shapes=work,
        compiler_params=limit,
        name="inner_later",
    )(
        ilist, ylist, reaction_index, counts, held_b, t_b, numbers,
        jnp.asarray(table["entries"]), jnp.asarray(table["cells"]),
        jnp.asarray(table["cells_rows"]),
    )

    result, conc_out = pl.pallas_call(
        advect_kernel,
        out_shape=[shape(group, species, halves, LANES), shape(species, halves, LANES)],
        in_specs=[vmem] * 9,
        out_specs=[hbm, hbm],
        scratch_shapes=[
            raw,
            pltpu.VMEM((halves, species, LANES), F32),
            pltpu.VMEM((group // 8, species * 8, LANES), F32),
            pltpu.SemaphoreType.DMA((2,)),
        ],
        compiler_params=limit,
        name="advection",
    )(
        conc_end, x_one, x_two, y_one, y_two, map_high, map_low, t_a, t_b,
    )
    return (
        conc_out.reshape(species, 1, cells),
        result.reshape(group, species, 1, cells),
    )


def solution(mesh):
    in_specs = (
        P(None, "tile", None),
        P("pgrp", None, "tile", None),
        P(None, "tile", None),
        P("tile", None),
        P(None, "tile", None),
        P(),
        P(),
        P(),
        P("pgrp"),
    )
    out_specs = (P(None, "tile", None), P("pgrp", None, "tile", None))
    return jax.shard_map(
        per_device, mesh=mesh, in_specs=in_specs, out_specs=out_specs, check_vma=False
    )
```

```python
import functools
import math

import jax
import jax.numpy as jnp
import numpy as np
from jax import lax
from jax.experimental import pallas as pl
from jax.experimental.pallas import tpu as pltpu
from jax.sharding import PartitionSpec as P

CX = 16
CY = 16
NMAX = 4
LANES = 128
UNROLL = 32
BUFFERS = 2
SPLIT = 2
VMEM_LIMIT = 36 * 2**20
F32 = jnp.float32
BF16 = jnp.bfloat16


def orders():
    last, end = CX - 2, CY - 2
    west = [(i, j) for i in range(2) for j in range(CY)]
    east = [(i, j) for i in range(last, CX) for j in range(CY)]
    south = [(i, j) for j in range(2) for i in range(CX)]
    north = [(i, j) for j in range(end, CY) for i in range(CX)]
    strips = west + east + south + north
    edge = list(dict.fromkeys(strips))
    inner = [(i, j) for i in range(CX) for j in range(CY) if (i, j) not in set(edge)]
    return edge + inner, strips


def one_hot(source, wanted):
    place = {cell: k for k, cell in enumerate(source)}
    table = np.zeros((len(source), len(wanted)), np.float32)
    for lane, cell in enumerate(wanted):
        if cell is not None:
            table[place[cell], lane] = 1.0
    return table


def static_tables():
    order, strips = orders()
    cells = [(i, j) for i in range(CX) for j in range(CY)]
    west = [(i - CX, j) for i, j in strips[32:64]]
    east = [(i + CX, j) for i, j in strips[0:32]]
    south = [(i, j - CY) for i, j in strips[96:128]]
    north = [(i, j + CY) for i, j in strips[64:96]]
    blocks = [order[32 * k : 32 * k + 32] for k in range(4)] + [west, east]
    side_in = [(i, j, q) for block in blocks for q in range(4) for i, j in block]
    own_sides = (strips[64:96], strips[96:128])
    side_out = [(i, j, q) for block in own_sides for q in range(4) for i, j in block]
    entries = order + west + east + south + north
    return {
        "permute": one_hot(cells, order),
        "side_pick": one_hot(cells, [(i, j) for i, j, _ in side_out]),
        "side_in": np.array(side_in, np.int32),
        "side_out": np.array(side_out, np.int32).T,
        "entries": np.array(entries, np.int32),
        "cells": np.array(cells, np.int32),
        "cells_rows": np.array(cells, np.int32).T,
    }


def dot(left, right):
    return jnp.dot(left, right, preferred_element_type=F32)


def parts_of(value, count):
    parts = []
    for k in range(count):
        part = value.astype(BF16)
        parts.append(part)
        if k + 1 < count:
            value = value - part.astype(F32)
    return parts


def select_left(exact, value, count):
    return sum(dot(exact, part) for part in parts_of(value, count))


def select_right(value, exact, count):
    return sum(dot(part, exact) for part in parts_of(value, count))


def product(left_parts, value):
    high, low = parts_of(value, 2)
    return dot(left_parts[0], high) + (dot(left_parts[0], low) + dot(left_parts[1], high))


def product_right(value, right_parts):
    high, low = parts_of(value, 2)
    return dot(high, right_parts[0]) + (dot(low, right_parts[0]) + dot(high, right_parts[1]))


def lane_of(rows):
    return lax.broadcasted_iota(jnp.int32, (rows, LANES), 1)


def swap_blocks(arrays):
    lane = lane_of(arrays[0].shape[0])
    low = lane < 64
    even = (lane // 32) % 2 == 0
    a, b, c, d = arrays
    a, c = (
        jnp.where(low, a, pltpu.roll(c, 64, 1)),
        jnp.where(low, pltpu.roll(a, 64, 1), c),
    )
    b, d = (
        jnp.where(low, b, pltpu.roll(d, 64, 1)),
        jnp.where(low, pltpu.roll(b, 64, 1), d),
    )
    a, b = (
        jnp.where(even, a, pltpu.roll(b, 32, 1)),
        jnp.where(even, pltpu.roll(a, 96, 1), b),
    )
    c, d = (
        jnp.where(even, c, pltpu.roll(d, 32, 1)),
        jnp.where(even, pltpu.roll(c, 96, 1), d),
    )
    return [a, b, c, d]


def tangent_copies(source, target, sems):
    return [
        pltpu.make_async_copy(source.at[p], target.at[:, p // 8, :, p % 8, :], sems.at[p // 8])
        for p in range(source.shape[0])
    ]


def up_to(value, step):
    return -(-value // step) * step


def rows_of(reactions, species):
    padded = up_to(species, 8)
    starts = [0, reactions, 2 * reactions]
    starts += [3 * reactions + k * padded for k in range(3)]
    return starts, 3 * reactions + 3 * padded


def tangent_chemistry(
    ilist, ylist, chosen, held, real, group, origin, t, x, used, made, start, stop
):
    species = t.shape[0] // group - 1
    reactions = up_to(real, 8)
    listed = ilist.shape[0] // 4
    at_a, at_b, at_flux, at_fd, at_fda, at_again = [at // 8 for at in rows_of(reactions, species)[0]]
    sublane = lax.broadcasted_iota(jnp.int32, (8, LANES), 0)

    def rows(place):
        return pl.ds(pl.multiple_of(place, group), group)

    def apply(source, n):
        def some(step, count):
            for k0 in range(0, count, BUFFERS):
                batch = range(k0, min(k0 + BUFFERS, count))
                mixes, places, olds = [], [], []
                for k in batch:
                    r = step * UNROLL + k
                    tile, k8 = step * (UNROLL // 8) + k // 8, k % 8
                    place = [rows(ilist[row * listed + r]) for row in range(4)]
                    mixes.append(
                        held[n, at_a + tile, k8 : k8 + 1, :] * source[place[0], :]
                        + held[n, at_b + tile, k8 : k8 + 1, :] * source[place[1], :]
                    )
                    places.append(place)
                for k, (i1, i2, q1, q2) in enumerate(places):
                    lost, gained = used[k], made[k]
                    olds.append((lost[i1, :], lost[i2, :], gained[q1, :], gained[q2, :]))
                for k, (i1, i2, q1, q2) in enumerate(places):
                    r = step * UNROLL + k0 + k
                    mix, old = mixes[k], olds[k]
                    used[k][i1, :] = old[0] - mix
                    used[k][i2, :] = old[1] - mix
                    made[k][q1, :] = old[2] + ylist[r] * mix
                    made[k][q2, :] = old[3] + ylist[listed + r] * mix

        def body(step, carry):
            some(step, UNROLL)
            return carry

        lax.fori_loop(0, real // UNROLL, body, 0)
        if real % UNROLL:
            some(real // UNROLL, real % UNROLL)

    def force(n):
        def body(p8, carry):
            at = sublane == p8
            for q in range(group // 8):
                r = chosen[q * 8 + p8]
                flux = held[n, at_flux + r // 8, pl.ds(r % 8, 1), :]
                value = jnp.where(at, flux, 0.0)
                i1, i2, q1, q2 = [
                    pl.ds(pl.multiple_of(ilist[row * listed + r] + q * 8, 8), 8) for row in range(4)
                ]
                lost, gained = used[q % BUFFERS], made[q % BUFFERS]
                one, two = lost[i1, :], lost[i2, :]
                three, four = gained[q1, :], gained[q2, :]
                lost[i1, :] = one - value
                lost[i2, :] = two - value
                gained[q1, :] = three + ylist[r] * value
                gained[q2, :] = four + ylist[listed + r] * value
            return carry

        lax.fori_loop(0, 8, body, 0, unroll=4)

    def total(at):
        value = used[0][at, :] + made[0][at, :]
        for k in range(1, BUFFERS):
            value = value + (used[k][at, :] + made[k][at, :])
        return value

    def each(work, target):
        def batch(step, count):
            places = [rows((step * 8 + k) * group) for k in range(count)]
            news = [work(place, step, k) for k, place in enumerate(places)]
            for place, (value, kept) in zip(places, news, strict=True):
                target[place, :] = value
                used[0][place, :] = kept

        def body(step, carry):
            batch(step, 8)
            return carry

        lax.fori_loop(0, species // 8, body, 0)
        if species % 8:
            batch(species // 8, species % 8)

    def substep(n, before):
        force(n)
        apply(before, n)

        def first(at, tile, k):
            right = total(at)
            value = right * held[n, at_fd + tile, k : k + 1, :]
            return value, used[0][at, :] + right * held[n, at_again + tile, k : k + 1, :]

        each(first, x)
        apply(x, n)

        def second(at, tile, k):
            right = total(at)
            value = before[at, :] + right * held[n, at_fda + tile, k : k + 1, :]
            return value, used[0][at, :] - right

        each(second, t)

    def more(n, carry):
        substep(n, t)
        return carry

    if origin is t:
        lax.fori_loop(start, stop, more, 0)
        return

    t[species * group :, :] = jnp.zeros((group, LANES), F32)

    @pl.when(start < stop)
    def _():
        substep(start, origin)
        lax.fori_loop(start + 1, stop, more, 0)

    @pl.when(start >= stop)
    def _():
        t[...] = origin[...]


def clear(refs):
    zero = jnp.zeros((LANES, LANES), F32)
    length = refs[0].shape[0]
    for at in range(0, length, LANES):
        for ref in refs:
            ref[at : min(at + LANES, length), :] = zero[0 : min(LANES, length - at)]


def weights(c):
    g = c * (1.0 - c * c) / 6.0
    up = c > 0
    half, square = 0.5 * c, 0.5 * c * c
    return (
        jnp.where(up, -g, 0.0),
        half + square + jnp.where(up, 3.0 * g, -g),
        1.0 - c * c + jnp.where(up, -3.0 * g, 3.0 * g),
        square - half + jnp.where(up, g, -3.0 * g),
        jnp.where(up, 0.0, g),
    )


def edge_kernel(
    chosen_in, reactants_in, products_in, yields_in, counts_in, permute_in, conc, rates, tangents,
    ilist_out, ylist_out, counts_out, conc_out, t, inner, other, s0, s1, s2, s3,
    raw, x, held, conc_in, rates_in, reactants, products, yields, counts, permute,
    pairs, columns, net_parts, hot, uses, base, chosen, ilist, ylist, *rest,
):
    sems = rest[-1]
    used, made = list(rest[:BUFFERS]), list(rest[BUFFERS : 2 * BUFFERS])
    species, real = conc.shape[0], rates.shape[0]
    group = tangents.shape[0]
    reactions = rates_in.shape[1]
    halves = conc_in.shape[0]
    starts, _ = rows_of(reactions, species)
    aligned = real // 8 * 8
    for half in range(halves):
        rates_in[half, aligned:] = jnp.zeros((reactions - aligned, LANES), F32)
    small = [
        pltpu.make_async_copy(conc.at[:, half, :], conc_in.at[half], sems.at[4])
        for half in range(halves)
    ] + [
        pltpu.make_async_copy(rates.at[:, half, :], rates_in.at[half, 0:real, :], sems.at[5])
        for half in range(halves)
    ]
    copies = tangent_copies(tangents, raw, sems)
    tiny = [
        pltpu.make_async_copy(source, target, sems.at[8])
        for source, target in (
            (chosen_in, chosen),
            (reactants_in, reactants),
            (products_in, products),
            (yields_in, yields),
            (counts_in, counts),
            (permute_in, permute),
        )
    ]
    for copy in tiny + small + copies:
        copy.start()
    clear([*used, *made])
    x[species * group :, :] = jnp.zeros((group, LANES), F32)
    for copy in tiny:
        copy.wait()

    pairs[...] = jnp.full(pairs.shape, -1, jnp.int32)
    pairs[0:2, 0:real] = reactants[...]
    pairs[2:4, 0:real] = products[...]
    columns[...] = jnp.zeros(columns.shape, F32)
    columns[0:2, 0:real] = yields[...]
    r0, r1, p0, p1 = [pairs[k : k + 1, :] for k in range(4)]
    y0, y1 = columns[0:1, :], columns[1:2, :]
    same, equal = r0 == r1, p0 == p1
    scale = jnp.where(same, 0.5, 1.0)
    parts = pairs.shape[1] // LANES
    ilist_out[...] = jnp.zeros(ilist_out.shape, jnp.int32)
    ylist_out[...] = jnp.zeros(ylist_out.shape, F32)
    for k, value in enumerate(
        (r0, jnp.where(same, species, r1), p0, jnp.where(equal, species, p1))
    ):
        value = jnp.where(r0 < 0, species, value) * group
        for part in range(parts):
            row = k * parts + part
            ilist_out[row : row + 1, :] = value[:, part * LANES : (part + 1) * LANES]
    for k, value in enumerate(
        (scale * (y0 + jnp.where(equal, y1, 0.0)), scale * jnp.where(equal, 0.0, y1))
    ):
        for part in range(parts):
            row = k * parts + part
            ylist_out[row : row + 1, :] = value[:, part * LANES : (part + 1) * LANES]
    lists = [
        pltpu.make_async_copy(source.at[row], target.at[pl.ds(row * LANES, LANES)], sems.at[6])
        for source, target, count in ((ilist_out, ilist, 4), (ylist_out, ylist, 2))
        for row in range(count * parts)
    ]
    for copy in lists:
        copy.start()

    row = lax.broadcasted_iota(jnp.int32, (species, reactions), 0)
    r0, r1, p0, p1 = [value[:, 0:reactions] for value in (r0, r1, p0, p1)]
    y0, y1 = y0[:, 0:reactions], y1[:, 0:reactions]
    uses_one = row == r0
    uses_two = row == r1
    net = (
        jnp.where(row == p0, y0, 0.0)
        + jnp.where(row == p1, y1, 0.0)
        - jnp.where(uses_one, 1.0, 0.0)
        - jnp.where(uses_two, 1.0, 0.0)
    )
    high, low = parts_of(net, 2)
    net_parts[0] = high
    net_parts[1] = low
    uses[0] = jnp.where(uses_one, 1.0, 0.0).astype(BF16)
    uses[1] = jnp.where(uses_two, 1.0, 0.0).astype(BF16)
    for k, value in enumerate((r0, r1)):
        change = (
            jnp.where(value == p0, y0, 0.0)
            + jnp.where(value == p1, y1, 0.0)
            - jnp.where(value == r0, 1.0, 0.0)
            - jnp.where(value == r1, 1.0, 0.0)
        )
        columns[k : k + 1, 0:reactions] = value.astype(F32)
        columns[2 + k : 3 + k, 0:reactions] = change
    turned = jnp.transpose(columns[...])[0:reactions]
    column = [turned[:, k : k + 1] for k in range(4)]
    lane = lane_of(reactions).astype(F32)
    for k in range(2):
        for at in range(0, species, LANES):
            width = min(LANES, species - at)
            value = jnp.where(column[k] == lane + float(at), 1.0, 0.0)[:, 0:width]
            hot[k * reactions : (k + 1) * reactions, at : at + width] = value.astype(BF16)
    same = column[0] == column[1]
    own_one, own_two = column[2], column[3]

    order = permute[...].astype(BF16)
    count = dot(jnp.broadcast_to(counts[...].astype(F32), (8, counts.shape[1])).astype(BF16), order)
    counts_out[...] = count
    count = count[0:1, :]
    factor = 1.0 / count
    highest = jnp.max(count).astype(jnp.int32)
    for copy in small:
        copy.wait()
    base[...] = select_right(jnp.concatenate([conc_in[0], conc_in[1]], axis=1), order, 3)
    rate = select_right(jnp.concatenate([rates_in[0], rates_in[1]], axis=1), order, 3)

    def keep(n, k, value):
        for ref, part in ((held, value[:, :LANES]), (other, value[:, LANES:])):
            full = value.shape[0] // 8 * 8
            first, tile = starts[k] // 8, (starts[k] + full) // 8
            ref[n, first:tile] = part[:full].reshape(full // 8, 8, LANES)
            if full < value.shape[0]:
                ref[n, tile, 0 : value.shape[0] - full, :] = part[full:]

    def substep(n, carry):
        c = base[...]
        picked = select_left(hot[...], c, 2)
        one, two = picked[:reactions], picked[reactions:]
        a = rate * two
        b = rate * one
        flux = a * one
        nets = (net_parts[0], net_parts[1])
        diagonal = select_left(uses[0], own_one * a, 2) + select_left(uses[1], own_two * b, 2)
        change = product(nets, flux)
        divisor = 1.0 - factor * diagonal
        fd = factor / divisor
        start = fd * change
        along = select_left(hot[...], start, 2)
        again = product(nets, a * along[:reactions] + b * along[reactions:])
        move = fd * (change + (again - diagonal * start))
        active = n.astype(F32) < count
        base[...] = c + jnp.where(active, move, 0.0)
        keep(n, 0, jnp.where(same, 2.0 * (a + b), a))
        keep(n, 1, jnp.where(same, 0.0, b))
        keep(n, 2, jnp.where(same, 2.0 * flux, flux))
        keep(n, 3, fd)
        keep(n, 4, jnp.where(active, fd, 0.0))
        keep(n, 5, fd * (count - 2.0 * diagonal) - 1.0)
        return carry

    lax.fori_loop(0, highest, substep, 0)
    conc_out[...] = base[...]

    for copy in copies:
        copy.wait()
    for q in range(raw.shape[1]):
        both = jnp.concatenate(
            [raw[:, q, half].reshape(species * 8, LANES) for half in range(halves)], axis=1
        )
        picked = select_right(both, order, 2)
        rows = slice(q * 8, (q + 1) * 8)
        for ref, part in ((t, picked[:, :LANES]), (inner, picked[:, LANES:])):
            by_species(ref, group)[0:species, rows, :] = part.reshape(species, 8, LANES)
    for ref in (t, inner):
        ref[species * group :, :] = jnp.zeros((group, LANES), F32)
    for copy in lists:
        copy.wait()
    own = jnp.max(count[:, :LANES]).astype(jnp.int32)
    tangent_chemistry(ilist, ylist, chosen, held, real, group, t, t, x, used, made, 0, own)

    rows = species * 8
    strips = swap_blocks(
        [
            by_species(t, group)[0:species, q * 8 : (q + 1) * 8, :].reshape(rows, LANES)
            for q in range(4)
        ]
    )
    quarter = up_to(-(-species // 4), 8)
    tails = []
    for q in range(4):
        part = base[q * quarter : min((q + 1) * quarter, species), 0:LANES]
        if part.shape[0] < quarter:
            empty = jnp.zeros((quarter - part.shape[0], LANES), F32)
            part = jnp.concatenate([part, empty], axis=0)
        tails.append(part)
    tails = swap_blocks(tails)
    even = even_row()
    strips[0:2] = ordered(even, strips[1], strips[0])
    tails[0:2] = ordered(even, tails[1], tails[0])
    for ref, value, last in zip((s0, s1, s2, s3), strips, tails, strict=True):
        ref[0:rows] = value
        ref[rows:] = last


def even_row():
    return (lax.axis_index("tile") // math.isqrt(lax.axis_size("tile"))) % 2 == 0


def even_tile():
    return lax.axis_index("tile") % 2 == 0


def ordered(even, one, two):
    return jnp.where(even, one, two), jnp.where(even, two, one)


def by_species(ref, group):
    return ref.reshape(ref.shape[0] // group, group, LANES)


def section(di, dj, c):
    value = jnp.zeros(di.shape, F32)
    for k, weight in enumerate(weights(c)):
        value = jnp.where((di == k - 2) & (dj == 0), weight, value)
    return value


def inner_kernel(
    real, ilist, ylist, chosen, counts, courant, side_pick, side_in, side_out, s0, s1, s2, s3,
    held, t_b,
    t, part, side_high, side_low,
    x, *rest,
):
    used, made = list(rest[:BUFFERS]), list(rest[BUFFERS : 2 * BUFFERS])
    group = chosen.shape[0]
    species = t_b.shape[0] // group - 1
    cx = jnp.concatenate([courant[0:1, :], courant[1:2, :]], axis=1)
    c = select_right(jnp.broadcast_to(cx, (8, cx.shape[1])), side_pick[...].astype(BF16), 3)[0:1, :]
    di = side_in[:, 0:1] - side_out[0:1, :]
    dj = side_in[:, 1:2] - side_out[1:2, :]
    map_ = jnp.where(side_in[:, 2:3] == side_out[2:3, :], section(di, dj, c), 0.0)
    high, low = parts_of(map_, 2)
    near = 4 * LANES
    side_high[...] = high[near:]
    side_low[...] = low[near:]
    last, first = ordered(even_row(), s0[...], s1[...])
    strips = jnp.concatenate([first, last, s2[...], s3[...]], axis=1)
    part[...] = product_right(strips, (high[:near], low[:near]))

    clear([*used, *made])
    x[species * group :, :] = jnp.zeros((group, LANES), F32)
    own = jnp.max(counts[0:1, LANES:]).astype(jnp.int32)
    tangent_chemistry(
        ilist, ylist, chosen, held, real, group, t_b, t, x, used, made,
        0, jnp.minimum(own, SPLIT),
    )


def side_kernel(part, one, two, side_high, side_low, to_one, to_two):
    east, west = ordered(even_row(), one[...], two[...])
    both = jnp.concatenate([west, east], axis=1)
    value = part[...] + product_right(both, (side_high[...], side_low[...]))
    to_one[...], to_two[...] = ordered(even_tile(), value[:, LANES:], value[:, :LANES])


def later_kernel(
    real, ilist, ylist, chosen, counts, held, t_b, courant, entries, cells, cells_rows,
    t, map_high, map_low,
    x, *rest,
):
    cx = jnp.concatenate([courant[0:1, :], courant[1:2, :]], axis=1)
    cy = jnp.concatenate([courant[2:3, :], courant[3:4, :]], axis=1)
    di = entries[:, 0:1] - cells_rows[0:1, :]
    dj = entries[:, 1:2] - cells_rows[1:2, :]
    along_x = section(di, dj, cx)
    late = lax.broadcasted_iota(jnp.int32, di.shape, 0) >= di.shape[0] - 64
    along_y = jnp.where(late, section(dj, di, cy), 0.0)
    both = section(cells[:, 1:2] - cells_rows[1:2, :], cells[:, 0:1] - cells_rows[0:1, :], cy)
    whole = along_y + jnp.dot(
        along_x, both, precision=lax.Precision.HIGHEST, preferred_element_type=F32
    )
    map_high[...], map_low[...] = parts_of(whole, 2)
    used, made = list(rest[:BUFFERS]), list(rest[BUFFERS : 2 * BUFFERS])
    group = chosen.shape[0]
    species = t_b.shape[0] // group - 1
    clear([*used, *made])
    x[species * group :, :] = jnp.zeros((group, LANES), F32)
    own = jnp.max(counts[0:1, LANES:]).astype(jnp.int32)
    tangent_chemistry(
        ilist, ylist, chosen, held, real, group, t_b, t, x, used, made,
        SPLIT, own,
    )


def advect_kernel(
    conc, h0, h1, h3, h2, map_high, map_low, t_a, t_b,
    t_out, conc_out,
    done, conc_done, halo_ref, sems,
):
    species = conc.shape[0]
    group = t_out.shape[0]
    rows = species * 8
    high, low = map_high[...], map_low[...]
    own = 2 * LANES
    local, outer = (high[:own], low[:own]), (high[own:], low[own:])

    east, west = ordered(even_row(), h0[...], h1[...])
    north, south = ordered(even_tile(), h2[...], h3[...])
    halo = swap_blocks([west, east, south, north])
    twice = jnp.concatenate([outer[0], outer[0]], axis=0)

    def from_halo(value):
        high, low = parts_of(value, 2)
        return dot(jnp.concatenate([high, low], axis=1), twice) + dot(high, outer[1])

    outside = jnp.concatenate([value[rows:] for value in halo], axis=0)
    base = product_right(conc[...], local) + from_halo(outside[0:species])
    copies = []
    for half in range(2):
        conc_done[half] = base[:, half * LANES : (half + 1) * LANES]
        copies.append(
            pltpu.make_async_copy(conc_done.at[half], conc_out.at[:, half, :], sems.at[1])
        )
        copies[-1].start()
    for q in range(4):
        halo_ref[q] = halo[q][0:rows]

    def sent(q):
        return [
            pltpu.make_async_copy(done.at[:, q, :, p8, :], t_out.at[q * 8 + p8], sems.at[0])
            for p8 in range(8)
        ]

    def body(q, carry):
        part = pl.ds(pl.multiple_of(q * 8, 8), 8)
        inside = jnp.concatenate(
            [by_species(ref, group)[0:species, part, :].reshape(rows, LANES) for ref in (t_a, t_b)],
            axis=1,
        )
        value = product_right(inside, local) + from_halo(halo_ref[q])
        for half in range(2):
            done[:, q, half] = value[:, half * LANES : (half + 1) * LANES].reshape(
                species, 8, LANES
            )
        for copy in sent(q):
            copy.start()
        return carry

    lax.fori_loop(0, group // 8, body, 0)
    for q in range(group // 8):
        copies += sent(q)
    for copy in copies:
        copy.wait()


def exchanged(value, by, odd):
    size = lax.axis_size("tile")
    pairs = [(i, i + by) for i in range(size - by) if (i // by) % 2 == odd]
    return lax.ppermute(value, "tile", pairs + [(j, i) for i, j in pairs])


def per_device(
    concentrations, tangents, rates, substeps, courant, reactants, products, yields, reaction_index
):
    species = concentrations.shape[0]
    cells = CX * CY
    halves = cells // LANES
    group = tangents.shape[0]
    real = rates.shape[0]
    reactions = up_to(real, 8)
    listed = up_to(reactions, LANES)
    lists = up_to(4 * listed // LANES, 8)
    across = math.isqrt(lax.axis_size("tile"))
    table = static_tables()
    vmem = pl.BlockSpec(memory_space=pltpu.VMEM)
    smem = pl.BlockSpec(memory_space=pltpu.SMEM)
    hbm = pl.BlockSpec(memory_space=pltpu.HBM)
    limit = pltpu.CompilerParams(vmem_limit_bytes=VMEM_LIMIT)
    _, held_rows = rows_of(reactions, species)

    def shape(*sizes, dtype=F32):
        return jax.ShapeDtypeStruct(sizes, dtype)

    conc = concentrations.reshape(species, halves, LANES)
    sens = tangents.reshape(group, species, halves, LANES)
    rate_rows = rates.reshape(real, halves, LANES)
    numbers = courant.reshape(2 * halves, LANES)

    state = shape((species + 1) * group, LANES)
    strip = shape(species * 8 + up_to(-(-species // 4), 8), LANES)
    wide = shape(strip.shape[0], 2 * LANES)
    held = shape(NMAX, held_rows // 8, 8, LANES)
    work = [pltpu.VMEM(state.shape, F32)] * (1 + 2 * BUFFERS)
    raw = pltpu.VMEM((species, group // 8, halves, 8, LANES), F32)

    ilist, ylist, counts, conc_end, t_a, t_b, held_b, s0, s1, s2, s3 = pl.pallas_call(
        edge_kernel,
        out_shape=[
            shape(lists, LANES, dtype=jnp.int32),
            shape(lists, LANES),
            shape(8, cells),
            shape(species, cells),
            state,
            state,
            held,
            *([strip] * 4),
        ],
        in_specs=[hbm] * 9,
        out_specs=[vmem] * 11,
        scratch_shapes=[
            raw,
            work[0],
            pltpu.VMEM(held.shape, F32),
            pltpu.VMEM((halves, species, LANES), F32),
            pltpu.VMEM((halves, reactions, LANES), F32),
            pltpu.VMEM((2, real), jnp.int32),
            pltpu.VMEM((2, real), jnp.int32),
            pltpu.VMEM((2, real), F32),
            pltpu.VMEM((1, cells), jnp.int32),
            pltpu.VMEM((cells, cells), F32),
            pltpu.VMEM((8, listed), jnp.int32),
            pltpu.VMEM((LANES, listed), F32),
            pltpu.VMEM((2, species, reactions), BF16),
            pltpu.VMEM((2 * reactions, species), BF16),
            pltpu.VMEM((2, species, reactions), BF16),
            pltpu.VMEM((species, cells), F32),
            pltpu.SMEM((group,), jnp.int32),
            pltpu.SMEM((4 * listed,), jnp.int32),
            pltpu.SMEM((2 * listed,), F32),
            *work[1:],
            pltpu.SemaphoreType.DMA((9,)),
        ],
        compiler_params=limit,
        name="edge_columns",
    )(
        *[
            pltpu.with_memory_space_constraint(value, pltpu.HBM)
            for value in (
                reaction_index, reactants.T, products.T, yields.T, substeps,
                jnp.asarray(table["permute"]), conc, rate_rows, sens,
            )
        ]
    )

    ilist, ylist = ilist.reshape(-1)[: 4 * listed], ylist.reshape(-1)
    x_one = exchanged(s0, across, 0)
    x_two = exchanged(s1, across, 1)

    t_b, part, side_high, side_low = pl.pallas_call(
        functools.partial(inner_kernel, real),
        out_shape=[state, wide] + [shape(2 * LANES, 2 * LANES, dtype=BF16)] * 2,
        in_specs=[smem] * 3 + [vmem] * 11,
        out_specs=[vmem] * 4,
        scratch_shapes=work,
        compiler_params=limit,
        name="inner_columns",
    )(
        ilist, ylist, reaction_index, counts, numbers, jnp.asarray(table["side_pick"]),
        jnp.asarray(table["side_in"]), jnp.asarray(table["side_out"]), s0, s1, s2, s3,
        held_b, t_b,
    )

    to_one, to_two = pl.pallas_call(
        side_kernel,
        out_shape=[strip, strip],
        in_specs=[vmem] * 5,
        out_specs=[vmem] * 2,
        compiler_params=limit,
        name="y_edges",
    )(part, x_one, x_two, side_high, side_low)
    y_two = exchanged(to_two, 1, 1)
    y_one = exchanged(to_one, 1, 0)

    map_ = shape(3 * LANES, cells, dtype=BF16)
    t_b, map_high, map_low = pl.pallas_call(
        functools.partial(later_kernel, real),
        out_shape=[state, map_, map_],
        in_specs=[smem] * 3 + [vmem] * 7,
        out_specs=[vmem] * 3,
        scratch_shapes=work,
        compiler_params=limit,
        name="inner_later",
    )(
        ilist, ylist, reaction_index, counts, held_b, t_b, numbers,
        jnp.asarray(table["entries"]), jnp.asarray(table["cells"]),
        jnp.asarray(table["cells_rows"]),
    )

    result, conc_out = pl.pallas_call(
        advect_kernel,
        out_shape=[shape(group, species, halves, LANES), shape(species, halves, LANES)],
        in_specs=[vmem] * 9,
        out_specs=[hbm, hbm],
        scratch_shapes=[
            raw,
            pltpu.VMEM((halves, species, LANES), F32),
            pltpu.VMEM((group // 8, species * 8, LANES), F32),
            pltpu.SemaphoreType.DMA((2,)),
        ],
        compiler_params=limit,
        name="advection",
    )(
        conc_end, x_one, x_two, y_two, y_one, map_high, map_low, t_a, t_b,
    )
    return (
        conc_out.reshape(species, 1, cells),
        result.reshape(group, species, 1, cells),
    )


def solution(mesh):
    in_specs = (
        P(None, "tile", None),
        P("pgrp", None, "tile", None),
        P(None, "tile", None),
        P("tile", None),
        P(None, "tile", None),
        P(),
        P(),
        P(),
        P("pgrp"),
    )
    out_specs = (P(None, "tile", None), P("pgrp", None, "tile", None))
    return jax.shard_map(
        per_device, mesh=mesh, in_specs=in_specs, out_specs=out_specs, check_vma=False
    )
```

```python
import functools
import math

import jax
import jax.numpy as jnp
import numpy as np
from jax import lax
from jax.experimental import pallas as pl
from jax.experimental.pallas import tpu as pltpu
from jax.sharding import PartitionSpec as P

CX = 16
CY = 16
NMAX = 4
LANES = 128
UNROLL = 32
BUFFERS = 2
SPLIT = 2
VMEM_LIMIT = 36 * 2**20
F32 = jnp.float32
BF16 = jnp.bfloat16


def orders():
    last, end = CX - 2, CY - 2
    west = [(i, j) for i in range(2) for j in range(CY)]
    east = [(i, j) for i in range(last, CX) for j in range(CY)]
    south = [(i, j) for j in range(2) for i in range(CX)]
    north = [(i, j) for j in range(end, CY) for i in range(CX)]
    strips = west + east + south + north
    edge = list(dict.fromkeys(strips))
    inner = [(i, j) for i in range(CX) for j in range(CY) if (i, j) not in set(edge)]
    return edge + inner, strips


def one_hot(source, wanted):
    place = {cell: k for k, cell in enumerate(source)}
    table = np.zeros((len(source), len(wanted)), np.float32)
    for lane, cell in enumerate(wanted):
        if cell is not None:
            table[place[cell], lane] = 1.0
    return table


def static_tables():
    order, strips = orders()
    cells = [(i, j) for i in range(CX) for j in range(CY)]
    west = [(i - CX, j) for i, j in strips[32:64]]
    east = [(i + CX, j) for i, j in strips[0:32]]
    south = [(i, j - CY) for i, j in strips[96:128]]
    north = [(i, j + CY) for i, j in strips[64:96]]
    blocks = [order[32 * k : 32 * k + 32] for k in range(4)] + [west, east]
    side_in = [(i, j, q) for block in blocks for q in range(4) for i, j in block]
    own_sides = (strips[64:96], strips[96:128])
    side_out = [(i, j, q) for block in own_sides for q in range(4) for i, j in block]
    entries = order + west + east + south + north
    return {
        "permute": one_hot(cells, order),
        "side_pick": one_hot(cells, [(i, j) for i, j, _ in side_out]),
        "side_in": np.array(side_in, np.int32),
        "side_out": np.array(side_out, np.int32).T,
        "entries": np.array(entries, np.int32),
        "cells": np.array(cells, np.int32),
        "cells_rows": np.array(cells, np.int32).T,
    }


def dot(left, right):
    return jnp.dot(left, right, preferred_element_type=F32)


def parts_of(value, count):
    parts = []
    for k in range(count):
        part = value.astype(BF16)
        parts.append(part)
        if k + 1 < count:
            value = value - part.astype(F32)
    return parts


def select_left(exact, value, count):
    return sum(dot(exact, part) for part in parts_of(value, count))


def select_right(value, exact, count):
    return sum(dot(part, exact) for part in parts_of(value, count))


def product(left_parts, value):
    high, low = parts_of(value, 2)
    return dot(left_parts[0], high) + (dot(left_parts[0], low) + dot(left_parts[1], high))


def product_right(value, right_parts):
    high, low = parts_of(value, 2)
    return dot(high, right_parts[0]) + (dot(low, right_parts[0]) + dot(high, right_parts[1]))


def lane_of(rows):
    return lax.broadcasted_iota(jnp.int32, (rows, LANES), 1)


def swap_blocks(arrays):
    lane = lane_of(arrays[0].shape[0])
    low = lane < 64
    even = (lane // 32) % 2 == 0
    a, b, c, d = arrays
    a, c = (
        jnp.where(low, a, pltpu.roll(c, 64, 1)),
        jnp.where(low, pltpu.roll(a, 64, 1), c),
    )
    b, d = (
        jnp.where(low, b, pltpu.roll(d, 64, 1)),
        jnp.where(low, pltpu.roll(b, 64, 1), d),
    )
    a, b = (
        jnp.where(even, a, pltpu.roll(b, 32, 1)),
        jnp.where(even, pltpu.roll(a, 96, 1), b),
    )
    c, d = (
        jnp.where(even, c, pltpu.roll(d, 32, 1)),
        jnp.where(even, pltpu.roll(c, 96, 1), d),
    )
    return [a, b, c, d]


def tangent_copies(source, target, sems):
    return [
        pltpu.make_async_copy(source.at[p], target.at[:, p // 8, :, p % 8, :], sems.at[p // 8])
        for p in range(source.shape[0])
    ]


def up_to(value, step):
    return -(-value // step) * step


def rows_of(reactions, species):
    padded = up_to(species, 8)
    starts = [0, reactions, 2 * reactions]
    starts += [3 * reactions + k * padded for k in range(3)]
    return starts, 3 * reactions + 3 * padded


def tangent_chemistry(
    ilist, ylist, chosen, held, real, group, origin, t, x, used, made, start, stop
):
    species = t.shape[0] // group - 1
    reactions = up_to(real, 8)
    listed = ilist.shape[0] // 4
    at_a, at_b, at_flux, at_fd, at_fda, at_again = [at // 8 for at in rows_of(reactions, species)[0]]
    sublane = lax.broadcasted_iota(jnp.int32, (8, LANES), 0)

    def rows(place):
        return pl.ds(pl.multiple_of(place, group), group)

    def apply(source, n):
        def some(step, count):
            for k0 in range(0, count, BUFFERS):
                batch = range(k0, min(k0 + BUFFERS, count))
                mixes, places, olds = [], [], []
                for k in batch:
                    r = step * UNROLL + k
                    tile, k8 = step * (UNROLL // 8) + k // 8, k % 8
                    place = [rows(ilist[row * listed + r]) for row in range(4)]
                    mixes.append(
                        held[n, at_a + tile, k8 : k8 + 1, :] * source[place[0], :]
                        + held[n, at_b + tile, k8 : k8 + 1, :] * source[place[1], :]
                    )
                    places.append(place)
                for k, (i1, i2, q1, q2) in enumerate(places):
                    lost, gained = used[k], made[k]
                    olds.append((lost[i1, :], lost[i2, :], gained[q1, :], gained[q2, :]))
                for k, (i1, i2, q1, q2) in enumerate(places):
                    r = step * UNROLL + k0 + k
                    mix, old = mixes[k], olds[k]
                    used[k][i1, :] = old[0] - mix
                    used[k][i2, :] = old[1] - mix
                    made[k][q1, :] = old[2] + ylist[r] * mix
                    made[k][q2, :] = old[3] + ylist[listed + r] * mix

        def body(step, carry):
            some(step, UNROLL)
            return carry

        lax.fori_loop(0, real // UNROLL, body, 0)
        if real % UNROLL:
            some(real // UNROLL, real % UNROLL)

    def force(n):
        def body(p8, carry):
            at = sublane == p8
            for q in range(group // 8):
                r = chosen[q * 8 + p8]
                flux = held[n, at_flux + r // 8, pl.ds(r % 8, 1), :]
                value = jnp.where(at, flux, 0.0)
                i1, i2, q1, q2 = [
                    pl.ds(pl.multiple_of(ilist[row * listed + r] + q * 8, 8), 8) for row in range(4)
                ]
                lost, gained = used[q % BUFFERS], made[q % BUFFERS]
                one, two = lost[i1, :], lost[i2, :]
                three, four = gained[q1, :], gained[q2, :]
                lost[i1, :] = one - value
                lost[i2, :] = two - value
                gained[q1, :] = three + ylist[r] * value
                gained[q2, :] = four + ylist[listed + r] * value
            return carry

        lax.fori_loop(0, 8, body, 0, unroll=4)

    def total(at):
        value = used[0][at, :] + made[0][at, :]
        for k in range(1, BUFFERS):
            value = value + (used[k][at, :] + made[k][at, :])
        return value

    def each(work, target):
        def batch(step, count):
            places = [rows((step * 8 + k) * group) for k in range(count)]
            news = [work(place, step, k) for k, place in enumerate(places)]
            for place, (value, kept) in zip(places, news, strict=True):
                target[place, :] = value
                used[0][place, :] = kept

        def body(step, carry):
            batch(step, 8)
            return carry

        lax.fori_loop(0, species // 8, body, 0, unroll=2)
        if species % 8:
            batch(species // 8, species % 8)

    def substep(n, before):
        force(n)
        apply(before, n)

        def first(at, tile, k):
            right = total(at)
            value = right * held[n, at_fd + tile, k : k + 1, :]
            return value, used[0][at, :] + right * held[n, at_again + tile, k : k + 1, :]

        each(first, x)
        apply(x, n)

        def second(at, tile, k):
            right = total(at)
            value = before[at, :] + right * held[n, at_fda + tile, k : k + 1, :]
            return value, used[0][at, :] - right

        each(second, t)

    def more(n, carry):
        substep(n, t)
        return carry

    if origin is t:
        lax.fori_loop(start, stop, more, 0)
        return

    t[species * group :, :] = jnp.zeros((group, LANES), F32)

    @pl.when(start < stop)
    def _():
        substep(start, origin)
        lax.fori_loop(start + 1, stop, more, 0)

    @pl.when(start >= stop)
    def _():
        t[...] = origin[...]


def clear(refs):
    zero = jnp.zeros((LANES, LANES), F32)
    length = refs[0].shape[0]
    for at in range(0, length, LANES):
        for ref in refs:
            ref[at : min(at + LANES, length), :] = zero[0 : min(LANES, length - at)]


def weights(c):
    g = c * (1.0 - c * c) / 6.0
    up = c > 0
    half, square = 0.5 * c, 0.5 * c * c
    return (
        jnp.where(up, -g, 0.0),
        half + square + jnp.where(up, 3.0 * g, -g),
        1.0 - c * c + jnp.where(up, -3.0 * g, 3.0 * g),
        square - half + jnp.where(up, g, -3.0 * g),
        jnp.where(up, 0.0, g),
    )


def edge_kernel(
    chosen_in, reactants_in, products_in, yields_in, counts_in, permute_in, conc, rates, tangents,
    ilist_out, ylist_out, counts_out, conc_out, t, inner, other, s0, s1, s2, s3,
    raw, x, held, conc_in, rates_in, reactants, products, yields, counts, permute,
    pairs, columns, net_parts, hot, uses, base, chosen, ilist, ylist, *rest,
):
    sems = rest[-1]
    used, made = list(rest[:BUFFERS]), list(rest[BUFFERS : 2 * BUFFERS])
    species, real = conc.shape[0], rates.shape[0]
    group = tangents.shape[0]
    reactions = rates_in.shape[1]
    halves = conc_in.shape[0]
    starts, _ = rows_of(reactions, species)
    aligned = real // 8 * 8
    for half in range(halves):
        rates_in[half, aligned:] = jnp.zeros((reactions - aligned, LANES), F32)
    small = [
        pltpu.make_async_copy(conc.at[:, half, :], conc_in.at[half], sems.at[4])
        for half in range(halves)
    ] + [
        pltpu.make_async_copy(rates.at[:, half, :], rates_in.at[half, 0:real, :], sems.at[5])
        for half in range(halves)
    ]
    copies = tangent_copies(tangents, raw, sems)
    tiny = [
        pltpu.make_async_copy(source, target, sems.at[8])
        for source, target in (
            (chosen_in, chosen),
            (reactants_in, reactants),
            (products_in, products),
            (yields_in, yields),
            (counts_in, counts),
            (permute_in, permute),
        )
    ]
    for copy in tiny + small + copies:
        copy.start()
    clear([*used, *made])
    x[species * group :, :] = jnp.zeros((group, LANES), F32)
    for copy in tiny:
        copy.wait()

    pairs[...] = jnp.full(pairs.shape, -1, jnp.int32)
    pairs[0:2, 0:real] = reactants[...]
    pairs[2:4, 0:real] = products[...]
    columns[...] = jnp.zeros(columns.shape, F32)
    columns[0:2, 0:real] = yields[...]
    r0, r1, p0, p1 = [pairs[k : k + 1, :] for k in range(4)]
    y0, y1 = columns[0:1, :], columns[1:2, :]
    same, equal = r0 == r1, p0 == p1
    scale = jnp.where(same, 0.5, 1.0)
    parts = pairs.shape[1] // LANES
    ilist_out[...] = jnp.zeros(ilist_out.shape, jnp.int32)
    ylist_out[...] = jnp.zeros(ylist_out.shape, F32)
    for k, value in enumerate(
        (r0, jnp.where(same, species, r1), p0, jnp.where(equal, species, p1))
    ):
        value = jnp.where(r0 < 0, species, value) * group
        for part in range(parts):
            row = k * parts + part
            ilist_out[row : row + 1, :] = value[:, part * LANES : (part + 1) * LANES]
    for k, value in enumerate(
        (scale * (y0 + jnp.where(equal, y1, 0.0)), scale * jnp.where(equal, 0.0, y1))
    ):
        for part in range(parts):
            row = k * parts + part
            ylist_out[row : row + 1, :] = value[:, part * LANES : (part + 1) * LANES]
    lists = [
        pltpu.make_async_copy(source.at[row], target.at[pl.ds(row * LANES, LANES)], sems.at[6])
        for source, target, count in ((ilist_out, ilist, 4), (ylist_out, ylist, 2))
        for row in range(count * parts)
    ]
    for copy in lists:
        copy.start()

    row = lax.broadcasted_iota(jnp.int32, (species, reactions), 0)
    r0, r1, p0, p1 = [value[:, 0:reactions] for value in (r0, r1, p0, p1)]
    y0, y1 = y0[:, 0:reactions], y1[:, 0:reactions]
    uses_one = row == r0
    uses_two = row == r1
    net = (
        jnp.where(row == p0, y0, 0.0)
        + jnp.where(row == p1, y1, 0.0)
        - jnp.where(uses_one, 1.0, 0.0)
        - jnp.where(uses_two, 1.0, 0.0)
    )
    high, low = parts_of(net, 2)
    net_parts[0] = high
    net_parts[1] = low
    uses[0] = jnp.where(uses_one, 1.0, 0.0).astype(BF16)
    uses[1] = jnp.where(uses_two, 1.0, 0.0).astype(BF16)
    for k, value in enumerate((r0, r1)):
        change = (
            jnp.where(value == p0, y0, 0.0)
            + jnp.where(value == p1, y1, 0.0)
            - jnp.where(value == r0, 1.0, 0.0)
            - jnp.where(value == r1, 1.0, 0.0)
        )
        columns[k : k + 1, 0:reactions] = value.astype(F32)
        columns[2 + k : 3 + k, 0:reactions] = change
    turned = jnp.transpose(columns[...])[0:reactions]
    column = [turned[:, k : k + 1] for k in range(4)]
    lane = lane_of(reactions).astype(F32)
    for k in range(2):
        for at in range(0, species, LANES):
            width = min(LANES, species - at)
            value = jnp.where(column[k] == lane + float(at), 1.0, 0.0)[:, 0:width]
            hot[k * reactions : (k + 1) * reactions, at : at + width] = value.astype(BF16)
    same = column[0] == column[1]
    own_one, own_two = column[2], column[3]

    order = permute[...].astype(BF16)
    count = dot(jnp.broadcast_to(counts[...].astype(F32), (8, counts.shape[1])).astype(BF16), order)
    counts_out[...] = count
    count = count[0:1, :]
    factor = 1.0 / count
    highest = jnp.max(count).astype(jnp.int32)
    for copy in small:
        copy.wait()
    base[...] = select_right(jnp.concatenate([conc_in[0], conc_in[1]], axis=1), order, 3)
    rate = select_right(jnp.concatenate([rates_in[0], rates_in[1]], axis=1), order, 3)

    def keep(n, k, value):
        for ref, part in ((held, value[:, :LANES]), (other, value[:, LANES:])):
            full = value.shape[0] // 8 * 8
            first, tile = starts[k] // 8, (starts[k] + full) // 8
            ref[n, first:tile] = part[:full].reshape(full // 8, 8, LANES)
            if full < value.shape[0]:
                ref[n, tile, 0 : value.shape[0] - full, :] = part[full:]

    def substep(n, carry):
        c = base[...]
        picked = select_left(hot[...], c, 2)
        one, two = picked[:reactions], picked[reactions:]
        a = rate * two
        b = rate * one
        flux = a * one
        nets = (net_parts[0], net_parts[1])
        own = jnp.concatenate([own_one * a, own_two * b], axis=0)
        diagonal = select_left(jnp.concatenate([uses[0], uses[1]], axis=1), own, 2)
        change = product(nets, flux)
        divisor = 1.0 - factor * diagonal
        fd = factor / divisor
        start = fd * change
        along = select_left(hot[...], start, 2)
        again = product(nets, a * along[:reactions] + b * along[reactions:])
        move = fd * (change + (again - diagonal * start))
        active = n.astype(F32) < count
        base[...] = c + jnp.where(active, move, 0.0)
        keep(n, 0, jnp.where(same, 2.0 * (a + b), a))
        keep(n, 1, jnp.where(same, 0.0, b))
        keep(n, 2, jnp.where(same, 2.0 * flux, flux))
        keep(n, 3, fd)
        keep(n, 4, jnp.where(active, fd, 0.0))
        keep(n, 5, fd * (count - 2.0 * diagonal) - 1.0)
        return carry

    lax.fori_loop(0, highest, substep, 0)
    conc_out[...] = base[...]

    for copy in copies:
        copy.wait()
    for q in range(raw.shape[1]):
        both = jnp.concatenate(
            [raw[:, q, half].reshape(species * 8, LANES) for half in range(halves)], axis=1
        )
        picked = select_right(both, order, 2)
        rows = slice(q * 8, (q + 1) * 8)
        for ref, part in ((t, picked[:, :LANES]), (inner, picked[:, LANES:])):
            by_species(ref, group)[0:species, rows, :] = part.reshape(species, 8, LANES)
    for ref in (t, inner):
        ref[species * group :, :] = jnp.zeros((group, LANES), F32)
    for copy in lists:
        copy.wait()
    own = jnp.max(count[:, :LANES]).astype(jnp.int32)
    tangent_chemistry(ilist, ylist, chosen, held, real, group, t, t, x, used, made, 0, own)

    rows = species * 8
    strips = swap_blocks(
        [
            by_species(t, group)[0:species, q * 8 : (q + 1) * 8, :].reshape(rows, LANES)
            for q in range(4)
        ]
    )
    quarter = up_to(-(-species // 4), 8)
    tails = []
    for q in range(4):
        part = base[q * quarter : min((q + 1) * quarter, species), 0:LANES]
        if part.shape[0] < quarter:
            empty = jnp.zeros((quarter - part.shape[0], LANES), F32)
            part = jnp.concatenate([part, empty], axis=0)
        tails.append(part)
    tails = swap_blocks(tails)
    even = even_row()
    strips[0:2] = ordered(even, strips[1], strips[0])
    tails[0:2] = ordered(even, tails[1], tails[0])
    for ref, value, last in zip((s0, s1, s2, s3), strips, tails, strict=True):
        ref[0:rows] = value
        ref[rows:] = last


def even_row():
    return (lax.axis_index("tile") // math.isqrt(lax.axis_size("tile"))) % 2 == 0


def even_tile():
    return lax.axis_index("tile") % 2 == 0


def ordered(even, one, two):
    return jnp.where(even, one, two), jnp.where(even, two, one)


def by_species(ref, group):
    return ref.reshape(ref.shape[0] // group, group, LANES)


def section(di, dj, c):
    value = jnp.zeros(di.shape, F32)
    for k, weight in enumerate(weights(c)):
        value = jnp.where((di == k - 2) & (dj == 0), weight, value)
    return value


def inner_kernel(
    real, ilist, ylist, chosen, counts, courant, side_pick, side_in, side_out, s0, s1, s2, s3,
    held, t_b,
    t, part, side_high, side_low,
    x, *rest,
):
    used, made = list(rest[:BUFFERS]), list(rest[BUFFERS : 2 * BUFFERS])
    group = chosen.shape[0]
    species = t_b.shape[0] // group - 1
    cx = jnp.concatenate([courant[0:1, :], courant[1:2, :]], axis=1)
    c = select_right(jnp.broadcast_to(cx, (8, cx.shape[1])), side_pick[...].astype(BF16), 3)[0:1, :]
    di = side_in[:, 0:1] - side_out[0:1, :]
    dj = side_in[:, 1:2] - side_out[1:2, :]
    map_ = jnp.where(side_in[:, 2:3] == side_out[2:3, :], section(di, dj, c), 0.0)
    high, low = parts_of(map_, 2)
    near = 4 * LANES
    side_high[...] = high[near:]
    side_low[...] = low[near:]
    last, first = ordered(even_row(), s0[...], s1[...])
    strips = jnp.concatenate([first, last, s2[...], s3[...]], axis=1)
    part[...] = product_right(strips, (high[:near], low[:near]))

    clear([*used, *made])
    x[species * group :, :] = jnp.zeros((group, LANES), F32)
    own = jnp.max(counts[0:1, LANES:]).astype(jnp.int32)
    tangent_chemistry(
        ilist, ylist, chosen, held, real, group, t_b, t, x, used, made,
        0, jnp.minimum(own, SPLIT),
    )


def side_kernel(part, one, two, side_high, side_low, to_one, to_two):
    east, west = ordered(even_row(), one[...], two[...])
    both = jnp.concatenate([west, east], axis=1)
    value = part[...] + product_right(both, (side_high[...], side_low[...]))
    to_one[...], to_two[...] = ordered(even_tile(), value[:, LANES:], value[:, :LANES])


def later_kernel(
    real, ilist, ylist, chosen, counts, held, t_b, courant, entries, cells, cells_rows,
    t, map_high, map_low,
    x, *rest,
):
    cx = jnp.concatenate([courant[0:1, :], courant[1:2, :]], axis=1)
    cy = jnp.concatenate([courant[2:3, :], courant[3:4, :]], axis=1)
    di = entries[:, 0:1] - cells_rows[0:1, :]
    dj = entries[:, 1:2] - cells_rows[1:2, :]
    along_x = section(di, dj, cx)
    late = lax.broadcasted_iota(jnp.int32, di.shape, 0) >= di.shape[0] - 64
    along_y = jnp.where(late, section(dj, di, cy), 0.0)
    both = section(cells[:, 1:2] - cells_rows[1:2, :], cells[:, 0:1] - cells_rows[0:1, :], cy)
    whole = along_y + jnp.dot(
        along_x, both, precision=lax.Precision.HIGHEST, preferred_element_type=F32
    )
    map_high[...], map_low[...] = parts_of(whole, 2)
    used, made = list(rest[:BUFFERS]), list(rest[BUFFERS : 2 * BUFFERS])
    group = chosen.shape[0]
    species = t_b.shape[0] // group - 1
    clear([*used, *made])
    x[species * group :, :] = jnp.zeros((group, LANES), F32)
    own = jnp.max(counts[0:1, LANES:]).astype(jnp.int32)
    tangent_chemistry(
        ilist, ylist, chosen, held, real, group, t_b, t, x, used, made,
        SPLIT, own,
    )


def advect_kernel(
    conc, h0, h1, h3, h2, map_high, map_low, t_a, t_b,
    t_out, conc_out,
    done, conc_done, halo_ref, sems,
):
    species = conc.shape[0]
    group = t_out.shape[0]
    rows = species * 8
    high, low = map_high[...], map_low[...]
    own = 2 * LANES
    local, outer = (high[:own], low[:own]), (high[own:], low[own:])

    east, west = ordered(even_row(), h0[...], h1[...])
    north, south = ordered(even_tile(), h2[...], h3[...])
    halo = swap_blocks([west, east, south, north])
    twice = jnp.concatenate([outer[0], outer[0]], axis=0)

    def from_halo(value):
        high, low = parts_of(value, 2)
        return dot(jnp.concatenate([high, low], axis=1), twice) + dot(high, outer[1])

    outside = jnp.concatenate([value[rows:] for value in halo], axis=0)
    base = product_right(conc[...], local) + from_halo(outside[0:species])
    copies = []
    for half in range(2):
        conc_done[half] = base[:, half * LANES : (half + 1) * LANES]
        copies.append(
            pltpu.make_async_copy(conc_done.at[half], conc_out.at[:, half, :], sems.at[1])
        )
        copies[-1].start()
    for q in range(4):
        halo_ref[q] = halo[q][0:rows]

    def sent(q):
        return [
            pltpu.make_async_copy(done.at[:, q, :, p8, :], t_out.at[q * 8 + p8], sems.at[0])
            for p8 in range(8)
        ]

    def body(q, carry):
        part = pl.ds(pl.multiple_of(q * 8, 8), 8)
        inside = jnp.concatenate(
            [by_species(ref, group)[0:species, part, :].reshape(rows, LANES) for ref in (t_a, t_b)],
            axis=1,
        )
        value = product_right(inside, local) + from_halo(halo_ref[q])
        for half in range(2):
            done[:, q, half] = value[:, half * LANES : (half + 1) * LANES].reshape(
                species, 8, LANES
            )
        for copy in sent(q):
            copy.start()
        return carry

    lax.fori_loop(0, group // 8, body, 0)
    for q in range(group // 8):
        copies += sent(q)
    for copy in copies:
        copy.wait()


def exchanged(value, by, odd):
    size = lax.axis_size("tile")
    pairs = [(i, i + by) for i in range(size - by) if (i // by) % 2 == odd]
    return lax.ppermute(value, "tile", pairs + [(j, i) for i, j in pairs])


def per_device(
    concentrations, tangents, rates, substeps, courant, reactants, products, yields, reaction_index
):
    species = concentrations.shape[0]
    cells = CX * CY
    halves = cells // LANES
    group = tangents.shape[0]
    real = rates.shape[0]
    reactions = up_to(real, 8)
    listed = up_to(reactions, LANES)
    lists = up_to(4 * listed // LANES, 8)
    across = math.isqrt(lax.axis_size("tile"))
    table = static_tables()
    vmem = pl.BlockSpec(memory_space=pltpu.VMEM)
    smem = pl.BlockSpec(memory_space=pltpu.SMEM)
    hbm = pl.BlockSpec(memory_space=pltpu.HBM)
    limit = pltpu.CompilerParams(vmem_limit_bytes=VMEM_LIMIT)
    _, held_rows = rows_of(reactions, species)

    def shape(*sizes, dtype=F32):
        return jax.ShapeDtypeStruct(sizes, dtype)

    conc = concentrations.reshape(species, halves, LANES)
    sens = tangents.reshape(group, species, halves, LANES)
    rate_rows = rates.reshape(real, halves, LANES)
    numbers = courant.reshape(2 * halves, LANES)

    state = shape((species + 1) * group, LANES)
    strip = shape(species * 8 + up_to(-(-species // 4), 8), LANES)
    wide = shape(strip.shape[0], 2 * LANES)
    held = shape(NMAX, held_rows // 8, 8, LANES)
    work = [pltpu.VMEM(state.shape, F32)] * (1 + 2 * BUFFERS)
    raw = pltpu.VMEM((species, group // 8, halves, 8, LANES), F32)

    ilist, ylist, counts, conc_end, t_a, t_b, held_b, s0, s1, s2, s3 = pl.pallas_call(
        edge_kernel,
        out_shape=[
            shape(lists, LANES, dtype=jnp.int32),
            shape(lists, LANES),
            shape(8, cells),
            shape(species, cells),
            state,
            state,
            held,
            *([strip] * 4),
        ],
        in_specs=[hbm] * 9,
        out_specs=[vmem] * 11,
        scratch_shapes=[
            raw,
            work[0],
            pltpu.VMEM(held.shape, F32),
            pltpu.VMEM((halves, species, LANES), F32),
            pltpu.VMEM((halves, reactions, LANES), F32),
            pltpu.VMEM((2, real), jnp.int32),
            pltpu.VMEM((2, real), jnp.int32),
            pltpu.VMEM((2, real), F32),
            pltpu.VMEM((1, cells), jnp.int32),
            pltpu.VMEM((cells, cells), F32),
            pltpu.VMEM((8, listed), jnp.int32),
            pltpu.VMEM((LANES, listed), F32),
            pltpu.VMEM((2, species, reactions), BF16),
            pltpu.VMEM((2 * reactions, species), BF16),
            pltpu.VMEM((2, species, reactions), BF16),
            pltpu.VMEM((species, cells), F32),
            pltpu.SMEM((group,), jnp.int32),
            pltpu.SMEM((4 * listed,), jnp.int32),
            pltpu.SMEM((2 * listed,), F32),
            *work[1:],
            pltpu.SemaphoreType.DMA((9,)),
        ],
        compiler_params=limit,
        name="edge_columns",
    )(
        *[
            pltpu.with_memory_space_constraint(value, pltpu.HBM)
            for value in (
                reaction_index, reactants.T, products.T, yields.T, substeps,
                jnp.asarray(table["permute"]), conc, rate_rows, sens,
            )
        ]
    )

    ilist, ylist = ilist.reshape(-1)[: 4 * listed], ylist.reshape(-1)
    x_one = exchanged(s0, across, 0)
    x_two = exchanged(s1, across, 1)

    t_b, part, side_high, side_low = pl.pallas_call(
        functools.partial(inner_kernel, real),
        out_shape=[state, wide] + [shape(2 * LANES, 2 * LANES, dtype=BF16)] * 2,
        in_specs=[smem] * 3 + [vmem] * 11,
        out_specs=[vmem] * 4,
        scratch_shapes=work,
        compiler_params=limit,
        name="inner_columns",
    )(
        ilist, ylist, reaction_index, counts, numbers, jnp.asarray(table["side_pick"]),
        jnp.asarray(table["side_in"]), jnp.asarray(table["side_out"]), s0, s1, s2, s3,
        held_b, t_b,
    )

    to_one, to_two = pl.pallas_call(
        side_kernel,
        out_shape=[strip, strip],
        in_specs=[vmem] * 5,
        out_specs=[vmem] * 2,
        compiler_params=limit,
        name="y_edges",
    )(part, x_one, x_two, side_high, side_low)
    y_two = exchanged(to_two, 1, 1)
    y_one = exchanged(to_one, 1, 0)

    map_ = shape(3 * LANES, cells, dtype=BF16)
    t_b, map_high, map_low = pl.pallas_call(
        functools.partial(later_kernel, real),
        out_shape=[state, map_, map_],
        in_specs=[smem] * 3 + [vmem] * 7,
        out_specs=[vmem] * 3,
        scratch_shapes=work,
        compiler_params=limit,
        name="inner_later",
    )(
        ilist, ylist, reaction_index, counts, held_b, t_b, numbers,
        jnp.asarray(table["entries"]), jnp.asarray(table["cells"]),
        jnp.asarray(table["cells_rows"]),
    )

    result, conc_out = pl.pallas_call(
        advect_kernel,
        out_shape=[shape(group, species, halves, LANES), shape(species, halves, LANES)],
        in_specs=[vmem] * 9,
        out_specs=[hbm, hbm],
        scratch_shapes=[
            raw,
            pltpu.VMEM((halves, species, LANES), F32),
            pltpu.VMEM((group // 8, species * 8, LANES), F32),
            pltpu.SemaphoreType.DMA((2,)),
        ],
        compiler_params=limit,
        name="advection",
    )(
        conc_end, x_one, x_two, y_two, y_one, map_high, map_low, t_a, t_b,
    )
    return (
        conc_out.reshape(species, 1, cells),
        result.reshape(group, species, 1, cells),
    )


def solution(mesh):
    in_specs = (
        P(None, "tile", None),
        P("pgrp", None, "tile", None),
        P(None, "tile", None),
        P("tile", None),
        P(None, "tile", None),
        P(),
        P(),
        P(),
        P("pgrp"),
    )
    out_specs = (P(None, "tile", None), P("pgrp", None, "tile", None))
    return jax.shard_map(
        per_device, mesh=mesh, in_specs=in_specs, out_specs=out_specs, check_vma=False
    )
```
